128 devices in a mesh: hst: 32 (over z, y, core), local: 4 (over x).
Axes of the slice: x: 4, y: 4, z: 4, core: 2. Of those that a mesh axis runs over, the one named last changes fastest.
Arguments:
- features: bfloat16 [16384, 3456], P(('hst', 'local')), may hold values from -6 to 6
- labels: int32 [16384], P(('hst', 'local')), may hold values 0 or 1
- cross_down: bfloat16 [512, 3456], replicated, may hold values from -0.109375 to 0.109375
- cross_up: bfloat16 [512, 3456], replicated, may hold values from -0.25 to 0.25
- cross_bias: float32 [3456], replicated, may hold values from -2 to 2
- head_weight: float32 [3456], replicated, may hold values from -0.109375 to 0.109375
- head_bias: float32 [1], replicated, may hold values from -2 to 2
- table_place: int32 [22], replicated, may hold values from 0 to 31, as said below
- bag_rows: int32 [16384, 22, 4], P(('hst', 'local')), may hold values from 0 to 16383
- small_rows: int32 [16384, 4, 4], P(('hst', 'local')), may hold values from 0 to 1023
- table_store: float32 [524288, 128], P(('hst', 'local')), may hold values from -0.6 to 0.6
- table_acc: float32 [524288], P(('hst', 'local')), may hold values from 0.01 to 1
- small_store: float32 [4096, 128], replicated, may hold values from -0.6 to 0.6
- small_acc: float32 [4096], replicated, may hold values from 0.001 to 0.1
- down_acc: float32 [512, 3456], P(('hst', 'local')), may hold values from 1 to 100
- up_acc: float32 [512, 3456], P(('hst', 'local')), may hold values from 1 to 100
Outputs:
- table_new: float32 [524288, 128], P(('hst', 'local'))
- table_acc_new: float32 [524288], P(('hst', 'local'))
- small_new: float32 [4096, 128], replicated
- small_acc_new: float32 [4096], replicated
- down_step: float32 [512, 3456], P(('hst', 'local'))
- up_step: float32 [512, 3456], P(('hst', 'local'))
The draws below stay inside these ranges and needn't reach their ends.
Inputs may be any that keep to these rules, and one draw needn't show every extreme that they name: `table_place`: the 22 values are distinct, so no two tables share a slot; the last slot of the last host is always used.
All inputs are finite; a program needn't handle non-finite values. No bound on the sum of `labels` on one device may be relied on, other than what follows from the above.
Results may differ from the reference program's by a relative error of at most 0.0047.
Values sent between devices are 32-bit elements; how exact they have to be, the bound alone decides.
A program may use at most 128 MiB of HBM per device.

```python
import math
import jax
import jax.numpy as jnp
import numpy as np
from jax import lax

EMB = 128
TS = 22
TR = 4
LOWRANK = 512
RS = 1024
HOT = 4
SHARD = 4096
TPH = 1
R_DEV = 4096
TROWS = 16384
WIDTH = 3456
BATCH = 16384
N_HST = 32
N_LOCAL = 4


def draw_table_place(key, part):
    key = jax.random.fold_in(key, 11)
    first_key = jax.random.fold_in(key, 1)
    second_key = jax.random.fold_in(key, 2)
    slot_total = N_HST * TPH
    chosen = jax.random.permutation(first_key, slot_total - 1)[:TS - 1].astype(jnp.int32)
    values = jnp.concatenate([chosen, jnp.full((1,), slot_total - 1, jnp.int32)])
    order = jax.random.permutation(second_key, TS)
    return values[order].astype(jnp.int32)


def with_ends(entries, rng, least, top_value):
    extent = entries.shape
    index_at = [jax.random.randint(jax.random.fold_in(rng, axis), (), 0, extent[axis]) for axis in range(len(extent))]
    entries = entries.at[tuple(index_at)].set(least)
    longest = extent.index(max(extent))
    index_at[longest] = (index_at[longest] + 1) % extent[longest]
    return entries.at[tuple(index_at)].set(top_value)


def block_scale(own_key, extent, shards, least, top_value):
    loudness, own = 1.0, jax.random.fold_in(own_key, 6)
    for position, blocks in shards:
        draws = jnp.exp(jax.random.uniform(jax.random.fold_in(own, position), (blocks,), jnp.float32, least / len(shards), top_value / len(shards)))
        loudness = loudness * jnp.repeat(draws, extent[position] // blocks).reshape([-1 if axis == position else 1 for axis in range(len(extent))])
    return loudness


def rank_bounds(count, slope):
    loads = [(1 << 20) // math.isqrt(standing ** slope) + 1 for standing in range(1, count + 1)]
    deviation = 1 + sum(loads) // (1 << 30)
    return np.cumsum(np.array([max(1, weight // deviation) for weight in loads]))


def skewed_ids(rng, shape, amount, slope):
    listing = rank_bounds(amount, slope)
    ticket = jax.random.randint(jax.random.fold_in(rng, 1), shape, 0, int(listing[amount - 1]))
    standing = jnp.searchsorted(jnp.asarray(listing, jnp.int32), ticket, side="right")
    return jax.random.permutation(jax.random.fold_in(rng, 2), amount)[standing].astype(jnp.int32)


def scatter_about(rng, dims, width, limit, shards=(), kind=jnp.bfloat16):
    array = jax.random.normal(rng, dims, jnp.float32) * width
    if len(shards) > 0:
        array = block_scale(rng, dims, shards, -0.22, 0.18) * array
    return jnp.clip(array, min=-limit, max=limit).astype(kind)


def setup_inputs(seed: int = 0) -> dict:
    keys = jax.random.split(jax.random.key(seed), 17)
    features = scatter_about(keys[0], (BATCH, WIDTH), 1.0, 6.0, ((0, 128),))
    labels = with_ends((jax.random.randint(keys[1], (BATCH,), 0, 4) < 1).astype(jnp.int32), jax.random.fold_in(keys[1], 1), 0, 1)
    cross_down = scatter_about(keys[2], (LOWRANK, WIDTH), WIDTH ** -0.5, 0.109375)
    cross_up = scatter_about(keys[3], (LOWRANK, WIDTH), LOWRANK ** -0.5, 0.25)
    cross_bias = scatter_about(keys[4], (WIDTH,), 0.3, 2.0, (), jnp.float32)
    head_weight = scatter_about(keys[5], (WIDTH,), WIDTH ** -0.5, 0.109375, (), jnp.float32)
    head_bias = scatter_about(keys[6], (1,), 0.5, 2.0, (), jnp.float32)
    table_place = draw_table_place(jax.random.fold_in(keys[16], 71), 0)
    bag_rows = with_ends(skewed_ids(keys[8], (BATCH, TS, HOT), TROWS, 2), jax.random.fold_in(keys[8], 3), 0, TROWS - 1).astype(jnp.int32)
    small_rows = with_ends(skewed_ids(keys[9], (BATCH, TR, HOT), RS, 2), jax.random.fold_in(keys[9], 3), 0, RS - 1).astype(jnp.int32)
    table_store = scatter_about(keys[10], (N_HST * N_LOCAL * R_DEV, EMB), 0.1, 0.6, ((0, 128),), jnp.float32)
    table_acc = jnp.clip(jnp.exp(math.log(1.0) - 4.6051702 * jax.random.uniform(keys[11], (N_HST * N_LOCAL * R_DEV,), jnp.float32) ** block_scale(keys[11], (N_HST * N_LOCAL * R_DEV,), ((0, 128),), -0.2, 0.2)), 0.01, 1.0)
    small_store = scatter_about(keys[12], (TR * RS, EMB), 0.1, 0.6, (), jnp.float32)
    small_acc = jnp.clip(jnp.exp(jax.random.uniform(keys[13], (TR * RS,), jnp.float32, math.log(0.001), math.log(0.1))), 0.001, 0.1)
    down_acc = jnp.clip(jnp.exp(math.log(100.0) - 4.6051702 * jax.random.uniform(keys[14], (LOWRANK, WIDTH), jnp.float32) ** block_scale(keys[14], (LOWRANK, WIDTH), ((0, 128),), -0.2, 0.2)), 1.0, 100.0)
    up_acc = jnp.clip(jnp.exp(math.log(100.0) - 4.6051702 * jax.random.uniform(keys[15], (LOWRANK, WIDTH), jnp.float32) ** block_scale(keys[15], (LOWRANK, WIDTH), ((0, 128),), -0.2, 0.2)), 1.0, 100.0)
    return {"features": features, "labels": labels, "cross_down": cross_down, "cross_up": cross_up, "cross_bias": cross_bias, "head_weight": head_weight, "head_bias": head_bias, "table_place": table_place, "bag_rows": bag_rows, "small_rows": small_rows, "table_store": table_store, "table_acc": table_acc, "small_store": small_store, "small_acc": small_acc, "down_acc": down_acc, "up_acc": up_acc}


LEARN_RATE = 0.05

def dense_backward(block_features, block_labels, cross_down, cross_up, cross_bias, head_weight, head_bias):
    low_proj = lax.dot_general(block_features, cross_down, (((1,), (1,)), ((), ())), preferred_element_type=jnp.float32).astype(jnp.bfloat16)
    cross_out = jnp.dot(low_proj, cross_up, preferred_element_type=jnp.float32) + cross_bias
    wide_input = block_features.astype(jnp.float32)
    layer_out = wide_input * cross_out + wide_input
    logit = jnp.dot(layer_out, head_weight, precision=lax.Precision.HIGHEST) + head_bias[0]
    logit_grad = jax.nn.sigmoid(logit) - block_labels.astype(jnp.float32)
    layer_grad = logit_grad[:, None] * head_weight[None, :]
    cross_grad = (layer_grad * wide_input).astype(jnp.bfloat16)
    low_grad = lax.dot_general(cross_grad, cross_up, (((1,), (1,)), ((), ())), preferred_element_type=jnp.float32).astype(jnp.bfloat16)
    feature_grad = layer_grad * (cross_out + 1.0) + jnp.dot(low_grad, cross_down, preferred_element_type=jnp.float32)
    return (feature_grad, low_proj, cross_grad, low_grad)

def rowwise_adagrad(stored, accum, grads):
    accum_new = accum + lax.optimization_barrier(jnp.mean(grads * grads, axis=1))
    return (stored - LEARN_RATE * grads / jnp.sqrt(accum_new)[:, None], accum_new)

def reference(features, labels, cross_down, cross_up, cross_bias, head_weight, head_bias, table_place, bag_rows, small_rows, table_store, table_acc, small_store, small_acc, down_acc, up_acc):
    block_rows = min(BATCH, 1024)
    block_total = BATCH // block_rows
    emb_width = table_store.shape[1]
    table_total = table_store.shape[0]
    host_of = (table_place // TPH).astype(jnp.int32)
    slot_of = (table_place % TPH).astype(jnp.int32)

    def one_block(carry, block_index):
        down_sum, up_sum, table_sum, small_sum = carry
        begin_row = (block_index * block_rows).astype(jnp.int32)
        block_features = lax.dynamic_slice_in_dim(features, begin_row, block_rows, 0)
        block_labels = lax.dynamic_slice_in_dim(labels, begin_row, block_rows, 0)
        row_ids = lax.dynamic_slice_in_dim(bag_rows, begin_row, block_rows, 0)
        small_ids = lax.dynamic_slice_in_dim(small_rows, begin_row, block_rows, 0)
        feature_grad, low_proj, cross_grad, low_grad = dense_backward(block_features, block_labels, cross_down, cross_up, cross_bias, head_weight, head_bias)
        down_sum = down_sum + lax.dot_general(low_grad, block_features, (((0,), (0,)), ((), ())), preferred_element_type=jnp.float32)
        up_sum = up_sum + lax.dot_general(low_proj, cross_grad, (((0,), (0,)), ((), ())), preferred_element_type=jnp.float32)
        bag_grads = feature_grad[:, emb_width:emb_width * (1 + TS)].reshape(block_rows, TS, emb_width)
        targets = (host_of[None, :, None] * N_LOCAL + row_ids // SHARD) * R_DEV + slot_of[None, :, None] * SHARD + row_ids % SHARD
        spread = jnp.broadcast_to(bag_grads[:, :, None, :], (block_rows, TS, HOT, emb_width))
        table_sum = table_sum.at[targets.reshape(-1).astype(jnp.int32)].add(spread.reshape(-1, emb_width))
        small_grads = feature_grad[:, emb_width * (1 + TS):].reshape(block_rows, TR, emb_width)
        small_targets = jnp.arange(TR, dtype=jnp.int32)[None, :, None] * RS + small_ids
        small_spread = jnp.broadcast_to(small_grads[:, :, None, :], (block_rows, TR, HOT, emb_width))
        small_sum = small_sum.at[small_targets.reshape(-1).astype(jnp.int32)].add(small_spread.reshape(-1, emb_width))
        return ((down_sum, up_sum, table_sum, small_sum), None)
    start_carry = (jnp.zeros(cross_down.shape, jnp.float32), jnp.zeros(cross_up.shape, jnp.float32), jnp.zeros((table_total, emb_width), jnp.float32), jnp.zeros(small_store.shape, jnp.float32))
    sums, unused = lax.scan(one_block, start_carry, jnp.arange(block_total, dtype=jnp.int32))
    down_grad, up_grad, table_grad, small_grad = sums
    table_new, table_acc_new = rowwise_adagrad(table_store, table_acc, table_grad)
    small_new, small_acc_new = rowwise_adagrad(small_store, small_acc, small_grad)
    down_step = down_grad / jnp.sqrt(down_acc + down_grad * down_grad)
    up_step = up_grad / jnp.sqrt(up_acc + up_grad * up_grad)
    return (table_new, table_acc_new, small_new, small_acc_new, down_step, up_step)
```

```python
import functools

import jax
import jax.numpy as jnp
from jax import lax
from jax.experimental import pallas as pl
from jax.experimental.pallas import tpu as pltpu
from jax.sharding import PartitionSpec as P

TS = 22
TR = 4
RS = 1024
HOT = 4
SHARD = 4096


LEARN_RATE = 0.05


def dense_backward(
    block_features, block_labels, cross_down, cross_up, cross_bias, head_weight, head_bias
):
    low_proj = lax.dot_general(
        block_features, cross_down, (((1,), (1,)), ((), ())), preferred_element_type=jnp.float32
    ).astype(jnp.bfloat16)
    cross_out = jnp.dot(low_proj, cross_up, preferred_element_type=jnp.float32) + cross_bias
    wide_input = block_features.astype(jnp.float32)
    layer_out = wide_input * cross_out + wide_input
    logit = jnp.dot(layer_out, head_weight, precision=lax.Precision.HIGHEST) + head_bias[0]
    logit_grad = jax.nn.sigmoid(logit) - block_labels.astype(jnp.float32)
    layer_grad = logit_grad[:, None] * head_weight[None, :]
    cross_grad = (layer_grad * wide_input).astype(jnp.bfloat16)
    low_grad = lax.dot_general(
        cross_grad, cross_up, (((1,), (1,)), ((), ())), preferred_element_type=jnp.float32
    ).astype(jnp.bfloat16)
    feature_grad = layer_grad * (cross_out + 1.0) + jnp.dot(
        low_grad, cross_down, preferred_element_type=jnp.float32
    )
    return (feature_grad, low_proj, cross_grad, low_grad)


def rowwise_adagrad(stored, accum, grads):
    accum_new = accum + jnp.mean(grads * grads, axis=1)
    return (stored - LEARN_RATE * grads / jnp.sqrt(accum_new)[:, None], accum_new)


def pooled_kernel(row_total, ids, grads, out, *sums):
    step = min(row_total, 256)

    @pl.loop(0, row_total // step)
    def _(i):
        rows = pl.ds(pl.multiple_of(i * step, step), step)
        for total in sums:
            total[rows, :] = jnp.zeros((step, total.shape[1]), jnp.float32)

    @pl.loop(0, grads.shape[0] // 8)
    def _(group):
        for pair in range(4):
            sample = group * 8 + pair * 2
            first = grads[pl.ds(sample, 1), :]
            second = grads[pl.ds(sample + 1, 1), :]
            at = [ids[sample * HOT + k] for k in range(2 * HOT)]
            held = [sums[k % HOT][pl.ds(at[k], 1), :] for k in range(2 * HOT)]
            new = [held[k] + first for k in range(HOT)]
            for k in range(HOT):
                new.append(jnp.where(at[k] == at[HOT + k], new[k], held[HOT + k]) + second)
            for k in range(2 * HOT):
                sums[k % HOT][pl.ds(at[k], 1), :] = new[k]

    @pl.loop(0, row_total // step)
    def _(i):
        rows = pl.ds(pl.multiple_of(i * step, step), step)
        out[rows, :] = (sums[0][rows, :] + sums[1][rows, :]) + (sums[2][rows, :] + sums[3][rows, :])


def pooled_rows(row_ids, grads, row_total):
    width = grads.shape[1]
    return pl.pallas_call(
        functools.partial(pooled_kernel, row_total),
        out_shape=jax.ShapeDtypeStruct((row_total, width), jnp.float32),
        in_specs=[pl.BlockSpec(memory_space=pltpu.SMEM), pl.BlockSpec(memory_space=pltpu.VMEM)],
        out_specs=pl.BlockSpec(memory_space=pltpu.VMEM),
        scratch_shapes=[pltpu.VMEM((row_total, width), jnp.float32)] * HOT,
        compiler_params=pltpu.CompilerParams(vmem_limit_bytes=48 << 20),
        name="pooled_rows",
    )(row_ids.reshape(-1), grads)


def on_device(
    features,
    labels,
    cross_down,
    cross_up,
    cross_bias,
    head_weight,
    head_bias,
    table_place,
    bag_rows,
    small_rows,
    table_store,
    table_acc,
    small_store,
    small_acc,
    down_acc,
    up_acc,
):
    n_hosts = lax.axis_size("hst")
    n_locals = lax.axis_size("local")
    sample_count = features.shape[0]
    emb_width = table_store.shape[1]
    dev_rows = table_store.shape[0]
    slots_host = dev_rows // SHARD
    slot_total = n_hosts * slots_host
    feature_grad, low_proj, cross_grad, low_grad = dense_backward(
        features, labels, cross_down, cross_up, cross_bias, head_weight, head_bias
    )
    bag_grads = feature_grad[:, emb_width : emb_width * (1 + TS)].reshape(
        sample_count, TS, emb_width
    )
    slot_of = table_place % slots_host
    host_ids = bag_rows // SHARD * dev_rows + slot_of[None, :, None] * SHARD + bag_rows % SHARD
    placing = table_place[None, :] == jnp.arange(slot_total, dtype=jnp.int32)[:, None]
    send_grads = jnp.einsum(
        "st,bte->sbe", placing.astype(jnp.float32), bag_grads, precision=lax.Precision.HIGHEST
    )
    send_ids = jnp.sum(
        jnp.where(placing[:, :, None, None], jnp.transpose(host_ids, (1, 0, 2))[None], 0), axis=1
    )
    got_grads, got_ids = (
        lax.all_to_all(send_grads, "hst", split_axis=0, concat_axis=0, tiled=True),
        lax.all_to_all(send_ids, "hst", split_axis=0, concat_axis=0, tiled=True),
    )
    got_grads = got_grads.reshape(-1, emb_width)
    got_ids = got_ids.reshape(-1, HOT)
    host_grad = pooled_rows(got_ids, got_grads, n_locals * dev_rows)
    table_grad = lax.psum_scatter(host_grad, "local", scatter_dimension=0, tiled=True)
    table_new, table_acc_new = rowwise_adagrad(table_store, table_acc, table_grad)
    part = low_grad
    down_grad = lax.psum_scatter(
        lax.dot_general(
            part, features, (((0,), (0,)), ((), ())), preferred_element_type=jnp.float32
        ),
        ("hst", "local"),
        scatter_dimension=0,
        tiled=True,
    )
    part = low_proj
    up_grad = lax.psum_scatter(
        lax.dot_general(
            part, cross_grad, (((0,), (0,)), ((), ())), preferred_element_type=jnp.float32
        ),
        ("hst", "local"),
        scatter_dimension=0,
        tiled=True,
    )
    down_step = down_grad / jnp.sqrt(down_acc + down_grad * down_grad)
    up_step = up_grad / jnp.sqrt(up_acc + up_grad * up_grad)
    small_grads = feature_grad[:, emb_width * (1 + TS) :].reshape(sample_count, TR, emb_width)
    small_ids = small_rows + RS * jnp.arange(TR, dtype=jnp.int32)[None, :, None]
    small_local = pooled_rows(
        small_ids.reshape(-1, HOT), small_grads.reshape(-1, emb_width), TR * RS
    )
    small_total = lax.psum(small_local, ("hst", "local"))
    small_new, small_acc_new = rowwise_adagrad(small_store, small_acc, small_total)
    return (table_new, table_acc_new, small_new, small_acc_new, down_step, up_step)


def solution(mesh):
    placed = (
        P(("hst", "local"), None),
        P(("hst", "local")),
        P(),
        P(),
        P(),
        P(),
        P(),
        P(),
        P(("hst", "local"), None, None),
        P(("hst", "local"), None, None),
        P(("hst", "local"), None),
        P(("hst", "local")),
        P(),
        P(),
        P(("hst", "local"), None),
        P(("hst", "local"), None),
    )
    return jax.shard_map(
        on_device,
        mesh=mesh,
        in_specs=placed,
        out_specs=(
            P(("hst", "local"), None),
            P(("hst", "local")),
            P(),
            P(),
            P(("hst", "local"), None),
            P(("hst", "local"), None),
        ),
        check_vma=False,
    )
```

```python
import functools

import jax
import jax.numpy as jnp
from jax import lax
from jax.experimental import pallas as pl
from jax.experimental.pallas import tpu as pltpu
from jax.sharding import PartitionSpec as P

TS = 22
TR = 4
RS = 1024
HOT = 4
SHARD = 4096
EMB = 128
RANK = 512
WIDTH = 3456
HOSTS = 32
LOCALS = 4
SAMPLES = 128
PACK = SAMPLES + 8
CUT = 1792
LEARN_RATE = 0.05
MESH = pl.DeviceIdType.MESH
F32 = jnp.float32
BF16 = jnp.bfloat16


def product(left, right, left_dim=1, right_dim=0):
    return lax.dot_general(
        left, right, (((left_dim,), (right_dim,)), ((), ())), preferred_element_type=F32
    )


def diagonal():
    return lax.broadcasted_iota(jnp.int32, (128, 128), 0) == lax.broadcasted_iota(
        jnp.int32, (128, 128), 1
    )


def dense_kernel(
    features, labels, bias, head, head_bias, place, bags, down_hbm, up_hbm,
    send, small, rights, lows, down, up, cross, sems,
):
    down_copy = pltpu.make_async_copy(down_hbm, down, sems.at[0])
    up_copy = pltpu.make_async_copy(up_hbm, up, sems.at[1])
    down_copy.start()
    up_copy.start()

    @pl.loop(0, HOSTS)
    def _(slot):
        send[slot] = jnp.zeros((PACK, EMB), F32)

    rights[0:SAMPLES, :] = features[...]
    parts = [(start, min(256, WIDTH - start)) for start in range(0, WIDTH, 256)]
    down_copy.wait()
    low_proj = product(features[...], down[...], 1, 1).astype(BF16)
    lows[SAMPLES:, :] = low_proj
    up_copy.wait()
    terms = jnp.zeros((SAMPLES, 128), F32)
    for start, width in parts:
        at = pl.ds(start, width)
        out = product(low_proj, up[:, at]) + bias[:, at]
        cross[:, at] = out
        wide = features[:, at].astype(F32)
        weighted = (wide * out + wide) * head[:, at]
        for tile in range(width // 128):
            terms = terms + weighted[:, tile * 128 : (tile + 1) * 128]
    logit = jnp.sum(terms, axis=1, keepdims=True) + head_bias[0]
    label = jnp.sum(
        jnp.where(diagonal(), labels[...].astype(F32), 0.0), axis=1, keepdims=True
    )
    logit_grad = jax.nn.sigmoid(logit) - label
    for start, width in parts:
        at = pl.ds(start, width)
        layer_grad = logit_grad * head[:, at]
        rights[SAMPLES:, at] = (layer_grad * features[:, at].astype(F32)).astype(BF16)
    low_grad = product(rights[SAMPLES:, :], up[...], 1, 1).astype(BF16)
    lows[0:SAMPLES, :] = low_grad
    for start, width in parts:
        at = pl.ds(start, width)
        layer_grad = logit_grad * head[:, at]
        grad = layer_grad * (cross[:, at] + 1.0) + product(low_grad, down[:, at])
        for tile in range(width // 128):
            piece = grad[:, tile * 128 : (tile + 1) * 128]
            table = start // 128 + tile - 1
            if 0 <= table < TS:
                slot = place[table]
                send[slot, 0:SAMPLES, :] = piece
                send[slot, SAMPLES:, :] = bags[table]
            elif table >= TS:
                small[:, (table - TS) * EMB : (table - TS + 1) * EMB] = piece


def exchange_kernel(
    send, rights, lows, small, small_ids,
    got, ids, dense, small_sum,
    left_own, left_other, own, other, arrived, split, sems, core_sems, out_sems, own_sem,
):
    host = lax.axis_index("hst")
    core = lax.rem(host, 2)
    partner = host + 1 - 2 * core
    barrier = pltpu.get_barrier_semaphore()

    @pl.loop(1, HOSTS)
    def _(off):
        pl.semaphore_signal(
            barrier, inc=1, device_id={"hst": lax.rem(host + off, HOSTS)}, device_id_type=MESH
        )

    pl.semaphore_wait(barrier, HOSTS - 1)

    def bag_copy(off, to, slot):
        return pltpu.make_async_remote_copy(
            src_ref=send.at[to],
            dst_ref=got.at[slot],
            send_sem=sems.at[0, off],
            recv_sem=sems.at[1, off],
            device_id={"hst": to},
            device_id_type=MESH,
        )

    @pl.loop(1, HOSTS)
    def _(off):
        bag_copy(off, lax.rem(host + off, HOSTS), host).start()

    mine = pltpu.make_async_copy(send.at[host], got.at[host], own_sem)
    mine.start()

    def spread(target, left):
        row = lax.broadcasted_iota(jnp.int32, (RANK, RANK), 0)
        rank = lax.broadcasted_iota(jnp.int32, (RANK, RANK), 1)
        place = row & 7
        base = ((row >> 5) * 2 + target) * 16 + ((row >> 3) & 3) * 4
        for part in range(2):
            want = jnp.where((place >> 2) == part, base + place - 4 * part, -1)
            chosen = jnp.where(want == rank, 1.0, 0.0).astype(BF16)
            left[:, part * SAMPLES : (part + 1) * SAMPLES] = product(
                chosen, lows[part * SAMPLES : (part + 1) * SAMPLES, :], 1, 1
            ).astype(BF16)

    def grads(left, out, group):
        @pl.loop(0, WIDTH // 384)
        def _(part):
            at = pl.ds(pl.multiple_of(part * 384, 384), 384)
            out[group * 128 : (group + 1) * 128, at] = product(
                left[group * 128 : (group + 1) * 128, :], rights[:, at]
            )

    def core_copy(group):
        rows = pl.ds(group * 128, 128)
        return pltpu.make_async_remote_copy(
            src_ref=other.at[rows],
            dst_ref=arrived.at[rows],
            send_sem=core_sems.at[0, group],
            recv_sem=core_sems.at[1, group],
            device_id={"hst": partner},
            device_id_type=MESH,
        )

    def out_copy(group):
        rows = pl.ds(group * 128, 128)
        return pltpu.make_async_copy(own.at[rows], dense.at[rows], out_sems.at[group])

    spread(1 - core, left_other)
    for group in range(4):
        grads(left_other, other, group)
        core_copy(group).start()
    spread(core, left_own)
    for group in range(4):
        grads(left_own, own, group)

    for table in range(TR):
        value = small[:, table * EMB : (table + 1) * EMB]
        high = value.astype(BF16)
        split[table, :, 0:EMB] = high
        split[table, :, EMB:] = (value - high.astype(F32)).astype(BF16)

    @pl.loop(0, TR * RS // 128)
    def _(block):
        table = block // 8
        rows = (block % 8) * 128 + lax.broadcasted_iota(jnp.int32, (128, SAMPLES), 0)
        wanted = small_ids[table]
        counts = jnp.zeros((128, SAMPLES), F32)
        for k in range(HOT):
            counts = counts + jnp.where(rows == wanted[k : k + 1, :], 1.0, 0.0)
        both = product(counts.astype(BF16), split[table])
        small_sum[pl.ds(pl.multiple_of(block * 128, 128), 128), :] = both[:, 0:EMB] + both[:, EMB:]

    for group in range(4):
        core_copy(group).wait_recv()

        @pl.loop(0, 4)
        def _(part):
            rows = pl.ds(pl.multiple_of(group * 128 + part * 32, 32), 32)
            own[rows, :] = own[rows, :] + arrived[rows, :]

        out_copy(group).start()

    mine.wait()

    @pl.loop(1, HOSTS)
    def _(off):
        bag_copy(off, lax.rem(host + off, HOSTS), lax.rem(host - off + HOSTS, HOSTS)).wait_recv()

    @pl.loop(0, HOSTS // 2)
    def _(pair):
        low = got[pair * 2, pl.ds(SAMPLES, 8), :]
        high = got[pair * 2 + 1, pl.ds(SAMPLES, 8), :]
        ids[pl.ds(pl.multiple_of(pair * 8, 8), 8), :] = jnp.concatenate(
            [low[0:HOT], high[0:HOT]], axis=0
        ).astype(jnp.int32)

    @pl.loop(1, HOSTS)
    def _(off):
        bag_copy(off, lax.rem(host + off, HOSTS), host).wait_send()

    for group in range(4):
        core_copy(group).wait_send()
        out_copy(group).wait()


def pooled_kernel(ids, grads, out, *sums):
    row_total = out.shape[0]
    step = 256

    @pl.loop(0, row_total // step)
    def _(i):
        rows = pl.ds(pl.multiple_of(i * step, step), step)
        for total in sums:
            total[rows, :] = jnp.zeros((step, EMB), F32)

    @pl.loop(0, HOSTS)
    def _(source):
        @pl.loop(0, SAMPLES // 16)
        def _(group):
            for pair in range(8):
                sample = group * 16 + pair * 2
                first = grads[source, pl.ds(sample, 1), :]
                second = grads[source, pl.ds(sample + 1, 1), :]
                at = [
                    ids[(source * HOT + k % HOT) * SAMPLES + sample + k // HOT]
                    for k in range(2 * HOT)
                ]
                held = [sums[k % HOT][pl.ds(at[k], 1), :] for k in range(2 * HOT)]
                new = [held[k] + first for k in range(HOT)]
                for k in range(HOT):
                    new.append(jnp.where(at[k] == at[HOT + k], new[k], held[HOT + k]) + second)
                for k in range(2 * HOT):
                    sums[k % HOT][pl.ds(at[k], 1), :] = new[k]

    @pl.loop(0, row_total // step)
    def _(i):
        rows = pl.ds(pl.multiple_of(i * step, step), step)
        out[rows, :] = (sums[0][rows, :] + sums[1][rows, :]) + (sums[2][rows, :] + sums[3][rows, :])


class Ring:
    def __init__(self, place, right, left, sent, held, near, passed, sems, chunks=1):
        self.place, self.right, self.left = place, right, left
        self.sent, self.held, self.near, self.passed, self.sems = sent, held, near, passed, sems
        self.chunks = chunks

    def piece(self, ref, chunk):
        if self.chunks == 1:
            return ref
        rows = ref.shape[0] // self.chunks
        return ref.at[pl.ds(chunk * rows, rows)]

    def copy(self, src, dst, index, to):
        return pltpu.make_async_remote_copy(
            src_ref=src, dst_ref=dst, send_sem=self.sems.at[0, index],
            recv_sem=self.sems.at[1, index], device_id=to, device_id_type=MESH,
        )

    def far(self, side, chunk):
        src = self.sent(lax.rem(self.place + 2, 4), side)
        to = self.left if side else self.right
        return self.copy(
            self.piece(src, chunk), self.piece(self.passed[side], chunk),
            2 + side * self.chunks + chunk, to,
        )

    def direct(self, side):
        to = self.left if side else self.right
        target = lax.rem(self.place + (3 if side else 1), 4)
        return self.copy(self.sent(target, 1 - side), self.near[side], side, to)

    def relay(self, side, chunk, sums):
        to = self.left if side else self.right
        return self.copy(
            self.piece(self.passed[side], chunk), self.piece(sums[side], chunk),
            2 + (2 + side) * self.chunks + chunk, to,
        )

    def start(self):
        for chunk in range(self.chunks):
            self.far(0, chunk).start()
            self.far(1, chunk).start()
        self.direct(0).start()
        self.direct(1).start()

    def middle(self, sums):
        for chunk in range(self.chunks):
            for side in range(2):
                self.far(side, chunk).wait_recv()
                target = lax.rem(self.place + (3 if side else 1), 4)
                add_into(self.piece(self.passed[side], chunk), self.piece(self.held(target, side), chunk))
                self.relay(side, chunk, sums).start()

    def drain(self, sums):
        for side in range(2):
            self.direct(side).wait_send()
            for chunk in range(self.chunks):
                self.far(side, chunk).wait_send()
                self.relay(side, chunk, sums).wait_send()


def blocks_of(shape):
    if len(shape) == 3:
        return shape[0], lambda ref, i: ref.at[i]
    rows = min(shape[0], 32 if shape[1] > 256 else 128)
    return shape[0] // rows, lambda ref, i: ref.at[pl.ds(pl.multiple_of(i * rows, rows), rows)]


def add_into(total, term):
    count, at = blocks_of(total.shape)

    @pl.loop(0, count)
    def _(i):
        at(total, i)[...] = at(total, i)[...] + at(term, i)[...]


def add_three(out, first, second, third):
    count, at = blocks_of(out.shape)

    @pl.loop(0, count)
    def _(i):
        at(out, i)[...] = at(first, i)[...] + at(second, i)[...] + at(third, i)[...]


CHUNKS = 4


def reduce_kernel(
    tables, dense, store_hbm, acc, down_acc, up_acc,
    table_new, acc_new, down_step, up_step,
    store, mine, ahead, behind, grads,
    t_near0, t_near1, t_pass0, t_pass1, t_sum0, t_sum1,
    a_near0, a_near1, a_pass0, a_pass1, a_sum0, a_sum1,
    b_near0, b_near1, b_pass0, b_pass1, b_sum0, b_sum1,
    c_near0, c_near1, c_pass0, c_pass1, c_sum0, c_sum1,
    d_near0, d_near1, d_pass0, d_pass1, d_sum0, d_sum1,
    e_near0, e_near1, e_pass0, e_pass1, e_sum0, e_sum1,
    a_out, b_out, c_out, d_out,
    t_sems, r_sems, local_sems,
):
    host = lax.axis_index("hst")
    x = lax.axis_index("local")
    z, y, core = host // 8, (host // 2) % 4, host % 2

    def on_z(step):
        return {"hst": (lax.rem(z + step, 4) * 4 + y) * 2 + core}

    def on_y(step):
        return {"hst": (z * 4 + lax.rem(y + step, 4)) * 2 + core}

    def on_x(step):
        return {"local": lax.rem(x + step, 4)}

    barrier = pltpu.get_barrier_semaphore()
    for neighbours in (on_x, on_y, on_z):
        for step in (1, 3):
            pl.semaphore_signal(
                barrier, inc=1, device_id=neighbours(step), device_id_type=MESH
            )
    half = SHARD // 2
    right, left = lax.rem(x + 1, 4), lax.rem(x + 3, 4)
    locals_ = [
        pltpu.make_async_copy(tables.at[right, pl.ds(0, half)], ahead, local_sems.at[0]),
        pltpu.make_async_copy(tables.at[left, pl.ds(half, half)], behind, local_sems.at[1]),
        pltpu.make_async_copy(dense, grads, local_sems.at[2]),
        pltpu.make_async_copy(tables.at[x], mine, local_sems.at[3]),
        pltpu.make_async_copy(store_hbm, store, local_sems.at[4]),
    ]
    for copy in locals_:
        copy.start()
    pl.semaphore_wait(barrier, 6)

    first = {0: pl.ds(0, 896), 1: pl.ds(896, 896)}
    second = {0: pl.ds(CUT, 896), 1: pl.ds(CUT + 896, 768)}
    inner = {0: pl.ds(0, 896), 1: pl.ds(896, 768)}
    table_ring = Ring(
        x, on_x(1), on_x(3),
        lambda t, s: tables.at[t, pl.ds(s * half, half)],
        lambda t, s: behind if s else ahead,
        (t_near0, t_near1), (t_pass0, t_pass1), t_sems, CHUNKS,
    )
    table_sums = (t_sum0, t_sum1)
    a_ring = Ring(
        z, on_z(1), on_z(3),
        lambda t, s: dense.at[t, :, :, first[s]],
        lambda t, s: grads.at[t, :, :, first[s]],
        (a_near0, a_near1), (a_pass0, a_pass1), r_sems.at[0],
    )
    b_ring = Ring(
        y, on_y(1), on_y(3),
        lambda t, s: dense.at[:, t, :, second[s]],
        lambda t, s: grads.at[:, t, :, second[s]],
        (b_near0, b_near1), (b_pass0, b_pass1), r_sems.at[1],
    )
    c_at = lambda t, s: a_out.at[t, :, first[s]]
    c_ring = Ring(
        y, on_y(1), on_y(3), c_at, c_at, (c_near0, c_near1), (c_pass0, c_pass1), r_sems.at[2]
    )
    d_at = lambda t, s: b_out.at[t, :, inner[s]]
    d_ring = Ring(
        z, on_z(1), on_z(3), d_at, d_at, (d_near0, d_near1), (d_pass0, d_pass1), r_sems.at[3]
    )
    e_at = lambda t, s: (d_out if s else c_out).at[pl.ds(pl.multiple_of(t * 8, 8), 8)]
    e_ring = Ring(
        x, on_x(1), on_x(3), e_at, e_at, (e_near0, e_near1), (e_pass0, e_pass1), r_sems.at[4]
    )

    a_ring.start()
    b_ring.start()
    table_ring.start()
    for copy in locals_[:3]:
        copy.wait()
    a_ring.middle((a_sum0, a_sum1))
    b_ring.middle((b_sum0, b_sum1))
    table_ring.middle(table_sums)

    def finish(ring, sums, outs, place):
        for side in range(2):
            ring.direct(side).wait_recv()
            ring.relay(side, 0, sums).wait_recv()
        add_three(outs[0], ring.held(place, 0), sums[0], ring.near[1])
        add_three(outs[1], ring.held(place, 1), ring.near[0], sums[1])

    finish(a_ring, (a_sum0, a_sum1), [a_out.at[:, :, first[s]] for s in range(2)], z)
    c_ring.start()
    finish(b_ring, (b_sum0, b_sum1), [b_out.at[:, :, inner[s]] for s in range(2)], y)
    d_ring.start()
    c_ring.middle((c_sum0, c_sum1))
    d_ring.middle((d_sum0, d_sum1))
    finish(c_ring, (c_sum0, c_sum1), [c_out.at[:, first[s]] for s in range(2)], y)
    finish(d_ring, (d_sum0, d_sum1), [d_out.at[:, inner[s]] for s in range(2)], z)
    e_ring.start()
    e_ring.middle((e_sum0, e_sum1))
    for copy in locals_[3:]:
        copy.wait()

    eye = diagonal()

    def update(block, first_term, second_term, third_term):
        rows = pl.ds(pl.multiple_of(block * 128, 128), 128)
        grad = first_term + second_term + third_term
        acc_here = jnp.sum(jnp.where(eye, acc[pl.ds(block, 1), :], 0.0), axis=1, keepdims=True)
        total = acc_here + jnp.sum(grad * grad, axis=1, keepdims=True) * (1.0 / EMB)
        table_new[rows, :] = store[rows, :] - grad * (LEARN_RATE * lax.rsqrt(total))
        acc_new[pl.ds(block, 1), :] = jnp.sum(jnp.where(eye, total, 0.0), axis=0, keepdims=True)

    for side in range(2):
        table_ring.direct(side).wait_recv()
    rows_chunk = half // CHUNKS
    for chunk in range(CHUNKS):
        for side in range(2):
            table_ring.relay(side, chunk, table_sums).wait_recv()
            near = (t_near1, t_near0)[side]

            @pl.loop(0, rows_chunk // 128)
            def _(part):
                inside = pl.ds(pl.multiple_of(chunk * rows_chunk + part * 128, 128), 128)
                block = side * (half // 128) + chunk * (rows_chunk // 128) + part
                rows = pl.ds(pl.multiple_of(block * 128, 128), 128)
                update(block, mine[rows, :], table_sums[side][inside, :], near[inside, :])

    e_sums = (e_sum0, e_sum1)
    for side in range(2):
        e_ring.direct(side).wait_recv()
        e_ring.relay(side, 0, e_sums).wait_recv()
    for side, start, width in ((0, 0, CUT), (1, CUT, WIDTH - CUT)):
        at = pl.ds(start, width)
        near = (e_near1, e_near0)[side]
        total = e_ring.held(x, side)[...] + e_sums[side][...] + near[...]
        for step, sums, rows in ((down_step, down_acc, 0), (up_step, up_acc, 4)):
            grad = total[rows : rows + 4]
            step[:, at] = grad * lax.rsqrt(sums[:, at] + grad * grad)

    table_ring.drain(table_sums)
    a_ring.drain((a_sum0, a_sum1))
    b_ring.drain((b_sum0, b_sum1))
    c_ring.drain((c_sum0, c_sum1))
    d_ring.drain((d_sum0, d_sum1))
    e_ring.drain(e_sums)


def small_kernel(store, acc, grads, new, acc_new):
    eye = diagonal()

    @pl.loop(0, TR * RS // 128)
    def _(block):
        rows = pl.ds(pl.multiple_of(block * 128, 128), 128)
        grad = grads[rows, :]
        acc_here = jnp.sum(jnp.where(eye, acc[pl.ds(block, 1), :], 0.0), axis=1, keepdims=True)
        total = acc_here + jnp.sum(grad * grad, axis=1, keepdims=True) * (1.0 / EMB)
        new[rows, :] = store[rows, :] - grad * (LEARN_RATE * lax.rsqrt(total))
        acc_new[pl.ds(block, 1), :] = jnp.sum(jnp.where(eye, total, 0.0), axis=0, keepdims=True)


def shaped(shape, dtype=F32):
    return jax.ShapeDtypeStruct(shape, dtype)


ANY = pl.BlockSpec(memory_space=pl.ANY)
VMEM = pl.BlockSpec(memory_space=pltpu.VMEM)
SMEM = pl.BlockSpec(memory_space=pltpu.SMEM)
DMA = pltpu.SemaphoreType.DMA


def params(mebibytes, **others):
    return pltpu.CompilerParams(vmem_limit_bytes=mebibytes << 20, **others)


def on_device(
    features, labels, cross_down, cross_up, cross_bias, head_weight, head_bias, table_place,
    bag_rows, small_rows, table_store, table_acc, small_store, small_acc, down_acc, up_acc,
):
    bags = jnp.pad(
        jnp.transpose(bag_rows, (1, 2, 0)).astype(F32), ((0, 0), (0, 8 - HOT), (0, 0))
    )
    small_ids = jnp.transpose(small_rows, (1, 2, 0))
    send, small, rights, lows = pl.pallas_call(
        dense_kernel,
        out_shape=(
            shaped((HOSTS, PACK, EMB)), shaped((SAMPLES, TR * EMB)),
            shaped((2 * SAMPLES, WIDTH), BF16), shaped((2 * SAMPLES, RANK), BF16),
        ),
        in_specs=[VMEM] * 4 + [SMEM] * 2 + [VMEM] + [ANY] * 2,
        out_specs=(VMEM,) * 4,
        scratch_shapes=[
            pltpu.VMEM((RANK, WIDTH), BF16), pltpu.VMEM((RANK, WIDTH), BF16),
            pltpu.VMEM((SAMPLES, WIDTH), F32), DMA((2,)),
        ],
        compiler_params=params(40),
        name="dense_backward",
    )(
        features, labels.reshape(1, -1), cross_bias.reshape(1, -1), head_weight.reshape(1, -1),
        head_bias, table_place, bags, cross_down, cross_up,
    )
    whole = (RANK, WIDTH)
    got, ids, dense, small_sum = pl.pallas_call(
        exchange_kernel,
        out_shape=(
            shaped((HOSTS, PACK, EMB)), shaped((HOSTS * HOT, SAMPLES), jnp.int32),
            shaped(whole), shaped((TR * RS, EMB)),
        ),
        in_specs=[ANY] + [VMEM] * 4,
        out_specs=(VMEM, VMEM, ANY, VMEM),
        scratch_shapes=[
            pltpu.VMEM((RANK, 2 * SAMPLES), BF16), pltpu.VMEM((RANK, 2 * SAMPLES), BF16),
            pltpu.VMEM(whole, F32), pltpu.VMEM(whole, F32), pltpu.VMEM(whole, F32),
            pltpu.VMEM((TR, SAMPLES, 2 * EMB), BF16),
            DMA((2, HOSTS)), DMA((2, 4)), DMA((4,)), DMA,
        ],
        compiler_params=params(48, collective_id=0, has_side_effects=True),
        name="exchange",
    )(send, rights, lows, small, small_ids)
    small_total = lax.psum(small_sum, ("hst", "local"))
    tables = pl.pallas_call(
        pooled_kernel,
        out_shape=shaped((LOCALS * SHARD, EMB)),
        in_specs=[SMEM, VMEM],
        out_specs=VMEM,
        scratch_shapes=[pltpu.VMEM((LOCALS * SHARD, EMB), F32)] * HOT,
        compiler_params=params(50),
        name="pooled_rows",
    )(ids.reshape(-1), got)

    def ring_buffers(first_shape, second_shape):
        near = [pltpu.VMEM(second_shape, F32), pltpu.VMEM(first_shape, F32)]
        return near + [pltpu.VMEM(first_shape, F32), pltpu.VMEM(second_shape, F32)] * 2

    rest = WIDTH - CUT
    half = SHARD // 2
    table_new, acc_new, down_step, up_step = pl.pallas_call(
        reduce_kernel,
        out_shape=(
            shaped((SHARD, EMB)), shaped((SHARD // 128, 128)),
            shaped((4, WIDTH)), shaped((4, WIDTH)),
        ),
        in_specs=[ANY] * 3 + [VMEM] * 3,
        out_specs=(VMEM,) * 4,
        scratch_shapes=[
            pltpu.VMEM((SHARD, EMB), F32), pltpu.VMEM((SHARD, EMB), F32),
            pltpu.VMEM((half, EMB), F32), pltpu.VMEM((half, EMB), F32),
            pltpu.VMEM((4, 4, 32, WIDTH), F32),
        ]
        + ring_buffers((half, EMB), (half, EMB))
        + ring_buffers((4, 32, 896), (4, 32, 896))
        + ring_buffers((4, 32, 896), (4, 32, 768))
        + ring_buffers((32, 896), (32, 896))
        + ring_buffers((32, 896), (32, 768))
        + ring_buffers((8, CUT), (8, rest))
        + [
            pltpu.VMEM((4, 32, CUT), F32), pltpu.VMEM((4, 32, rest), F32),
            pltpu.VMEM((32, CUT), F32), pltpu.VMEM((32, rest), F32),
            DMA((2, 2 + 4 * CHUNKS)), DMA((5, 2, 6)), DMA((5,)),
        ],
        compiler_params=params(50, collective_id=1, has_side_effects=True),
        name="reduce_update",
    )(
        tables.reshape(LOCALS, SHARD, EMB), dense.reshape(4, 4, 32, WIDTH), table_store,
        table_acc.reshape(-1, 128), down_acc, up_acc,
    )
    small_new, small_acc_new = pl.pallas_call(
        small_kernel,
        out_shape=(shaped((TR * RS, EMB)), shaped((TR * RS // 128, 128))),
        in_specs=[VMEM] * 3,
        out_specs=(VMEM,) * 2,
        compiler_params=params(16),
        name="small_update",
    )(small_store, small_acc.reshape(-1, 128), small_total)
    return (
        table_new, acc_new.reshape(-1), small_new, small_acc_new.reshape(-1), down_step, up_step,
    )


def solution(mesh):
    both = ("hst", "local")
    rows = P(both, None)
    return jax.shard_map(
        on_device,
        mesh=mesh,
        in_specs=(
            rows, P(both), P(), P(), P(), P(), P(), P(), P(both, None, None), P(both, None, None),
            rows, P(both), P(), P(), rows, rows,
        ),
        out_specs=(rows, P(both), P(), P(), rows, rows),
        check_vma=False,
    )
```

```python
import functools

import jax
import jax.numpy as jnp
from jax import lax
from jax.experimental import pallas as pl
from jax.experimental.pallas import tpu as pltpu
from jax.sharding import PartitionSpec as P

TS = 22
TR = 4
RS = 1024
HOT = 4
SHARD = 4096
EMB = 128
RANK = 512
WIDTH = 3456
HOSTS = 32
LOCALS = 4
SAMPLES = 128
PACK = SAMPLES + 8
FULL = WIDTH + TR * EMB
CUT = 2048
TIES = ((2, 0), (2, 1), (2, 3), (0, 2), (1, 2), (3, 2), (2, 2))
STRAIGHT = ((0, 1), (0, 3), (1, 0), (3, 0), (1, 1), (1, 3), (3, 1), (3, 3))
LEARN_RATE = 0.05
MESH = pl.DeviceIdType.MESH
F32 = jnp.float32
BF16 = jnp.bfloat16


def product(left, right, left_dim=1, right_dim=0):
    return lax.dot_general(
        left, right, (((left_dim,), (right_dim,)), ((), ())), preferred_element_type=F32
    )


def diagonal():
    return lax.broadcasted_iota(jnp.int32, (128, 128), 0) == lax.broadcasted_iota(
        jnp.int32, (128, 128), 1
    )


def dense_kernel(
    labels, bias, head, head_bias, place, bags, features_hbm, down_hbm, up_hbm,
    send, small, rights, lows, down, up, cross, sems,
):
    features = rights.at[0:SAMPLES]
    features_copy = pltpu.make_async_copy(features_hbm, features, sems.at[2])
    down_copy = pltpu.make_async_copy(down_hbm, down, sems.at[0])
    up_copy = pltpu.make_async_copy(up_hbm, up, sems.at[1])
    features_copy.start()
    down_copy.start()
    up_copy.start()

    @pl.loop(0, HOSTS)
    def _(slot):
        send[slot] = jnp.zeros((PACK, EMB), F32)

    parts = [(start, min(256, WIDTH - start)) for start in range(0, WIDTH, 256)]

    def tiles(ref, start, width):
        rows = [ref[t : t + 1, :] for t in range(start // 128, (start + width) // 128)]
        return jnp.concatenate(rows, axis=1)

    features_copy.wait()
    down_copy.wait()
    low_proj = product(features[...], down[...], 1, 1).astype(BF16)
    lows[SAMPLES:, :] = low_proj
    up_copy.wait()
    terms = jnp.zeros((SAMPLES, 128), F32)
    for start, width in parts:
        at = pl.ds(start, width)
        out = product(low_proj, up[:, at]) + tiles(bias, start, width)
        cross[:, at] = out
        wide = features[:, at].astype(F32)
        weighted = (wide * out + wide) * tiles(head, start, width)
        for tile in range(width // 128):
            terms = terms + weighted[:, tile * 128 : (tile + 1) * 128]
    logit = jnp.sum(terms, axis=1, keepdims=True) + head_bias[0]
    label = jnp.sum(
        jnp.where(diagonal(), labels[...].astype(F32), 0.0), axis=1, keepdims=True
    )
    logit_grad = jax.nn.sigmoid(logit) - label
    for start, width in parts:
        at = pl.ds(start, width)
        layer_grad = logit_grad * tiles(head, start, width)
        rights[SAMPLES:, at] = (layer_grad * features[:, at].astype(F32)).astype(BF16)
    low_grad = product(rights[SAMPLES:, :], up[...], 1, 1).astype(BF16)
    lows[0:SAMPLES, :] = low_grad
    for start, width in parts:
        at = pl.ds(start, width)
        layer_grad = logit_grad * tiles(head, start, width)
        grad = layer_grad * (cross[:, at] + 1.0) + product(low_grad, down[:, at])
        for tile in range(width // 128):
            piece = grad[:, tile * 128 : (tile + 1) * 128]
            table = start // 128 + tile - 1
            if 0 <= table < TS:
                slot = place[table]
                send[slot, 0:SAMPLES, :] = piece
                send[slot, SAMPLES : SAMPLES + HOT, :] = bags[table].astype(F32)
            elif table >= TS:
                small[:, (table - TS) * EMB : (table - TS + 1) * EMB] = piece


def exchange_kernel(
    send, rights_hbm, lows_hbm, small_hbm, small_ids,
    got_hbm, ids, dense,
    rights, lows, small, got, left_own, left_other, own, other, arrived, split, relayed,
    sems, relay_sems, core_sems, out_sems, in_sems, own_sem,
):
    host = lax.axis_index("hst")
    core = lax.rem(host, 2)
    z, y = host // 8, (host // 2) % 4
    partner = host + 1 - 2 * core
    operands = [
        pltpu.make_async_copy(source, target, in_sems.at[i])
        for i, (source, target) in enumerate(
            ((lows_hbm, lows), (rights_hbm, rights), (small_hbm, small))
        )
    ]
    for copy in operands:
        copy.start()
    barrier = pltpu.get_barrier_semaphore()

    @pl.loop(1, HOSTS)
    def _(off):
        pl.semaphore_signal(
            barrier, inc=1, device_id={"hst": lax.rem(host + off, HOSTS)}, device_id_type=MESH
        )

    def chip(dz, dy):
        return (lax.rem(z + dz + 4, 4) * 4 + lax.rem(y + dy + 4, 4)) * 2

    def bag_copy(src, to, slot, off, cores):
        at = (off[0] * 4 + off[1]) * 2
        return pltpu.make_async_remote_copy(
            src_ref=src,
            dst_ref=got.at[slot],
            send_sem=sems.at[0, at + cores[1]],
            recv_sem=sems.at[1, at + cores[0]],
            device_id={"hst": to},
            device_id_type=MESH,
        )

    def straight(off, target):
        to = chip(*off) + target
        return bag_copy(send.at[to], to, host, off, (core, target))

    turn = 1 - 2 * core

    def halfway(index):
        dz, dy = TIES[index]
        to = chip(turn if dz == 2 else 0, turn if dy == 2 else 0) + core
        return pltpu.make_async_remote_copy(
            src_ref=send.at[pl.ds(chip(dz, dy), 2)],
            dst_ref=relayed.at[index],
            send_sem=relay_sems.at[0, index],
            recv_sem=relay_sems.at[1, index],
            device_id={"hst": to},
            device_id_type=MESH,
        )

    def onward(index, target):
        dz, dy = TIES[index]
        to = chip(turn if dz == 2 else dz, turn if dy == 2 else dy) + target
        source = chip(-turn if dz == 2 else 0, -turn if dy == 2 else 0) + core
        return bag_copy(relayed.at[index, target], to, source, TIES[index], (core, target))

    def arrival(off, source_core):
        source = chip(-off[0], -off[1]) + source_core
        return bag_copy(send.at[source], source, source, off, (source_core, source_core))

    def neighbour():
        return pltpu.make_async_remote_copy(
            src_ref=send.at[partner],
            dst_ref=got.at[host],
            send_sem=sems.at[0, 0],
            recv_sem=sems.at[1, 0],
            device_id={"hst": partner},
            device_id_type=MESH,
        )

    def from_neighbour():
        return pltpu.make_async_remote_copy(
            src_ref=send.at[partner],
            dst_ref=got.at[partner],
            send_sem=sems.at[0, 0],
            recv_sem=sems.at[1, 0],
            device_id={"hst": partner},
            device_id_type=MESH,
        )

    pl.semaphore_wait(barrier, HOSTS - 1)
    for index in range(len(TIES)):
        halfway(index).start()
    for off in STRAIGHT:
        for target in range(2):
            straight(off, target).start()
    neighbour().start()
    mine = pltpu.make_async_copy(send.at[host], got.at[host], own_sem)
    mine.start()

    def spread(target, left):
        row = lax.broadcasted_iota(jnp.int32, (RANK, RANK), 0)
        rank = lax.broadcasted_iota(jnp.int32, (RANK, RANK), 1)
        place = row & 7
        base = ((row >> 5) * 2 + target) * 16 + ((row >> 3) & 3) * 4
        for part in range(2):
            want = jnp.where((place >> 2) == part, base + place - 4 * part, -1)
            chosen = jnp.where(want == rank, 1.0, 0.0).astype(BF16)
            left[:, part * SAMPLES : (part + 1) * SAMPLES] = product(
                chosen, lows[part * SAMPLES : (part + 1) * SAMPLES, :], 1, 1
            ).astype(BF16)

    def grads(left, out, group):
        @pl.loop(0, WIDTH // 384)
        def _(part):
            at = pl.ds(pl.multiple_of(part * 384, 384), 384)
            out[group * 128 : (group + 1) * 128, at] = product(
                left[group * 128 : (group + 1) * 128, :], rights[:, at]
            )

    for copy in operands:
        copy.wait()
    for table in range(TR):
        value = small[:, table * EMB : (table + 1) * EMB]
        high = value.astype(BF16)
        split[table, :, 0:EMB] = high
        split[table, :, EMB:] = (value - high.astype(F32)).astype(BF16)

    def small_sums(target, out, group):
        @pl.loop(0, 4)
        def _(part):
            block = (group * 4 + part) * 2 + target
            rows = (block % 8) * 128 + lax.broadcasted_iota(jnp.int32, (128, SAMPLES), 0)
            wanted = small_ids[group]
            counts = jnp.zeros((128, SAMPLES), F32)
            for k in range(HOT):
                counts = counts + jnp.where(rows == wanted[k : k + 1, :], 1.0, 0.0)
            both = product(counts.astype(BF16), split[group])
            total = both[:, 0:EMB] + both[:, EMB:]
            for x in range(LOCALS):
                at = pl.ds(pl.multiple_of((group * 4 + part) * 32 + x * 8, 8), 8)
                for tile in range(4):
                    start = x * 32 + tile * 8
                    lanes = pl.ds(WIDTH + tile * 128, 128)
                    out[at, lanes] = total[start : start + 8, :]

    def core_copy(group):
        rows = pl.ds(group * 128, 128)
        return pltpu.make_async_remote_copy(
            src_ref=other.at[rows],
            dst_ref=arrived.at[rows],
            send_sem=core_sems.at[0, group],
            recv_sem=core_sems.at[1, group],
            device_id={"hst": partner},
            device_id_type=MESH,
        )

    def out_copy(group):
        rows = pl.ds(group * 128, 128)
        return pltpu.make_async_copy(own.at[rows], dense.at[rows], out_sems.at[group])

    spread(1 - core, left_other)
    for group in range(4):
        grads(left_other, other, group)
        small_sums(1 - core, other, group)
        core_copy(group).start()
    for index in range(len(TIES)):
        halfway(index).wait_recv()
        for target in range(2):
            onward(index, target).start()
    spread(core, left_own)
    for group in range(4):
        grads(left_own, own, group)
        small_sums(core, own, group)
    for group in range(4):
        core_copy(group).wait_recv()

        @pl.loop(0, 4)
        def _(part):
            rows = pl.ds(pl.multiple_of(group * 128 + part * 32, 32), 32)
            own[rows, :] = own[rows, :] + arrived[rows, :]

        out_copy(group).start()

    mine.wait()
    from_neighbour().wait_recv()
    for off in STRAIGHT + TIES:
        for source_core in range(2):
            arrival(off, source_core).wait_recv()

    @pl.loop(0, HOSTS // 2)
    def _(pair):
        low = got[pair * 2, pl.ds(SAMPLES, 8), :]
        high = got[pair * 2 + 1, pl.ds(SAMPLES, 8), :]
        ids[pl.ds(pl.multiple_of(pair * 8, 8), 8), :] = jnp.concatenate(
            [low[0:HOT], high[0:HOT]], axis=0
        ).astype(jnp.int32)

    result = pltpu.make_async_copy(got, got_hbm, own_sem)
    result.start()
    neighbour().wait_send()
    for off in STRAIGHT:
        for target in range(2):
            straight(off, target).wait_send()
    for index in range(len(TIES)):
        halfway(index).wait_send()
        for target in range(2):
            onward(index, target).wait_send()
    for group in range(4):
        core_copy(group).wait_send()
        out_copy(group).wait()
    result.wait()


def pooled_kernel(ids, grads_hbm, out, grads, *scratch):
    sums, sem, in_sem = scratch[:HOT], scratch[HOT], scratch[HOT + 1]
    operand = pltpu.make_async_copy(grads_hbm, grads, in_sem)
    operand.start()
    row_total = out.shape[0]
    step = 256

    @pl.loop(0, row_total // step)
    def _(i):
        rows = pl.ds(pl.multiple_of(i * step, step), step)
        for total in sums:
            total[rows, :] = jnp.zeros((step, EMB), F32)

    operand.wait()

    @pl.loop(0, HOSTS)
    def _(source):
        @pl.loop(0, SAMPLES // 16)
        def _(group):
            for pair in range(8):
                sample = group * 16 + pair * 2
                first = grads[source, pl.ds(sample, 1), :]
                second = grads[source, pl.ds(sample + 1, 1), :]
                at = [
                    ids[(source * HOT + k % HOT) * SAMPLES + sample + k // HOT]
                    for k in range(2 * HOT)
                ]
                held = [sums[k % HOT][pl.ds(at[k], 1), :] for k in range(2 * HOT)]
                new = [held[k] + first for k in range(HOT)]
                for k in range(HOT):
                    new.append(jnp.where(at[k] == at[HOT + k], new[k], held[HOT + k]) + second)
                for k in range(2 * HOT):
                    sums[k % HOT][pl.ds(at[k], 1), :] = new[k]

    @pl.loop(0, row_total // step)
    def _(i):
        rows = pl.ds(pl.multiple_of(i * step, step), step)
        sums[0][rows, :] = (sums[0][rows, :] + sums[1][rows, :]) + (
            sums[2][rows, :] + sums[3][rows, :]
        )
        pltpu.make_async_copy(sums[0].at[rows], out.at[rows], sem.at[i]).start()

    @pl.loop(0, row_total // step)
    def _(i):
        rows = pl.ds(pl.multiple_of(i * step, step), step)
        pltpu.make_async_copy(sums[0].at[rows], out.at[rows], sem.at[i]).wait()


class Ring:
    def __init__(self, place, right, left, sent, held, near, passed, sums, sems, chunks=1):
        self.place, self.right, self.left = place, right, left
        self.sent, self.held, self.near, self.passed = sent, held, near, passed
        self.sums, self.sems, self.chunks = sums, sems, chunks

    def piece(self, ref, chunk):
        if self.chunks == 1:
            return ref
        rows = ref.shape[0] // self.chunks
        return ref.at[pl.ds(chunk * rows, rows)]

    def copy(self, src, dst, kind, side, chunk):
        index = (kind * 2 + side) * self.chunks + chunk
        return pltpu.make_async_remote_copy(
            src_ref=self.piece(src, chunk), dst_ref=self.piece(dst, chunk),
            send_sem=self.sems.at[0, index], recv_sem=self.sems.at[1, index],
            device_id=self.left if side else self.right, device_id_type=MESH,
        )

    def next(self, side):
        return lax.rem(self.place + (3 if side else 1), 4)

    def far(self, side, chunk=0):
        src = self.sent(lax.rem(self.place + 2, 4), side)
        return self.copy(src, self.passed[side], 0, side, chunk)

    def direct(self, side, chunk=0):
        return self.copy(self.sent(self.next(side), 1 - side), self.near[side], 1, side, chunk)

    def relay(self, side, chunk=0):
        return self.copy(self.passed[side], self.sums[side], 2, side, chunk)

    def start(self, chunk=0):
        for side in range(2):
            self.far(side, chunk).start()

    def middle(self, chunk=0):
        for side in range(2):
            self.far(side, chunk).wait_recv()
            add_into(
                self.piece(self.passed[side], chunk),
                self.piece(self.held(self.next(side), side), chunk),
            )
            self.relay(side, chunk).start()
            self.direct(side, chunk).start()

    def arrive(self, chunk=0):
        for side in range(2):
            self.relay(side, chunk).wait_recv()
            self.direct(side, chunk).wait_recv()

    def finish(self, outs):
        self.arrive()
        add_three(outs[0], self.held(self.place, 0), self.sums[0], self.near[1])
        add_three(outs[1], self.held(self.place, 1), self.near[0], self.sums[1])

    def drain(self):
        for chunk in range(self.chunks):
            for side in range(2):
                self.far(side, chunk).wait_send()
                self.direct(side, chunk).wait_send()
                self.relay(side, chunk).wait_send()


def blocks_of(shape):
    if len(shape) == 3:
        return shape[0], lambda ref, i: ref.at[i]
    rows = min(shape[0], 32 if shape[1] > 256 else 128)
    return shape[0] // rows, lambda ref, i: ref.at[pl.ds(pl.multiple_of(i * rows, rows), rows)]


def add_into(total, term):
    count, at = blocks_of(total.shape)

    @pl.loop(0, count)
    def _(i):
        at(total, i)[...] = at(total, i)[...] + at(term, i)[...]


def add_three(out, first, second, third):
    count, at = blocks_of(out.shape)

    @pl.loop(0, count)
    def _(i):
        at(out, i)[...] = at(first, i)[...] + at(second, i)[...] + at(third, i)[...]


CHUNKS = 8
AHEAD = 3


def reduce_kernel(
    tables, dense, store_hbm, small_hbm, acc, small_acc, down_acc, up_acc,
    table_new, acc_new, small_new, small_acc_new, down_step, up_step,
    store, small, gathered, mine, ahead, behind, grads,
    t_near0, t_near1, t_pass0, t_pass1, t_sum0, t_sum1,
    a_near0, a_near1, a_pass0, a_pass1, a_sum0, a_sum1,
    b_near0, b_near1, b_pass0, b_pass1, b_sum0, b_sum1,
    c_near0, c_near1, c_pass0, c_pass1, c_sum0, c_sum1,
    d_near0, d_near1, d_pass0, d_pass1, d_sum0, d_sum1,
    e_near0, e_near1, e_pass0, e_pass1, e_sum0, e_sum1,
    a_out, b_out, c_out, d_out,
    t_sems, r_sems, g_sems, local_sems,
):
    host = lax.axis_index("hst")
    x = lax.axis_index("local")
    z, y, core = host // 8, (host // 2) % 4, host % 2

    def on_z(step):
        return {"hst": (lax.rem(z + step, 4) * 4 + y) * 2 + core}

    def on_y(step):
        return {"hst": (z * 4 + lax.rem(y + step, 4)) * 2 + core}

    def on_x(step):
        return {"local": lax.rem(x + step, 4)}

    barrier = pltpu.get_barrier_semaphore()
    for neighbours in (on_x, on_y, on_z):
        for step in (1, 2, 3):
            pl.semaphore_signal(
                barrier, inc=1, device_id=neighbours(step), device_id_type=MESH
            )
    partner = {"hst": host + 1 - 2 * core}
    pl.semaphore_signal(barrier, inc=1, device_id=partner, device_id_type=MESH)
    half = SHARD // 2
    right, left = lax.rem(x + 1, 4), lax.rem(x + 3, 4)
    locals_ = [
        pltpu.make_async_copy(tables.at[right, pl.ds(0, half)], ahead, local_sems.at[0]),
        pltpu.make_async_copy(tables.at[left, pl.ds(half, half)], behind, local_sems.at[1]),
        pltpu.make_async_copy(dense, grads, local_sems.at[2]),
        pltpu.make_async_copy(tables.at[x], mine, local_sems.at[3]),
        pltpu.make_async_copy(store_hbm, store, local_sems.at[4]),
        pltpu.make_async_copy(small_hbm, small, local_sems.at[5]),
    ]
    for copy in locals_:
        copy.start()
    pl.semaphore_wait(barrier, 10)

    first = {0: pl.ds(0, 1024), 1: pl.ds(1024, 1024)}
    second = {0: pl.ds(CUT, 1024), 1: pl.ds(CUT + 1024, 896)}
    inner = {0: pl.ds(0, 1024), 1: pl.ds(1024, 896)}
    table_ring = Ring(
        x, on_x(1), on_x(3),
        lambda t, s: tables.at[t, pl.ds(s * half, half)],
        lambda t, s: behind if s else ahead,
        (t_near0, t_near1), (t_pass0, t_pass1), (t_sum0, t_sum1), t_sems, CHUNKS,
    )
    a_ring = Ring(
        z, on_z(1), on_z(3),
        lambda t, s: dense.at[t, :, :, first[s]],
        lambda t, s: grads.at[t, :, :, first[s]],
        (a_near0, a_near1), (a_pass0, a_pass1), (a_sum0, a_sum1), r_sems.at[0],
    )
    b_ring = Ring(
        y, on_y(1), on_y(3),
        lambda t, s: dense.at[:, t, :, second[s]],
        lambda t, s: grads.at[:, t, :, second[s]],
        (b_near0, b_near1), (b_pass0, b_pass1), (b_sum0, b_sum1), r_sems.at[1],
    )
    c_at = lambda t, s: a_out.at[t, :, first[s]]
    c_ring = Ring(
        y, on_y(1), on_y(3), c_at, c_at, (c_near0, c_near1), (c_pass0, c_pass1), (c_sum0, c_sum1), r_sems.at[2]
    )
    d_at = lambda t, s: b_out.at[t, :, inner[s]]
    d_ring = Ring(
        z, on_z(1), on_z(3), d_at, d_at, (d_near0, d_near1), (d_pass0, d_pass1), (d_sum0, d_sum1), r_sems.at[3]
    )
    e_at = lambda t, s: (d_out if s else c_out).at[pl.ds(pl.multiple_of(t * 8, 8), 8)]
    e_ring = Ring(
        x, on_x(1), on_x(3), e_at, e_at, (e_near0, e_near1), (e_pass0, e_pass1), (e_sum0, e_sum1), r_sems.at[4]
    )

    eye = diagonal()

    def update(block, grad, before, acc_before, after, acc_after):
        rows = pl.ds(pl.multiple_of(block * 128, 128), 128)
        at = pl.ds(block, 1)
        acc_here = jnp.sum(jnp.where(eye, acc_before[at, :], 0.0), axis=1, keepdims=True)
        total = acc_here + jnp.sum(grad * grad, axis=1, keepdims=True) * (1.0 / EMB)
        after[rows, :] = before[rows, :] - grad * (LEARN_RATE * lax.rsqrt(total))
        acc_after[at, :] = jnp.sum(jnp.where(eye, total, 0.0), axis=0, keepdims=True)

    def finish_dense(side, start, stop):
        near = (e_near1, e_near0)[side]
        at = pl.ds(start, stop - start)
        return e_ring.held(x, side)[:, at] + e_ring.sums[side][:, at] + near[:, at]

    halves = (pl.ds(0, 256), pl.ds(256, 256))

    def gather_copy(index, view, to):
        return pltpu.make_async_remote_copy(
            src_ref=view, dst_ref=view, send_sem=g_sems.at[0, index],
            recv_sem=g_sems.at[1, index], device_id=to, device_id_type=MESH,
        )

    def stage(number, back):
        copies = []
        for step in (1, 2, 3):
            there = lax.rem(4 - step, 4) if back else 0
            at_z, at_y, at_x = (lax.rem(place + there, 4) for place in (z, y, x))
            if number == 0:
                views = [(gathered.at[z, y, core, at_x], on_x)]
            elif number == 1:
                views = [
                    (gathered.at[z, at_y, core, :, :, halves[0]], on_y),
                    (gathered.at[at_z, y, core, :, :, halves[1]], on_z),
                ]
            else:
                views = [
                    (gathered.at[at_z, :, core, :, :, halves[0]], on_z),
                    (gathered.at[:, at_y, core, :, :, halves[1]], on_y),
                ]
            for view, axis in views:
                copies.append(gather_copy(number * 6 + len(copies), view, axis(step)))
        return copies

    def begin(number):
        for copy in stage(number, False):
            copy.start()

    def arrived(number):
        for copy in stage(number, True):
            copy.wait_recv()

    def pass_on(chunk):
        table_ring.middle(chunk)
        if chunk + AHEAD < CHUNKS:
            table_ring.start(chunk + AHEAD)

    rows_chunk = half // CHUNKS

    def update_tables(chunk):
        table_ring.arrive(chunk)
        for side in range(2):
            near = (t_near1, t_near0)[side]

            @pl.loop(0, rows_chunk // 128)
            def _(part):
                inside = pl.ds(pl.multiple_of(chunk * rows_chunk + part * 128, 128), 128)
                block = side * (half // 128) + chunk * (rows_chunk // 128) + part
                rows = pl.ds(pl.multiple_of(block * 128, 128), 128)
                grad = mine[rows, :] + table_ring.sums[side][inside, :] + near[inside, :]
                update(block, grad, store, acc, table_new, acc_new)

    a_ring.start()
    b_ring.start()
    for chunk in range(AHEAD):
        table_ring.start(chunk)
    for copy in locals_[:3]:
        copy.wait()
    pass_on(0)
    a_ring.middle()
    b_ring.middle()
    pass_on(1)
    pass_on(2)
    pass_on(3)
    for copy in locals_[3:]:
        copy.wait()
    a_ring.finish([a_out.at[:, :, first[s]] for s in range(2)])
    c_ring.start()
    b_ring.finish([b_out.at[:, :, inner[s]] for s in range(2)])
    d_ring.start()
    update_tables(0)
    pass_on(4)
    c_ring.middle()
    d_ring.middle()
    update_tables(1)
    c_ring.finish([c_out.at[:, first[s]] for s in range(2)])
    d_ring.finish([d_out.at[:, inner[s]] for s in range(2)])
    e_ring.start()
    pass_on(5)
    e_ring.middle()
    update_tables(2)
    e_ring.arrive()
    gathered[z, y, core, x] = finish_dense(1, WIDTH - CUT, FULL - CUT)
    begin(0)
    pass_on(6)
    for side, stop in ((0, CUT), (1, WIDTH - CUT)):
        total = finish_dense(side, 0, stop)
        at = pl.ds(side * CUT, stop)
        for step, before, rows in ((down_step, down_acc, 0), (up_step, up_acc, 4)):
            grad = total[rows : rows + 4]
            step[:, at] = grad * lax.rsqrt(before[:, at] + grad * grad)
    arrived(0)
    begin(1)
    update_tables(3)
    update_tables(4)
    arrived(1)
    begin(2)
    pass_on(7)
    update_tables(5)
    arrived(2)
    gather_copy(18, gathered.at[:, :, core], partner).start()
    update_tables(6)
    gather_copy(18, gathered.at[:, :, 1 - core], partner).wait_recv()

    @pl.loop(0, TR * RS // 128)
    def _(block):
        mixed = gathered.at[block // 8, (block // 2) % 4, block % 2]
        grad = jnp.concatenate(
            [
                mixed[place, :, tile * 128 : (tile + 1) * 128]
                for place in range(LOCALS)
                for tile in range(4)
            ],
            axis=0,
        )
        update(block, grad, small, small_acc, small_new, small_acc_new)

    update_tables(7)
    for ring in (table_ring, a_ring, b_ring, c_ring, d_ring, e_ring):
        ring.drain()
    for number in range(3):
        for copy in stage(number, False):
            copy.wait_send()
    gather_copy(18, gathered.at[:, :, core], partner).wait_send()


def shaped(shape, dtype=F32):
    return jax.ShapeDtypeStruct(shape, dtype)


HBM = pl.BlockSpec(memory_space=pltpu.HBM)
VMEM = pl.BlockSpec(memory_space=pltpu.VMEM)
SMEM = pl.BlockSpec(memory_space=pltpu.SMEM)
DMA = pltpu.SemaphoreType.DMA


def params(mebibytes, **others):
    return pltpu.CompilerParams(vmem_limit_bytes=mebibytes << 20, **others)


def on_device(
    features, labels, cross_down, cross_up, cross_bias, head_weight, head_bias, table_place,
    bag_rows, small_rows, table_store, table_acc, small_store, small_acc, down_acc, up_acc,
):
    bags = jnp.transpose(bag_rows, (1, 2, 0))
    small_ids = jnp.transpose(small_rows, (1, 2, 0))
    send, small, rights, lows = pl.pallas_call(
        dense_kernel,
        out_shape=(
            shaped((HOSTS, PACK, EMB)), shaped((SAMPLES, TR * EMB)),
            shaped((2 * SAMPLES, WIDTH), BF16), shaped((2 * SAMPLES, RANK), BF16),
        ),
        in_specs=[VMEM] * 3 + [SMEM] * 2 + [VMEM] + [HBM] * 3,
        out_specs=(VMEM,) * 4,
        scratch_shapes=[
            pltpu.VMEM((RANK, WIDTH), BF16), pltpu.VMEM((RANK, WIDTH), BF16),
            pltpu.VMEM((SAMPLES, WIDTH), F32), DMA((3,)),
        ],
        compiler_params=params(60),
        name="dense_backward",
    )(
        labels.reshape(1, -1), cross_bias.reshape(-1, 128), head_weight.reshape(-1, 128), head_bias,
        table_place, bags,
        features, cross_down, cross_up,
    )
    whole = (RANK, FULL)
    got, ids, dense = pl.pallas_call(
        exchange_kernel,
        out_shape=(
            shaped((HOSTS, PACK, EMB)), shaped((HOSTS * HOT, SAMPLES), jnp.int32), shaped(whole),
        ),
        in_specs=[HBM] * 4 + [VMEM],
        out_specs=(HBM, VMEM, HBM),
        scratch_shapes=[
            pltpu.VMEM((2 * SAMPLES, WIDTH), BF16), pltpu.VMEM((2 * SAMPLES, RANK), BF16),
            pltpu.VMEM((SAMPLES, TR * EMB), F32), pltpu.VMEM((HOSTS, PACK, EMB), F32),
            pltpu.VMEM((RANK, 2 * SAMPLES), BF16), pltpu.VMEM((RANK, 2 * SAMPLES), BF16),
            pltpu.VMEM(whole, F32), pltpu.VMEM(whole, F32), pltpu.VMEM(whole, F32),
            pltpu.VMEM((TR, SAMPLES, 2 * EMB), BF16),
            pltpu.VMEM((len(TIES), 2, PACK, EMB), F32),
            DMA((2, HOSTS)), DMA((2, len(TIES))), DMA((2, 4)), DMA((4,)), DMA((3,)), DMA,
        ],
        compiler_params=params(60, collective_id=0, has_side_effects=True),
        name="exchange",
    )(send, rights, lows, small, small_ids)
    tables = pl.pallas_call(
        pooled_kernel,
        out_shape=shaped((LOCALS * SHARD, EMB)),
        in_specs=[SMEM, HBM],
        out_specs=HBM,
        scratch_shapes=[pltpu.VMEM((HOSTS, PACK, EMB), F32)]
        + [pltpu.VMEM((LOCALS * SHARD, EMB), F32)] * HOT
        + [DMA((LOCALS * SHARD // 256,)), DMA],
        compiler_params=params(60),
        name="pooled_rows",
    )(ids.reshape(-1), got)

    def ring_buffers(first_shape, second_shape):
        near = [pltpu.VMEM(second_shape, F32), pltpu.VMEM(first_shape, F32)]
        return near + [pltpu.VMEM(first_shape, F32), pltpu.VMEM(second_shape, F32)] * 2

    rest = FULL - CUT
    half = SHARD // 2
    table_new, acc_new, small_new, small_acc_new, down_step, up_step = pl.pallas_call(
        reduce_kernel,
        out_shape=(
            shaped((SHARD, EMB)), shaped((SHARD // 128, 128)),
            shaped((TR * RS, EMB)), shaped((TR * RS // 128, 128)),
            shaped((4, WIDTH)), shaped((4, WIDTH)),
        ),
        in_specs=[HBM] * 4 + [VMEM] * 4,
        out_specs=(VMEM,) * 6,
        scratch_shapes=[
            pltpu.VMEM((SHARD, EMB), F32), pltpu.VMEM((TR * RS, EMB), F32),
            pltpu.VMEM((4, 4, 2, LOCALS, 8, TR * EMB), F32), pltpu.VMEM((SHARD, EMB), F32),
            pltpu.VMEM((half, EMB), F32), pltpu.VMEM((half, EMB), F32),
            pltpu.VMEM((4, 4, 32, FULL), F32),
        ]
        + ring_buffers((half, EMB), (half, EMB))
        + ring_buffers((4, 32, 1024), (4, 32, 1024))
        + ring_buffers((4, 32, 1024), (4, 32, 896))
        + ring_buffers((32, 1024), (32, 1024))
        + ring_buffers((32, 1024), (32, 896))
        + ring_buffers((8, CUT), (8, rest))
        + [
            pltpu.VMEM((4, 32, CUT), F32), pltpu.VMEM((4, 32, rest), F32),
            pltpu.VMEM((32, CUT), F32), pltpu.VMEM((32, rest), F32),
            DMA((2, 6 * CHUNKS)), DMA((5, 2, 6)), DMA((2, 19)), DMA((6,)),
        ],
        compiler_params=params(40, collective_id=1, has_side_effects=True),
        name="reduce_update",
    )(
        tables.reshape(LOCALS, SHARD, EMB), dense.reshape(4, 4, 32, FULL), table_store, small_store,
        table_acc.reshape(-1, 128), small_acc.reshape(-1, 128), down_acc, up_acc,
    )
    return (
        table_new, acc_new.reshape(-1), small_new, small_acc_new.reshape(-1), down_step, up_step,
    )


def solution(mesh):
    both = ("hst", "local")
    rows = P(both, None)
    return jax.shard_map(
        on_device,
        mesh=mesh,
        in_specs=(
            rows, P(both), P(), P(), P(), P(), P(), P(), P(both, None, None), P(both, None, None),
            rows, P(both), P(), P(), rows, rows,
        ),
        out_specs=(rows, P(both), P(), P(), rows, rows),
        check_vma=False,
    )
```

```python
import functools

import jax
import jax.numpy as jnp
from jax import lax
from jax.experimental import pallas as pl
from jax.experimental.pallas import tpu as pltpu
from jax.sharding import PartitionSpec as P

TS = 22
TR = 4
RS = 1024
HOT = 4
SHARD = 4096
EMB = 128
RANK = 512
WIDTH = 3456
HOSTS = 32
LOCALS = 4
SAMPLES = 128
PACK = SAMPLES + 8
FULL = WIDTH + EMB
CUT = 1792
TIES = ((2, 0), (2, 1), (2, 3), (0, 2), (1, 2), (3, 2), (2, 2))
STRAIGHT = ((0, 1), (0, 3), (1, 0), (3, 0), (1, 1), (1, 3), (3, 1), (3, 3))
LEARN_RATE = 0.05
MESH = pl.DeviceIdType.MESH
F32 = jnp.float32
BF16 = jnp.bfloat16


def product(left, right, left_dim=1, right_dim=0):
    return lax.dot_general(
        left, right, (((left_dim,), (right_dim,)), ((), ())), preferred_element_type=F32
    )


def diagonal():
    return lax.broadcasted_iota(jnp.int32, (128, 128), 0) == lax.broadcasted_iota(
        jnp.int32, (128, 128), 1
    )


def dense_kernel(
    labels, bias, head, head_bias, place, bags, small_ids, features_hbm, down_hbm, up_hbm,
    send, small, rights, lows, down, up, cross, sems,
):
    features = rights.at[0:SAMPLES]
    features_copy = pltpu.make_async_copy(features_hbm, features, sems.at[2])
    down_copy = pltpu.make_async_copy(down_hbm, down, sems.at[0])
    up_copy = pltpu.make_async_copy(up_hbm, up, sems.at[1])
    features_copy.start()
    down_copy.start()
    up_copy.start()

    @pl.loop(0, HOSTS)
    def _(slot):
        send[slot] = jnp.zeros((PACK, EMB), F32)

    for table in range(TR):
        small[table, SAMPLES:, :] = jnp.zeros((PACK - SAMPLES, EMB), F32)
        small[table, SAMPLES : SAMPLES + HOT, :] = small_ids[table].astype(F32)

    parts = [(start, min(256, WIDTH - start)) for start in range(0, WIDTH, 256)]

    def tiles(ref, start, width):
        rows = [ref[t : t + 1, :] for t in range(start // 128, (start + width) // 128)]
        return jnp.concatenate(rows, axis=1)

    features_copy.wait()
    down_copy.wait()
    low_proj = product(features[...], down[...], 1, 1).astype(BF16)
    lows[SAMPLES:, :] = low_proj
    up_copy.wait()
    terms = jnp.zeros((SAMPLES, 128), F32)
    for start, width in parts:
        at = pl.ds(start, width)
        out = product(low_proj, up[:, at]) + tiles(bias, start, width)
        cross[:, at] = out
        wide = features[:, at].astype(F32)
        weighted = (wide * out + wide) * tiles(head, start, width)
        for tile in range(width // 128):
            terms = terms + weighted[:, tile * 128 : (tile + 1) * 128]
    logit = jnp.sum(terms, axis=1, keepdims=True) + head_bias[0]
    label = jnp.sum(
        jnp.where(diagonal(), labels[...].astype(F32), 0.0), axis=1, keepdims=True
    )
    logit_grad = jax.nn.sigmoid(logit) - label
    for start, width in parts:
        at = pl.ds(start, width)
        layer_grad = logit_grad * tiles(head, start, width)
        rights[SAMPLES:, at] = (layer_grad * features[:, at].astype(F32)).astype(BF16)
    low_grad = product(rights[SAMPLES:, :], up[...], 1, 1).astype(BF16)
    lows[0:SAMPLES, :] = low_grad
    for start, width in parts:
        at = pl.ds(start, width)
        layer_grad = logit_grad * tiles(head, start, width)
        grad = layer_grad * (cross[:, at] + 1.0) + product(low_grad, down[:, at])
        for tile in range(width // 128):
            piece = grad[:, tile * 128 : (tile + 1) * 128]
            table = start // 128 + tile - 1
            if 0 <= table < TS:
                slot = place[table]
                send[slot, 0:SAMPLES, :] = piece
                send[slot, SAMPLES : SAMPLES + HOT, :] = bags[table].astype(F32)
            elif table >= TS:
                small[table - TS, 0:SAMPLES, :] = piece


def exchange_kernel(
    send, rights_hbm, lows_hbm, small_hbm,
    got_hbm, ids, dense,
    rights, lows, small, got, left_own, left_other, own, other, arrived, split, relayed,
    sems, relay_sems, core_sems, small_sems, out_sems, in_sems, own_sem,
):
    host = lax.axis_index("hst")
    core = lax.rem(host, 2)
    z, y = host // 8, (host // 2) % 4
    x = lax.axis_index("local")
    partner = host + 1 - 2 * core
    operands = [
        pltpu.make_async_copy(source, target, in_sems.at[i])
        for i, (source, target) in enumerate(
            ((lows_hbm, lows), (rights_hbm, rights), (small_hbm.at[x], small.at[x]))
        )
    ]
    for copy in operands:
        copy.start()
    barrier = pltpu.get_barrier_semaphore()

    @pl.loop(1, HOSTS)
    def _(off):
        pl.semaphore_signal(
            barrier, inc=1, device_id={"hst": lax.rem(host + off, HOSTS)}, device_id_type=MESH
        )

    def chip(dz, dy):
        return (lax.rem(z + dz + 4, 4) * 4 + lax.rem(y + dy + 4, 4)) * 2

    def bag_copy(src, to, slot, off, cores):
        at = (off[0] * 4 + off[1]) * 2
        return pltpu.make_async_remote_copy(
            src_ref=src,
            dst_ref=got.at[slot],
            send_sem=sems.at[0, at + cores[1]],
            recv_sem=sems.at[1, at + cores[0]],
            device_id={"hst": to},
            device_id_type=MESH,
        )

    def straight(off, target):
        to = chip(*off) + target
        return bag_copy(send.at[to], to, host, off, (core, target))

    turn = 1 - 2 * core

    def halfway(index):
        dz, dy = TIES[index]
        to = chip(turn if dz == 2 else 0, turn if dy == 2 else 0) + core
        return pltpu.make_async_remote_copy(
            src_ref=send.at[pl.ds(chip(dz, dy), 2)],
            dst_ref=relayed.at[index],
            send_sem=relay_sems.at[0, index],
            recv_sem=relay_sems.at[1, index],
            device_id={"hst": to},
            device_id_type=MESH,
        )

    def onward(index, target):
        dz, dy = TIES[index]
        to = chip(turn if dz == 2 else dz, turn if dy == 2 else dy) + target
        source = chip(-turn if dz == 2 else 0, -turn if dy == 2 else 0) + core
        return bag_copy(relayed.at[index, target], to, source, TIES[index], (core, target))

    def arrival(off, source_core):
        source = chip(-off[0], -off[1]) + source_core
        return bag_copy(send.at[source], source, source, off, (source_core, source_core))

    def neighbour():
        return pltpu.make_async_remote_copy(
            src_ref=send.at[partner],
            dst_ref=got.at[host],
            send_sem=sems.at[0, 0],
            recv_sem=sems.at[1, 0],
            device_id={"hst": partner},
            device_id_type=MESH,
        )

    def from_neighbour():
        return pltpu.make_async_remote_copy(
            src_ref=send.at[partner],
            dst_ref=got.at[partner],
            send_sem=sems.at[0, 0],
            recv_sem=sems.at[1, 0],
            device_id={"hst": partner},
            device_id_type=MESH,
        )

    for step in (1, 2, 3):
        pl.semaphore_signal(
            barrier, inc=1, device_id={"local": lax.rem(x + step, 4)}, device_id_type=MESH
        )

    def small_copy(step, slot):
        to = lax.rem(x + step, 4)
        return pltpu.make_async_remote_copy(
            src_ref=small_hbm.at[to],
            dst_ref=small.at[slot],
            send_sem=small_sems.at[0, step],
            recv_sem=small_sems.at[1, step],
            device_id={"local": to},
            device_id_type=MESH,
        )

    pl.semaphore_wait(barrier, HOSTS + 2)
    for step in (1, 2, 3):
        small_copy(step, x).start()
    for index in range(len(TIES)):
        halfway(index).start()
    for off in STRAIGHT:
        for target in range(2):
            straight(off, target).start()
    neighbour().start()
    mine = pltpu.make_async_copy(send.at[host], got.at[host], own_sem)
    mine.start()

    def spread(target, left):
        row = lax.broadcasted_iota(jnp.int32, (RANK, RANK), 0)
        rank = lax.broadcasted_iota(jnp.int32, (RANK, RANK), 1)
        place = row & 7
        base = ((row >> 5) * 2 + target) * 16 + ((row >> 3) & 3) * 4
        for part in range(2):
            want = jnp.where((place >> 2) == part, base + place - 4 * part, -1)
            chosen = jnp.where(want == rank, 1.0, 0.0).astype(BF16)
            left[:, part * SAMPLES : (part + 1) * SAMPLES] = product(
                chosen, lows[part * SAMPLES : (part + 1) * SAMPLES, :], 1, 1
            ).astype(BF16)

    def grads(left, out, group):
        @pl.loop(0, WIDTH // 384)
        def _(part):
            at = pl.ds(pl.multiple_of(part * 384, 384), 384)
            out[group * 128 : (group + 1) * 128, at] = product(
                left[group * 128 : (group + 1) * 128, :], rights[:, at]
            )

    for copy in operands:
        copy.wait()
    for step in (1, 2, 3):
        small_copy(step, lax.rem(x - step + 4, 4)).wait_recv()

    @pl.loop(0, LOCALS)
    def _(source):
        value = small[source, pl.ds(0, SAMPLES), :]
        high = value.astype(BF16)
        split[source, :, 0:EMB] = high
        split[source, :, EMB:] = (value - high.astype(F32)).astype(BF16)

    def small_sums(target, out, group):
        spot = group * 128 + lax.broadcasted_iota(jnp.int32, (128, SAMPLES), 0)
        row = ((spot >> 5) * 64 + target * 32 + (spot & 31)).astype(F32)
        here = pl.ds(group * 128, 128)
        lanes = pl.ds(WIDTH, EMB)
        out[here, lanes] = jnp.zeros((128, EMB), F32)

        @pl.loop(0, LOCALS)
        def _(source):
            wanted = small[source, pl.ds(SAMPLES, 8), :]
            counts = jnp.zeros((128, SAMPLES), F32)
            for k in range(HOT):
                counts = counts + jnp.where(row == wanted[k : k + 1, :], 1.0, 0.0)
            both = product(counts.astype(BF16), split[source])
            out[here, lanes] = out[here, lanes] + (both[:, 0:EMB] + both[:, EMB:])

    def core_copy(group):
        rows = pl.ds(group * 128, 128)
        return pltpu.make_async_remote_copy(
            src_ref=other.at[rows],
            dst_ref=arrived.at[rows],
            send_sem=core_sems.at[0, group],
            recv_sem=core_sems.at[1, group],
            device_id={"hst": partner},
            device_id_type=MESH,
        )

    def out_copy(group):
        rows = pl.ds(group * 128, 128)
        return pltpu.make_async_copy(own.at[rows], dense.at[rows], out_sems.at[group])

    spread(1 - core, left_other)
    for group in range(4):
        grads(left_other, other, group)
        small_sums(1 - core, other, group)
        core_copy(group).start()
    for index in range(len(TIES)):
        halfway(index).wait_recv()
        for target in range(2):
            onward(index, target).start()
    spread(core, left_own)
    for group in range(4):
        grads(left_own, own, group)
        small_sums(core, own, group)
    for group in range(4):
        core_copy(group).wait_recv()

        @pl.loop(0, 4)
        def _(part):
            rows = pl.ds(pl.multiple_of(group * 128 + part * 32, 32), 32)
            own[rows, :] = own[rows, :] + arrived[rows, :]

        out_copy(group).start()

    mine.wait()
    from_neighbour().wait_recv()
    for off in STRAIGHT + TIES:
        for source_core in range(2):
            arrival(off, source_core).wait_recv()

    @pl.loop(0, HOSTS // 2)
    def _(pair):
        low = got[pair * 2, pl.ds(SAMPLES, 8), :]
        high = got[pair * 2 + 1, pl.ds(SAMPLES, 8), :]
        ids[pl.ds(pl.multiple_of(pair * 8, 8), 8), :] = jnp.concatenate(
            [low[0:HOT], high[0:HOT]], axis=0
        ).astype(jnp.int32)

    result = pltpu.make_async_copy(got, got_hbm, own_sem)
    result.start()
    neighbour().wait_send()
    for step in (1, 2, 3):
        small_copy(step, x).wait_send()
    for off in STRAIGHT:
        for target in range(2):
            straight(off, target).wait_send()
    for index in range(len(TIES)):
        halfway(index).wait_send()
        for target in range(2):
            onward(index, target).wait_send()
    for group in range(4):
        core_copy(group).wait_send()
        out_copy(group).wait()
    result.wait()


def pooled_kernel(ids, grads_hbm, out, grads, *scratch):
    sums, sem, in_sem = scratch[:HOT], scratch[HOT], scratch[HOT + 1]
    operand = pltpu.make_async_copy(grads_hbm, grads, in_sem)
    operand.start()
    row_total = out.shape[0]
    step = 256

    @pl.loop(0, row_total // step)
    def _(i):
        rows = pl.ds(pl.multiple_of(i * step, step), step)
        for total in sums:
            total[rows, :] = jnp.zeros((step, EMB), F32)

    operand.wait()

    @pl.loop(0, HOSTS)
    def _(source):
        @pl.loop(0, SAMPLES // 16)
        def _(group):
            for pair in range(8):
                sample = group * 16 + pair * 2
                first = grads[source, pl.ds(sample, 1), :]
                second = grads[source, pl.ds(sample + 1, 1), :]
                at = [
                    ids[(source * HOT + k % HOT) * SAMPLES + sample + k // HOT]
                    for k in range(2 * HOT)
                ]
                held = [sums[k % HOT][pl.ds(at[k], 1), :] for k in range(2 * HOT)]
                new = [held[k] + first for k in range(HOT)]
                for k in range(HOT):
                    new.append(jnp.where(at[k] == at[HOT + k], new[k], held[HOT + k]) + second)
                for k in range(2 * HOT):
                    sums[k % HOT][pl.ds(at[k], 1), :] = new[k]

    @pl.loop(0, row_total // step)
    def _(i):
        rows = pl.ds(pl.multiple_of(i * step, step), step)
        sums[0][rows, :] = (sums[0][rows, :] + sums[1][rows, :]) + (
            sums[2][rows, :] + sums[3][rows, :]
        )
        pltpu.make_async_copy(sums[0].at[rows], out.at[rows], sem.at[i]).start()

    @pl.loop(0, row_total // step)
    def _(i):
        rows = pl.ds(pl.multiple_of(i * step, step), step)
        pltpu.make_async_copy(sums[0].at[rows], out.at[rows], sem.at[i]).wait()


class Ring:
    def __init__(self, place, right, left, sent, held, near, passed, sums, sems, chunks=1):
        self.place, self.right, self.left = place, right, left
        self.sent, self.held, self.near, self.passed = sent, held, near, passed
        self.sums, self.sems, self.chunks = sums, sems, chunks

    def piece(self, ref, chunk):
        if self.chunks == 1:
            return ref
        rows = ref.shape[0] // self.chunks
        return ref.at[pl.ds(chunk * rows, rows)]

    def copy(self, src, dst, kind, side, chunk):
        index = (kind * 2 + side) * self.chunks + chunk
        return pltpu.make_async_remote_copy(
            src_ref=self.piece(src, chunk), dst_ref=self.piece(dst, chunk),
            send_sem=self.sems.at[0, index], recv_sem=self.sems.at[1, index],
            device_id=self.left if side else self.right, device_id_type=MESH,
        )

    def next(self, side):
        return lax.rem(self.place + (3 if side else 1), 4)

    def far(self, side, chunk=0):
        src = self.sent(lax.rem(self.place + 2, 4), side)
        return self.copy(src, self.passed[side], 0, side, chunk)

    def direct(self, side, chunk=0):
        return self.copy(self.sent(self.next(side), 1 - side), self.near[side], 1, side, chunk)

    def relay(self, side, chunk=0):
        return self.copy(self.passed[side], self.sums[side], 2, side, chunk)

    def start(self, chunk=0):
        for side in range(2):
            self.far(side, chunk).start()

    def start_direct(self, chunk=0):
        for side in range(2):
            self.direct(side, chunk).start()

    def middle(self, chunk=0):
        for side in range(2):
            self.far(side, chunk).wait_recv()
            add_into(
                self.piece(self.passed[side], chunk),
                self.piece(self.held(self.next(side), side), chunk),
            )
            self.relay(side, chunk).start()

    def arrive(self, chunk=0):
        for side in range(2):
            self.relay(side, chunk).wait_recv()
            self.direct(side, chunk).wait_recv()

    def finish(self, outs):
        self.arrive()
        add_three(outs[0], self.held(self.place, 0), self.sums[0], self.near[1])
        add_three(outs[1], self.held(self.place, 1), self.near[0], self.sums[1])

    def drain(self):
        for chunk in range(self.chunks):
            for side in range(2):
                self.far(side, chunk).wait_send()
                self.direct(side, chunk).wait_send()
                self.relay(side, chunk).wait_send()


def blocks_of(shape):
    if len(shape) == 3:
        return shape[0], lambda ref, i: ref.at[i]
    rows = min(shape[0], 32 if shape[1] > 256 else 128)
    return shape[0] // rows, lambda ref, i: ref.at[pl.ds(pl.multiple_of(i * rows, rows), rows)]


def add_into(total, term):
    count, at = blocks_of(total.shape)

    @pl.loop(0, count)
    def _(i):
        at(total, i)[...] = at(total, i)[...] + at(term, i)[...]


def add_three(out, first, second, third):
    count, at = blocks_of(out.shape)

    @pl.loop(0, count)
    def _(i):
        at(out, i)[...] = at(first, i)[...] + at(second, i)[...] + at(third, i)[...]


CHUNKS = 8


def reduce_kernel(
    tables, dense, store_hbm, small_hbm, acc, small_acc, down_acc, up_acc,
    table_new, acc_new, small_new, small_acc_new, down_step, up_step,
    store, small, gathered, mine, ahead, behind, grads,
    t_near0, t_near1, t_pass0, t_pass1, t_sum0, t_sum1,
    a_near0, a_near1, a_pass0, a_pass1, a_sum0, a_sum1,
    b_near0, b_near1, b_pass0, b_pass1, b_sum0, b_sum1,
    c_near0, c_near1, c_pass0, c_pass1, c_sum0, c_sum1,
    d_near0, d_near1, d_pass0, d_pass1, d_sum0, d_sum1,
    e_near0, e_near1, e_pass0, e_pass1, e_sum0, e_sum1,
    u_near0, u_near1, u_pass0, u_pass1, u_sum0, u_sum1,
    v_near0, v_near1, v_pass0, v_pass1, v_sum0, v_sum1,
    a_out, b_out, c_out, d_out, u_out,
    t_sems, r_sems, g_sems, local_sems,
):
    host = lax.axis_index("hst")
    x = lax.axis_index("local")
    z, y, core = host // 8, (host // 2) % 4, host % 2

    def on_z(step):
        return {"hst": (lax.rem(z + step, 4) * 4 + y) * 2 + core}

    def on_y(step):
        return {"hst": (z * 4 + lax.rem(y + step, 4)) * 2 + core}

    def on_x(step):
        return {"local": lax.rem(x + step, 4)}

    barrier = pltpu.get_barrier_semaphore()
    for neighbours in (on_x, on_y, on_z):
        for step in (1, 2, 3):
            pl.semaphore_signal(
                barrier, inc=1, device_id=neighbours(step), device_id_type=MESH
            )
    partner = {"hst": host + 1 - 2 * core}
    pl.semaphore_signal(barrier, inc=1, device_id=partner, device_id_type=MESH)
    half = SHARD // 2
    right, left = lax.rem(x + 1, 4), lax.rem(x + 3, 4)
    locals_ = [
        pltpu.make_async_copy(tables.at[right, pl.ds(0, half)], ahead, local_sems.at[0]),
        pltpu.make_async_copy(tables.at[left, pl.ds(half, half)], behind, local_sems.at[1]),
        pltpu.make_async_copy(dense, grads, local_sems.at[2]),
        pltpu.make_async_copy(tables.at[x], mine, local_sems.at[3]),
        pltpu.make_async_copy(store_hbm, store, local_sems.at[4]),
        pltpu.make_async_copy(small_hbm, small, local_sems.at[5]),
    ]
    for copy in locals_:
        copy.start()
    pl.semaphore_wait(barrier, 10)

    first = {0: pl.ds(0, 896), 1: pl.ds(896, 896)}
    second = {0: pl.ds(CUT, 896), 1: pl.ds(CUT + 896, 768)}
    inner = {0: pl.ds(0, 896), 1: pl.ds(896, 768)}
    third = pl.ds(WIDTH, EMB)
    pairs = (pl.ds(0, 2), pl.ds(2, 2))
    halves = (pl.ds(0, 16), pl.ds(16, 16))
    table_ring = Ring(
        x, on_x(1), on_x(3),
        lambda t, s: tables.at[t, pl.ds(s * half, half)],
        lambda t, s: behind if s else ahead,
        (t_near0, t_near1), (t_pass0, t_pass1), (t_sum0, t_sum1), t_sems, CHUNKS,
    )
    a_ring = Ring(
        z, on_z(1), on_z(3),
        lambda t, s: dense.at[t, :, :, first[s]],
        lambda t, s: grads.at[t, :, :, first[s]],
        (a_near0, a_near1), (a_pass0, a_pass1), (a_sum0, a_sum1), r_sems.at[0],
    )
    b_ring = Ring(
        y, on_y(1), on_y(3),
        lambda t, s: dense.at[:, t, :, second[s]],
        lambda t, s: grads.at[:, t, :, second[s]],
        (b_near0, b_near1), (b_pass0, b_pass1), (b_sum0, b_sum1), r_sems.at[1],
    )
    c_at = lambda t, s: a_out.at[t, :, first[s]]
    c_ring = Ring(
        y, on_y(1), on_y(3), c_at, c_at, (c_near0, c_near1), (c_pass0, c_pass1), (c_sum0, c_sum1), r_sems.at[2]
    )
    d_at = lambda t, s: b_out.at[t, :, inner[s]]
    d_ring = Ring(
        z, on_z(1), on_z(3), d_at, d_at, (d_near0, d_near1), (d_pass0, d_pass1), (d_sum0, d_sum1), r_sems.at[3]
    )
    u_ring = Ring(
        z, on_z(1), on_z(3),
        lambda t, s: dense.at[t, pairs[s], :, third],
        lambda t, s: grads.at[t, pairs[s], :, third],
        (u_near0, u_near1), (u_pass0, u_pass1), (u_sum0, u_sum1), r_sems.at[5],
    )
    v_at = lambda t, s: u_out.at[t, halves[s]]
    v_ring = Ring(
        y, on_y(1), on_y(3), v_at, v_at,
        (v_near0, v_near1), (v_pass0, v_pass1), (v_sum0, v_sum1), r_sems.at[6],
    )
    e_at = lambda t, s: (d_out if s else c_out).at[pl.ds(pl.multiple_of(t * 8, 8), 8)]
    e_ring = Ring(
        x, on_x(1), on_x(3), e_at, e_at, (e_near0, e_near1), (e_pass0, e_pass1), (e_sum0, e_sum1), r_sems.at[4]
    )

    eye = diagonal()

    def update(block, grad, before, acc_before, after, acc_after):
        rows = pl.ds(pl.multiple_of(block * 128, 128), 128)
        at = pl.ds(block, 1)
        acc_here = jnp.sum(jnp.where(eye, acc_before[at, :], 0.0), axis=1, keepdims=True)
        total = acc_here + jnp.sum(grad * grad, axis=1, keepdims=True) * (1.0 / EMB)
        after[rows, :] = before[rows, :] - grad * (LEARN_RATE * lax.rsqrt(total))
        acc_after[at, :] = jnp.sum(jnp.where(eye, total, 0.0), axis=0, keepdims=True)

    def finish_dense(side, start, stop):
        near = (e_near1, e_near0)[side]
        at = pl.ds(start, stop - start)
        return e_ring.held(x, side)[:, at] + e_ring.sums[side][:, at] + near[:, at]

    def gather_copy(index, view, to):
        return pltpu.make_async_remote_copy(
            src_ref=view, dst_ref=view, send_sem=g_sems.at[0, index],
            recv_sem=g_sems.at[1, index], device_id=to, device_id_type=MESH,
        )

    def stage(number, back):
        copies = []
        for step in (1, 2, 3):
            there = lax.rem(4 - step, 4) if back else 0
            at_z, at_y, at_x = (lax.rem(place + there, 4) for place in (z, y, x))
            if number == 0:
                views = [(gathered.at[at_x, z, y, core], on_x)]
            elif number == 1:
                views = [
                    (gathered.at[:, z, at_y, core, halves[0]], on_y),
                    (gathered.at[:, at_z, y, core, halves[1]], on_z),
                ]
            else:
                views = [
                    (gathered.at[:, at_z, :, core, halves[0]], on_z),
                    (gathered.at[:, :, at_y, core, halves[1]], on_y),
                ]
            for view, axis in views:
                copies.append(gather_copy(number * 6 + len(copies), view, axis(step)))
        return copies

    def begin(number):
        for copy in stage(number, False):
            copy.start()

    def arrived(number):
        for copy in stage(number, True):
            copy.wait_recv()

    rows_chunk = half // CHUNKS

    def update_tables(chunk):
        table_ring.arrive(chunk)
        for side in range(2):
            near = (t_near1, t_near0)[side]

            @pl.loop(0, rows_chunk // 128)
            def _(part):
                inside = pl.ds(pl.multiple_of(chunk * rows_chunk + part * 128, 128), 128)
                block = side * (half // 128) + chunk * (rows_chunk // 128) + part
                rows = pl.ds(pl.multiple_of(block * 128, 128), 128)
                grad = mine[rows, :] + table_ring.sums[side][inside, :] + near[inside, :]
                update(block, grad, store, acc, table_new, acc_new)

    def update_small():
        @pl.loop(0, TR * RS // 128)
        def _(block):
            chip = (block % 8) * 2
            pieces = gathered.at[block // 8, chip // 4]
            grad = jnp.concatenate(
                [pieces[chip % 4 + part // 2, part % 2] for part in range(4)], axis=0
            )
            update(block, grad, small, small_acc, small_new, small_acc_new)

    def finish_steps():
        e_ring.arrive()
        for side, stop in ((0, CUT), (1, WIDTH - CUT)):
            total = finish_dense(side, 0, stop)
            at = pl.ds(side * CUT, stop)
            for step, before, rows in ((down_step, down_acc, 0), (up_step, up_acc, 4)):
                grad = total[rows : rows + 4]
                step[:, at] = grad * lax.rsqrt(before[:, at] + grad * grad)

    u_ring.start()
    u_ring.start_direct()
    table_ring.start(0)
    table_ring.start(1)
    table_ring.start(2)
    table_ring.start(3)
    locals_[2].wait()
    u_ring.middle()
    u_ring.finish([u_out.at[pairs[s]] for s in range(2)])
    v_ring.start()
    v_ring.start_direct()
    a_ring.start()
    b_ring.start()
    v_ring.middle()
    v_ring.finish([gathered.at[x, z, y, core, halves[s]] for s in range(2)])
    begin(0)
    locals_[0].wait()
    locals_[1].wait()
    table_ring.middle(0)
    table_ring.start(4)
    table_ring.start_direct(0)
    a_ring.middle()
    b_ring.middle()
    a_ring.start_direct()
    b_ring.start_direct()
    table_ring.middle(1)
    table_ring.start_direct(1)
    table_ring.start(5)
    table_ring.middle(2)
    table_ring.start_direct(2)
    table_ring.start(6)
    arrived(0)
    begin(1)
    for copy in locals_[3:]:
        copy.wait()
    table_ring.middle(3)
    table_ring.start_direct(3)
    table_ring.start(7)
    a_ring.finish([a_out.at[:, :, first[s]] for s in range(2)])
    c_ring.start()
    c_ring.start_direct()
    b_ring.finish([b_out.at[:, :, inner[s]] for s in range(2)])
    d_ring.start()
    d_ring.start_direct()
    update_tables(0)
    table_ring.middle(4)
    table_ring.start_direct(4)
    arrived(1)
    begin(2)
    c_ring.middle()
    d_ring.middle()
    table_ring.middle(5)
    table_ring.start_direct(5)
    c_ring.finish([c_out.at[:, first[s]] for s in range(2)])
    d_ring.finish([d_out.at[:, inner[s]] for s in range(2)])
    e_ring.start()
    e_ring.start_direct()
    update_tables(1)
    arrived(2)
    gather_copy(18, gathered.at[:, :, :, core], partner).start()
    table_ring.middle(6)
    table_ring.start_direct(6)
    e_ring.middle()
    update_tables(2)
    table_ring.middle(7)
    table_ring.start_direct(7)
    gather_copy(18, gathered.at[:, :, :, 1 - core], partner).wait_recv()
    update_small()
    finish_steps()
    update_tables(3)
    update_tables(4)
    update_tables(5)
    update_tables(6)
    update_tables(7)
    for ring in (table_ring, a_ring, b_ring, c_ring, d_ring, e_ring, u_ring, v_ring):
        ring.drain()
    for number in range(3):
        for copy in stage(number, False):
            copy.wait_send()
    gather_copy(18, gathered.at[:, :, :, core], partner).wait_send()


def shaped(shape, dtype=F32):
    return jax.ShapeDtypeStruct(shape, dtype)


HBM = pl.BlockSpec(memory_space=pltpu.HBM)
VMEM = pl.BlockSpec(memory_space=pltpu.VMEM)
SMEM = pl.BlockSpec(memory_space=pltpu.SMEM)
DMA = pltpu.SemaphoreType.DMA


def params(mebibytes, **others):
    return pltpu.CompilerParams(vmem_limit_bytes=mebibytes << 20, **others)


def on_device(
    features, labels, cross_down, cross_up, cross_bias, head_weight, head_bias, table_place,
    bag_rows, small_rows, table_store, table_acc, small_store, small_acc, down_acc, up_acc,
):
    bags = jnp.transpose(bag_rows, (1, 2, 0))
    small_ids = jnp.transpose(small_rows, (1, 2, 0))
    send, small, rights, lows = pl.pallas_call(
        dense_kernel,
        out_shape=(
            shaped((HOSTS, PACK, EMB)), shaped((TR, PACK, EMB)),
            shaped((2 * SAMPLES, WIDTH), BF16), shaped((2 * SAMPLES, RANK), BF16),
        ),
        in_specs=[VMEM] * 3 + [SMEM] * 2 + [VMEM] * 2 + [HBM] * 3,
        out_specs=(VMEM,) * 4,
        scratch_shapes=[
            pltpu.VMEM((RANK, WIDTH), BF16), pltpu.VMEM((RANK, WIDTH), BF16),
            pltpu.VMEM((SAMPLES, WIDTH), F32), DMA((3,)),
        ],
        compiler_params=params(60),
        name="dense_backward",
    )(
        labels.reshape(1, -1), cross_bias.reshape(-1, 128), head_weight.reshape(-1, 128), head_bias,
        table_place, bags, small_ids, features, cross_down, cross_up,
    )
    whole = (RANK, FULL)
    got, ids, dense = pl.pallas_call(
        exchange_kernel,
        out_shape=(
            shaped((HOSTS, PACK, EMB)), shaped((HOSTS * HOT, SAMPLES), jnp.int32), shaped(whole),
        ),
        in_specs=[HBM] * 4,
        out_specs=(HBM, VMEM, HBM),
        scratch_shapes=[
            pltpu.VMEM((2 * SAMPLES, WIDTH), BF16), pltpu.VMEM((2 * SAMPLES, RANK), BF16),
            pltpu.VMEM((LOCALS, PACK, EMB), F32), pltpu.VMEM((HOSTS, PACK, EMB), F32),
            pltpu.VMEM((RANK, 2 * SAMPLES), BF16), pltpu.VMEM((RANK, 2 * SAMPLES), BF16),
            pltpu.VMEM(whole, F32), pltpu.VMEM(whole, F32), pltpu.VMEM(whole, F32),
            pltpu.VMEM((TR, SAMPLES, 2 * EMB), BF16),
            pltpu.VMEM((len(TIES), 2, PACK, EMB), F32),
            DMA((2, HOSTS)), DMA((2, len(TIES))), DMA((2, 4)), DMA((2, 4)), DMA((4,)), DMA((3,)), DMA,
        ],
        compiler_params=params(60, collective_id=0, has_side_effects=True),
        name="exchange",
    )(send, rights, lows, small)
    tables = pl.pallas_call(
        pooled_kernel,
        out_shape=shaped((LOCALS * SHARD, EMB)),
        in_specs=[SMEM, HBM],
        out_specs=HBM,
        scratch_shapes=[pltpu.VMEM((HOSTS, PACK, EMB), F32)]
        + [pltpu.VMEM((LOCALS * SHARD, EMB), F32)] * HOT
        + [DMA((LOCALS * SHARD // 256,)), DMA],
        compiler_params=params(60),
        name="pooled_rows",
    )(ids.reshape(-1), got)

    def ring_buffers(first_shape, second_shape):
        near = [pltpu.VMEM(second_shape, F32), pltpu.VMEM(first_shape, F32)]
        return near + [pltpu.VMEM(first_shape, F32), pltpu.VMEM(second_shape, F32)] * 2

    rest = WIDTH - CUT
    half = SHARD // 2
    table_new, acc_new, small_new, small_acc_new, down_step, up_step = pl.pallas_call(
        reduce_kernel,
        out_shape=(
            shaped((SHARD, EMB)), shaped((SHARD // 128, 128)),
            shaped((TR * RS, EMB)), shaped((TR * RS // 128, 128)),
            shaped((4, WIDTH)), shaped((4, WIDTH)),
        ),
        in_specs=[HBM] * 4 + [VMEM] * 4,
        out_specs=(VMEM,) * 6,
        scratch_shapes=[
            pltpu.VMEM((SHARD, EMB), F32), pltpu.VMEM((TR * RS, EMB), F32),
            pltpu.VMEM((LOCALS, 4, 4, 2, 32, EMB), F32), pltpu.VMEM((SHARD, EMB), F32),
            pltpu.VMEM((half, EMB), F32), pltpu.VMEM((half, EMB), F32),
            pltpu.VMEM((4, 4, 32, FULL), F32),
        ]
        + ring_buffers((half, EMB), (half, EMB))
        + ring_buffers((4, 32, 896), (4, 32, 896))
        + ring_buffers((4, 32, 896), (4, 32, 768))
        + ring_buffers((32, 896), (32, 896))
        + ring_buffers((32, 896), (32, 768))
        + ring_buffers((8, CUT), (8, rest))
        + ring_buffers((2, 32, EMB), (2, 32, EMB))
        + ring_buffers((16, EMB), (16, EMB))
        + [
            pltpu.VMEM((4, 32, CUT), F32), pltpu.VMEM((4, 32, rest), F32),
            pltpu.VMEM((32, CUT), F32), pltpu.VMEM((32, rest), F32),
            pltpu.VMEM((4, 32, EMB), F32),
            DMA((2, 6 * CHUNKS)), DMA((7, 2, 6)), DMA((2, 19)), DMA((6,)),
        ],
        compiler_params=params(48, collective_id=1, has_side_effects=True),
        name="reduce_update",
    )(
        tables.reshape(LOCALS, SHARD, EMB), dense.reshape(4, 4, 32, FULL), table_store, small_store,
        table_acc.reshape(-1, 128), small_acc.reshape(-1, 128), down_acc, up_acc,
    )
    return (
        table_new, acc_new.reshape(-1), small_new, small_acc_new.reshape(-1), down_step, up_step,
    )


def solution(mesh):
    both = ("hst", "local")
    rows = P(both, None)
    return jax.shard_map(
        on_device,
        mesh=mesh,
        in_specs=(
            rows, P(both), P(), P(), P(), P(), P(), P(), P(both, None, None), P(both, None, None),
            rows, P(both), P(), P(), rows, rows,
        ),
        out_specs=(rows, P(both), P(), P(), rows, rows),
        check_vma=False,
    )
```

```python
import functools

import jax
import jax.numpy as jnp
from jax import lax
from jax.experimental import pallas as pl
from jax.experimental.pallas import tpu as pltpu
from jax.sharding import PartitionSpec as P

TS = 22
TR = 4
RS = 1024
HOT = 4
SHARD = 4096
EMB = 128
RANK = 512
WIDTH = 3456
HOSTS = 32
LOCALS = 4
SAMPLES = 128
PACK = SAMPLES + 8
FULL = WIDTH + EMB
CUT = 1792
TIES = ((2, 0), (2, 1), (2, 3), (0, 2), (1, 2), (3, 2), (2, 2))
STRAIGHT = ((0, 1), (0, 3), (1, 0), (3, 0), (1, 1), (1, 3), (3, 1), (3, 3))
LEARN_RATE = 0.05
MESH = pl.DeviceIdType.MESH
F32 = jnp.float32
BF16 = jnp.bfloat16


def product(left, right, left_dim=1, right_dim=0):
    return lax.dot_general(
        left, right, (((left_dim,), (right_dim,)), ((), ())), preferred_element_type=F32
    )


def diagonal():
    return lax.broadcasted_iota(jnp.int32, (128, 128), 0) == lax.broadcasted_iota(
        jnp.int32, (128, 128), 1
    )


def dense_backward(
    labels, bias, head, head_bias, place, bags, small_ids, features_hbm, down_hbm, up_hbm,
    pieces, send, small, rights, lows, down, up, cross, sems,
):
    features = rights.at[0:SAMPLES]
    features_copy = pltpu.make_async_copy(features_hbm, features, sems.at[2])
    down_copy = pltpu.make_async_copy(down_hbm, down, sems.at[0])
    up_copy = pltpu.make_async_copy(up_hbm, up, sems.at[1])
    features_copy.start()
    down_copy.start()
    up_copy.start()

    @pl.loop(0, TS)
    def _(table):
        pieces[table, pl.ds(SAMPLES, 8), :] = jnp.concatenate(
            [bags[table].astype(F32), jnp.zeros((HOT, EMB), F32)], axis=0
        )

    for table in range(TR):
        small[table, SAMPLES:, :] = jnp.zeros((PACK - SAMPLES, EMB), F32)
        small[table, SAMPLES : SAMPLES + HOT, :] = small_ids[table].astype(F32)

    parts = [(start, min(256, WIDTH - start)) for start in range(0, WIDTH, 256)]

    def tiles(ref, start, width):
        rows = [ref[t : t + 1, :] for t in range(start // 128, (start + width) // 128)]
        return jnp.concatenate(rows, axis=1)

    features_copy.wait()
    down_copy.wait()
    low_proj = product(features[...], down[...], 1, 1).astype(BF16)
    lows[SAMPLES:, :] = low_proj
    up_copy.wait()
    terms = jnp.zeros((SAMPLES, 128), F32)
    for start, width in parts:
        at = pl.ds(start, width)
        out = product(low_proj, up[:, at]) + tiles(bias, start, width)
        cross[:, at] = out
        wide = features[:, at].astype(F32)
        weighted = (wide * out + wide) * tiles(head, start, width)
        for tile in range(width // 128):
            terms = terms + weighted[:, tile * 128 : (tile + 1) * 128]
    logit = jnp.sum(terms, axis=1, keepdims=True) + head_bias[0]
    label = jnp.sum(
        jnp.where(diagonal(), labels[...].astype(F32), 0.0), axis=1, keepdims=True
    )
    logit_grad = jax.nn.sigmoid(logit) - label
    for start, width in parts:
        at = pl.ds(start, width)
        layer_grad = logit_grad * tiles(head, start, width)
        rights[SAMPLES:, at] = (layer_grad * features[:, at].astype(F32)).astype(BF16)
    low_grad = product(rights[SAMPLES:, :], up[...], 1, 1).astype(BF16)
    lows[0:SAMPLES, :] = low_grad
    for start, width in parts:
        at = pl.ds(start, width)
        layer_grad = logit_grad * tiles(head, start, width)
        grad = layer_grad * (cross[:, at] + 1.0) + product(low_grad, down[:, at])
        for tile in range(width // 128):
            piece = grad[:, tile * 128 : (tile + 1) * 128]
            table = start // 128 + tile - 1
            if 0 <= table < TS:
                pieces[table, 0:SAMPLES, :] = piece
            elif table >= TS:
                small[table - TS, 0:SAMPLES, :] = piece

    @pl.loop(0, HOSTS)
    def _(slot):
        held = jnp.int32(-1)
        for table in range(TS):
            held = jnp.where(place[table] == slot, table, held)
        keep = jnp.where(held >= 0, 1, 0)
        send[slot] = jnp.where(keep == 1, pieces[jnp.maximum(held, 0)], 0.0)


def exchange_kernel(
    labels, bias, head, head_bias, place, bags, small_ids, features_hbm, down_hbm, up_hbm,
    got_hbm, ids, dense,
    pieces, send, small_mine, down, up, cross, dense_sems,
    rights, lows, small, got, left_own, left_other, own, other, arrived, split, relayed,
    sems, relay_sems, core_sems, small_sems, out_sems, in_sem, own_sem,
):
    host = lax.axis_index("hst")
    core = lax.rem(host, 2)
    z, y = host // 8, (host // 2) % 4
    x = lax.axis_index("local")
    partner = host + 1 - 2 * core
    barrier = pltpu.get_barrier_semaphore()

    @pl.loop(1, HOSTS)
    def _(off):
        pl.semaphore_signal(
            barrier, inc=1, device_id={"hst": lax.rem(host + off, HOSTS)}, device_id_type=MESH
        )

    def chip(dz, dy):
        return (lax.rem(z + dz + 4, 4) * 4 + lax.rem(y + dy + 4, 4)) * 2

    def bag_copy(src, to, slot, off, cores):
        at = (off[0] * 4 + off[1]) * 2
        return pltpu.make_async_remote_copy(
            src_ref=src,
            dst_ref=got.at[slot],
            send_sem=sems.at[0, at + cores[1]],
            recv_sem=sems.at[1, at + cores[0]],
            device_id={"hst": to},
            device_id_type=MESH,
        )

    def straight(off, target):
        to = chip(*off) + target
        return bag_copy(send.at[to], to, host, off, (core, target))

    turn = 1 - 2 * core

    def halfway(index):
        dz, dy = TIES[index]
        to = chip(turn if dz == 2 else 0, turn if dy == 2 else 0) + core
        return pltpu.make_async_remote_copy(
            src_ref=send.at[pl.ds(chip(dz, dy), 2)],
            dst_ref=relayed.at[index],
            send_sem=relay_sems.at[0, index],
            recv_sem=relay_sems.at[1, index],
            device_id={"hst": to},
            device_id_type=MESH,
        )

    def onward(index, target):
        dz, dy = TIES[index]
        to = chip(turn if dz == 2 else dz, turn if dy == 2 else dy) + target
        source = chip(-turn if dz == 2 else 0, -turn if dy == 2 else 0) + core
        return bag_copy(relayed.at[index, target], to, source, TIES[index], (core, target))

    def arrival(off, source_core):
        source = chip(-off[0], -off[1]) + source_core
        return bag_copy(send.at[source], source, source, off, (source_core, source_core))

    def neighbour():
        return pltpu.make_async_remote_copy(
            src_ref=send.at[partner],
            dst_ref=got.at[host],
            send_sem=sems.at[0, 0],
            recv_sem=sems.at[1, 0],
            device_id={"hst": partner},
            device_id_type=MESH,
        )

    def from_neighbour():
        return pltpu.make_async_remote_copy(
            src_ref=send.at[partner],
            dst_ref=got.at[partner],
            send_sem=sems.at[0, 0],
            recv_sem=sems.at[1, 0],
            device_id={"hst": partner},
            device_id_type=MESH,
        )

    for step in (1, 2, 3):
        pl.semaphore_signal(
            barrier, inc=1, device_id={"local": lax.rem(x + step, 4)}, device_id_type=MESH
        )

    def small_copy(step, slot):
        to = lax.rem(x + step, 4)
        return pltpu.make_async_remote_copy(
            src_ref=small_mine.at[to],
            dst_ref=small.at[slot],
            send_sem=small_sems.at[0, step],
            recv_sem=small_sems.at[1, step],
            device_id={"local": to},
            device_id_type=MESH,
        )

    dense_backward(
        labels, bias, head, head_bias, place, bags, small_ids, features_hbm, down_hbm, up_hbm,
        pieces, send, small_mine, rights, lows, down, up, cross, dense_sems,
    )
    small_own = pltpu.make_async_copy(small_mine.at[x], small.at[x], in_sem)
    small_own.start()
    pl.semaphore_wait(barrier, HOSTS + 2)
    for step in (1, 2, 3):
        small_copy(step, x).start()
    for index in range(len(TIES)):
        halfway(index).start()
    for off in STRAIGHT:
        for target in range(2):
            straight(off, target).start()
    neighbour().start()
    mine = pltpu.make_async_copy(send.at[host], got.at[host], own_sem)
    mine.start()

    def spread(target, left):
        row = lax.broadcasted_iota(jnp.int32, (RANK, RANK), 0)
        rank = lax.broadcasted_iota(jnp.int32, (RANK, RANK), 1)
        place = row & 7
        base = ((row >> 5) * 2 + target) * 16 + ((row >> 3) & 3) * 4
        for part in range(2):
            want = jnp.where((place >> 2) == part, base + place - 4 * part, -1)
            chosen = jnp.where(want == rank, 1.0, 0.0).astype(BF16)
            left[:, part * SAMPLES : (part + 1) * SAMPLES] = product(
                chosen, lows[part * SAMPLES : (part + 1) * SAMPLES, :], 1, 1
            ).astype(BF16)

    def grads(left, out, group):
        @pl.loop(0, WIDTH // 384)
        def _(part):
            at = pl.ds(pl.multiple_of(part * 384, 384), 384)
            out[group * 128 : (group + 1) * 128, at] = product(
                left[group * 128 : (group + 1) * 128, :], rights[:, at]
            )

    small_own.wait()
    for step in (1, 2, 3):
        small_copy(step, lax.rem(x - step + 4, 4)).wait_recv()

    @pl.loop(0, LOCALS)
    def _(source):
        value = small[source, pl.ds(0, SAMPLES), :]
        high = value.astype(BF16)
        split[source, :, 0:EMB] = high
        split[source, :, EMB:] = (value - high.astype(F32)).astype(BF16)

    def small_sums(target, out, group):
        spot = group * 128 + lax.broadcasted_iota(jnp.int32, (128, SAMPLES), 0)
        row = ((spot >> 5) * 64 + target * 32 + (spot & 31)).astype(F32)
        here = pl.ds(group * 128, 128)
        lanes = pl.ds(WIDTH, EMB)
        out[here, lanes] = jnp.zeros((128, EMB), F32)

        @pl.loop(0, LOCALS)
        def _(source):
            wanted = small[source, pl.ds(SAMPLES, 8), :]
            counts = jnp.zeros((128, SAMPLES), F32)
            for k in range(HOT):
                counts = counts + jnp.where(row == wanted[k : k + 1, :], 1.0, 0.0)
            both = product(counts.astype(BF16), split[source])
            out[here, lanes] = out[here, lanes] + (both[:, 0:EMB] + both[:, EMB:])

    def core_copy(group):
        rows = pl.ds(group * 128, 128)
        return pltpu.make_async_remote_copy(
            src_ref=other.at[rows],
            dst_ref=arrived.at[rows],
            send_sem=core_sems.at[0, group],
            recv_sem=core_sems.at[1, group],
            device_id={"hst": partner},
            device_id_type=MESH,
        )

    def out_copy(group):
        rows = pl.ds(group * 128, 128)
        return pltpu.make_async_copy(own.at[rows], dense.at[rows], out_sems.at[group])

    spread(1 - core, left_other)
    for group in range(4):
        grads(left_other, other, group)
        small_sums(1 - core, other, group)
        core_copy(group).start()
    for index in range(len(TIES)):
        halfway(index).wait_recv()
        for target in range(2):
            onward(index, target).start()
    spread(core, left_own)
    for group in range(4):
        grads(left_own, own, group)
        small_sums(core, own, group)
    for group in range(4):
        core_copy(group).wait_recv()

        @pl.loop(0, 4)
        def _(part):
            rows = pl.ds(pl.multiple_of(group * 128 + part * 32, 32), 32)
            own[rows, :] = own[rows, :] + arrived[rows, :]

        out_copy(group).start()

    mine.wait()
    from_neighbour().wait_recv()
    for off in STRAIGHT + TIES:
        for source_core in range(2):
            arrival(off, source_core).wait_recv()

    @pl.loop(0, HOSTS // 2)
    def _(pair):
        low = got[pair * 2, pl.ds(SAMPLES, 8), :]
        high = got[pair * 2 + 1, pl.ds(SAMPLES, 8), :]
        ids[pl.ds(pl.multiple_of(pair * 8, 8), 8), :] = jnp.concatenate(
            [low[0:HOT], high[0:HOT]], axis=0
        ).astype(jnp.int32)

    result = pltpu.make_async_copy(got, got_hbm, own_sem)
    result.start()
    neighbour().wait_send()
    for step in (1, 2, 3):
        small_copy(step, x).wait_send()
    for off in STRAIGHT:
        for target in range(2):
            straight(off, target).wait_send()
    for index in range(len(TIES)):
        halfway(index).wait_send()
        for target in range(2):
            onward(index, target).wait_send()
    for group in range(4):
        core_copy(group).wait_send()
        out_copy(group).wait()
    result.wait()


def pooled_kernel(ids, grads_hbm, out, grads, *scratch):
    sums, sem, in_sem = scratch[:HOT], scratch[HOT], scratch[HOT + 1]
    operand = pltpu.make_async_copy(grads_hbm, grads, in_sem)
    operand.start()
    row_total = out.shape[0]
    step = 256

    @pl.loop(0, row_total // step)
    def _(i):
        rows = pl.ds(pl.multiple_of(i * step, step), step)
        for total in sums:
            total[rows, :] = jnp.zeros((step, EMB), F32)

    operand.wait()

    @pl.loop(0, HOSTS)
    def _(source):
        @pl.loop(0, SAMPLES // 16)
        def _(group):
            for pair in range(8):
                sample = group * 16 + pair * 2
                first = grads[source, pl.ds(sample, 1), :]
                second = grads[source, pl.ds(sample + 1, 1), :]
                at = [
                    ids[(source * HOT + k % HOT) * SAMPLES + sample + k // HOT]
                    for k in range(2 * HOT)
                ]
                held = [sums[k % HOT][pl.ds(at[k], 1), :] for k in range(2 * HOT)]
                new = [held[k] + first for k in range(HOT)]
                for k in range(HOT):
                    new.append(jnp.where(at[k] == at[HOT + k], new[k], held[HOT + k]) + second)
                for k in range(2 * HOT):
                    sums[k % HOT][pl.ds(at[k], 1), :] = new[k]

    @pl.loop(0, row_total // step)
    def _(i):
        rows = pl.ds(pl.multiple_of(i * step, step), step)
        sums[0][rows, :] = (sums[0][rows, :] + sums[1][rows, :]) + (
            sums[2][rows, :] + sums[3][rows, :]
        )
        pltpu.make_async_copy(sums[0].at[rows], out.at[rows], sem.at[i]).start()

    @pl.loop(0, row_total // step)
    def _(i):
        rows = pl.ds(pl.multiple_of(i * step, step), step)
        pltpu.make_async_copy(sums[0].at[rows], out.at[rows], sem.at[i]).wait()


class Ring:
    def __init__(self, place, right, left, sent, held, near, passed, sums, sems, chunks=1):
        self.place, self.right, self.left = place, right, left
        self.sent, self.held, self.near, self.passed = sent, held, near, passed
        self.sums, self.sems, self.chunks = sums, sems, chunks

    def piece(self, ref, chunk):
        if self.chunks == 1:
            return ref
        rows = ref.shape[0] // self.chunks
        return ref.at[pl.ds(chunk * rows, rows)]

    def copy(self, src, dst, kind, side, chunk):
        index = (kind * 2 + side) * self.chunks + chunk
        return pltpu.make_async_remote_copy(
            src_ref=self.piece(src, chunk), dst_ref=self.piece(dst, chunk),
            send_sem=self.sems.at[0, index], recv_sem=self.sems.at[1, index],
            device_id=self.left if side else self.right, device_id_type=MESH,
        )

    def next(self, side):
        return lax.rem(self.place + (3 if side else 1), 4)

    def far(self, side, chunk=0):
        src = self.sent(lax.rem(self.place + 2, 4), side)
        return self.copy(src, self.passed[side], 0, side, chunk)

    def direct(self, side, chunk=0):
        return self.copy(self.sent(self.next(side), 1 - side), self.near[side], 1, side, chunk)

    def relay(self, side, chunk=0):
        return self.copy(self.passed[side], self.sums[side], 2, side, chunk)

    def start(self, chunk=0):
        for side in range(2):
            self.far(side, chunk).start()

    def start_direct(self, chunk=0):
        for side in range(2):
            self.direct(side, chunk).start()

    def middle(self, chunk=0):
        for side in range(2):
            self.far(side, chunk).wait_recv()
            add_into(
                self.piece(self.passed[side], chunk),
                self.piece(self.held(self.next(side), side), chunk),
            )
            self.relay(side, chunk).start()

    def arrive(self, chunk=0):
        for side in range(2):
            self.relay(side, chunk).wait_recv()
            self.direct(side, chunk).wait_recv()

    def finish(self, outs):
        self.arrive()
        add_three(outs[0], self.held(self.place, 0), self.sums[0], self.near[1])
        add_three(outs[1], self.held(self.place, 1), self.near[0], self.sums[1])

    def drain(self):
        for chunk in range(self.chunks):
            for side in range(2):
                self.far(side, chunk).wait_send()
                self.direct(side, chunk).wait_send()
                self.relay(side, chunk).wait_send()


def blocks_of(shape):
    if len(shape) == 3:
        return shape[0], lambda ref, i: ref.at[i]
    rows = min(shape[0], 32 if shape[1] > 256 else 128)
    return shape[0] // rows, lambda ref, i: ref.at[pl.ds(pl.multiple_of(i * rows, rows), rows)]


def add_into(total, term):
    count, at = blocks_of(total.shape)

    @pl.loop(0, count)
    def _(i):
        at(total, i)[...] = at(total, i)[...] + at(term, i)[...]


def add_three(out, first, second, third):
    count, at = blocks_of(out.shape)

    @pl.loop(0, count)
    def _(i):
        at(out, i)[...] = at(first, i)[...] + at(second, i)[...] + at(third, i)[...]


CHUNKS = 8


def reduce_kernel(
    tables, dense, store_hbm, small_hbm, acc, small_acc, down_acc, up_acc,
    table_new, acc_new, small_new, small_acc_new, down_step, up_step,
    store, small, gathered, mine, ahead, behind, grads,
    t_near0, t_near1, t_pass0, t_pass1, t_sum0, t_sum1,
    a_near0, a_near1, a_pass0, a_pass1, a_sum0, a_sum1,
    b_near0, b_near1, b_pass0, b_pass1, b_sum0, b_sum1,
    c_near0, c_near1, c_pass0, c_pass1, c_sum0, c_sum1,
    d_near0, d_near1, d_pass0, d_pass1, d_sum0, d_sum1,
    e_near0, e_near1, e_pass0, e_pass1, e_sum0, e_sum1,
    u_near0, u_near1, u_pass0, u_pass1, u_sum0, u_sum1,
    v_near0, v_near1, v_pass0, v_pass1, v_sum0, v_sum1,
    a_out, b_out, c_out, d_out, u_out,
    t_sems, r_sems, g_sems, local_sems,
):
    host = lax.axis_index("hst")
    x = lax.axis_index("local")
    z, y, core = host // 8, (host // 2) % 4, host % 2

    def on_z(step):
        return {"hst": (lax.rem(z + step, 4) * 4 + y) * 2 + core}

    def on_y(step):
        return {"hst": (z * 4 + lax.rem(y + step, 4)) * 2 + core}

    def on_x(step):
        return {"local": lax.rem(x + step, 4)}

    barrier = pltpu.get_barrier_semaphore()
    for neighbours in (on_x, on_y, on_z):
        for step in (1, 2, 3):
            pl.semaphore_signal(
                barrier, inc=1, device_id=neighbours(step), device_id_type=MESH
            )
    partner = {"hst": host + 1 - 2 * core}
    pl.semaphore_signal(barrier, inc=1, device_id=partner, device_id_type=MESH)
    half = SHARD // 2
    right, left = lax.rem(x + 1, 4), lax.rem(x + 3, 4)
    locals_ = [
        pltpu.make_async_copy(tables.at[right, pl.ds(0, half)], ahead, local_sems.at[0]),
        pltpu.make_async_copy(tables.at[left, pl.ds(half, half)], behind, local_sems.at[1]),
        pltpu.make_async_copy(dense, grads, local_sems.at[2]),
        pltpu.make_async_copy(tables.at[x], mine, local_sems.at[3]),
        pltpu.make_async_copy(store_hbm, store, local_sems.at[4]),
        pltpu.make_async_copy(small_hbm, small, local_sems.at[5]),
    ]
    for copy in locals_:
        copy.start()
    pl.semaphore_wait(barrier, 10)

    first = {0: pl.ds(0, 896), 1: pl.ds(896, 896)}
    second = {0: pl.ds(CUT, 896), 1: pl.ds(CUT + 896, 768)}
    inner = {0: pl.ds(0, 896), 1: pl.ds(896, 768)}
    third = pl.ds(WIDTH, EMB)
    pairs = (pl.ds(0, 2), pl.ds(2, 2))
    halves = (pl.ds(0, 16), pl.ds(16, 16))
    table_ring = Ring(
        x, on_x(1), on_x(3),
        lambda t, s: tables.at[t, pl.ds(s * half, half)],
        lambda t, s: behind if s else ahead,
        (t_near0, t_near1), (t_pass0, t_pass1), (t_sum0, t_sum1), t_sems, CHUNKS,
    )
    a_ring = Ring(
        z, on_z(1), on_z(3),
        lambda t, s: dense.at[t, :, :, first[s]],
        lambda t, s: grads.at[t, :, :, first[s]],
        (a_near0, a_near1), (a_pass0, a_pass1), (a_sum0, a_sum1), r_sems.at[0],
    )
    b_ring = Ring(
        y, on_y(1), on_y(3),
        lambda t, s: dense.at[:, t, :, second[s]],
        lambda t, s: grads.at[:, t, :, second[s]],
        (b_near0, b_near1), (b_pass0, b_pass1), (b_sum0, b_sum1), r_sems.at[1],
    )
    c_at = lambda t, s: a_out.at[t, :, first[s]]
    c_ring = Ring(
        y, on_y(1), on_y(3), c_at, c_at, (c_near0, c_near1), (c_pass0, c_pass1), (c_sum0, c_sum1), r_sems.at[2]
    )
    d_at = lambda t, s: b_out.at[t, :, inner[s]]
    d_ring = Ring(
        z, on_z(1), on_z(3), d_at, d_at, (d_near0, d_near1), (d_pass0, d_pass1), (d_sum0, d_sum1), r_sems.at[3]
    )
    u_ring = Ring(
        z, on_z(1), on_z(3),
        lambda t, s: dense.at[t, pairs[s], :, third],
        lambda t, s: grads.at[t, pairs[s], :, third],
        (u_near0, u_near1), (u_pass0, u_pass1), (u_sum0, u_sum1), r_sems.at[5],
    )
    v_at = lambda t, s: u_out.at[t, halves[s]]
    v_ring = Ring(
        y, on_y(1), on_y(3), v_at, v_at,
        (v_near0, v_near1), (v_pass0, v_pass1), (v_sum0, v_sum1), r_sems.at[6],
    )
    e_at = lambda t, s: (d_out if s else c_out).at[pl.ds(pl.multiple_of(t * 8, 8), 8)]
    e_ring = Ring(
        x, on_x(1), on_x(3), e_at, e_at, (e_near0, e_near1), (e_pass0, e_pass1), (e_sum0, e_sum1), r_sems.at[4]
    )

    eye = diagonal()

    def update(block, grad, before, acc_before, after, acc_after):
        rows = pl.ds(pl.multiple_of(block * 128, 128), 128)
        at = pl.ds(block, 1)
        acc_here = jnp.sum(jnp.where(eye, acc_before[at, :], 0.0), axis=1, keepdims=True)
        total = acc_here + jnp.sum(grad * grad, axis=1, keepdims=True) * (1.0 / EMB)
        after[rows, :] = before[rows, :] - grad * (LEARN_RATE * lax.rsqrt(total))
        acc_after[at, :] = jnp.sum(jnp.where(eye, total, 0.0), axis=0, keepdims=True)

    def finish_dense(side, start, stop):
        near = (e_near1, e_near0)[side]
        at = pl.ds(start, stop - start)
        return e_ring.held(x, side)[:, at] + e_ring.sums[side][:, at] + near[:, at]

    def gather_copy(index, view, to):
        return pltpu.make_async_remote_copy(
            src_ref=view, dst_ref=view, send_sem=g_sems.at[0, index],
            recv_sem=g_sems.at[1, index], device_id=to, device_id_type=MESH,
        )

    def stage(number, back):
        copies = []
        for step in (1, 2, 3):
            there = lax.rem(4 - step, 4) if back else 0
            at_z, at_y, at_x = (lax.rem(place + there, 4) for place in (z, y, x))
            if number == 0:
                views = [(gathered.at[at_x, z, y, core], on_x)]
            elif number == 1:
                views = [
                    (gathered.at[:, z, at_y, core, halves[0]], on_y),
                    (gathered.at[:, at_z, y, core, halves[1]], on_z),
                ]
            else:
                views = [
                    (gathered.at[:, at_z, :, core, halves[0]], on_z),
                    (gathered.at[:, :, at_y, core, halves[1]], on_y),
                ]
            for view, axis in views:
                copies.append(gather_copy(number * 6 + len(copies), view, axis(step)))
        return copies

    def begin(number):
        for copy in stage(number, False):
            copy.start()

    def arrived(number):
        for copy in stage(number, True):
            copy.wait_recv()

    rows_chunk = half // CHUNKS

    def update_tables(chunk):
        table_ring.arrive(chunk)
        for side in range(2):
            near = (t_near1, t_near0)[side]

            @pl.loop(0, rows_chunk // 128)
            def _(part):
                inside = pl.ds(pl.multiple_of(chunk * rows_chunk + part * 128, 128), 128)
                block = side * (half // 128) + chunk * (rows_chunk // 128) + part
                rows = pl.ds(pl.multiple_of(block * 128, 128), 128)
                grad = mine[rows, :] + table_ring.sums[side][inside, :] + near[inside, :]
                update(block, grad, store, acc, table_new, acc_new)

    def update_small():
        @pl.loop(0, TR * RS // 128)
        def _(block):
            chip = (block % 8) * 2
            pieces = gathered.at[block // 8, chip // 4]
            grad = jnp.concatenate(
                [pieces[chip % 4 + part // 2, part % 2] for part in range(4)], axis=0
            )
            update(block, grad, small, small_acc, small_new, small_acc_new)

    def finish_steps():
        e_ring.arrive()
        for side, stop in ((0, CUT), (1, WIDTH - CUT)):
            total = finish_dense(side, 0, stop)
            at = pl.ds(side * CUT, stop)
            for step, before, rows in ((down_step, down_acc, 0), (up_step, up_acc, 4)):
                grad = total[rows : rows + 4]
                step[:, at] = grad * lax.rsqrt(before[:, at] + grad * grad)

    u_ring.start()
    u_ring.start_direct()
    table_ring.start(0)
    table_ring.start(1)
    table_ring.start(2)
    table_ring.start(3)
    locals_[2].wait()
    u_ring.middle()
    u_ring.finish([u_out.at[pairs[s]] for s in range(2)])
    v_ring.start()
    v_ring.start_direct()
    a_ring.start()
    b_ring.start()
    v_ring.middle()
    v_ring.finish([gathered.at[x, z, y, core, halves[s]] for s in range(2)])
    begin(0)
    locals_[0].wait()
    locals_[1].wait()
    table_ring.middle(0)
    table_ring.start(4)
    table_ring.start_direct(0)
    a_ring.middle()
    b_ring.middle()
    a_ring.start_direct()
    b_ring.start_direct()
    table_ring.middle(1)
    table_ring.start_direct(1)
    table_ring.start(5)
    table_ring.middle(2)
    table_ring.start_direct(2)
    table_ring.start(6)
    arrived(0)
    begin(1)
    for copy in locals_[3:]:
        copy.wait()
    table_ring.middle(3)
    table_ring.start_direct(3)
    table_ring.start(7)
    a_ring.finish([a_out.at[:, :, first[s]] for s in range(2)])
    c_ring.start()
    c_ring.start_direct()
    b_ring.finish([b_out.at[:, :, inner[s]] for s in range(2)])
    d_ring.start()
    d_ring.start_direct()
    update_tables(0)
    table_ring.middle(4)
    table_ring.start_direct(4)
    arrived(1)
    begin(2)
    c_ring.middle()
    d_ring.middle()
    table_ring.middle(5)
    table_ring.start_direct(5)
    c_ring.finish([c_out.at[:, first[s]] for s in range(2)])
    d_ring.finish([d_out.at[:, inner[s]] for s in range(2)])
    e_ring.start()
    e_ring.start_direct()
    update_tables(1)
    arrived(2)
    gather_copy(18, gathered.at[:, :, :, core], partner).start()
    table_ring.middle(6)
    table_ring.start_direct(6)
    e_ring.middle()
    update_tables(2)
    table_ring.middle(7)
    table_ring.start_direct(7)
    gather_copy(18, gathered.at[:, :, :, 1 - core], partner).wait_recv()
    update_small()
    finish_steps()
    update_tables(3)
    update_tables(4)
    update_tables(5)
    update_tables(6)
    update_tables(7)
    for ring in (table_ring, a_ring, b_ring, c_ring, d_ring, e_ring, u_ring, v_ring):
        ring.drain()
    for number in range(3):
        for copy in stage(number, False):
            copy.wait_send()
    gather_copy(18, gathered.at[:, :, :, core], partner).wait_send()


def shaped(shape, dtype=F32):
    return jax.ShapeDtypeStruct(shape, dtype)


HBM = pl.BlockSpec(memory_space=pltpu.HBM)
VMEM = pl.BlockSpec(memory_space=pltpu.VMEM)
SMEM = pl.BlockSpec(memory_space=pltpu.SMEM)
DMA = pltpu.SemaphoreType.DMA


def params(mebibytes, **others):
    return pltpu.CompilerParams(vmem_limit_bytes=mebibytes << 20, **others)


def on_device(
    features, labels, cross_down, cross_up, cross_bias, head_weight, head_bias, table_place,
    bag_rows, small_rows, table_store, table_acc, small_store, small_acc, down_acc, up_acc,
):
    bags = jnp.transpose(bag_rows, (1, 2, 0))
    small_ids = jnp.transpose(small_rows, (1, 2, 0))
    whole = (RANK, FULL)
    got, ids, dense = pl.pallas_call(
        exchange_kernel,
        out_shape=(
            shaped((HOSTS, PACK, EMB)), shaped((HOSTS * HOT, SAMPLES), jnp.int32), shaped(whole),
        ),
        in_specs=[VMEM] * 3 + [SMEM] * 2 + [VMEM] * 2 + [HBM] * 3,
        out_specs=(HBM, VMEM, HBM),
        scratch_shapes=[
            pltpu.VMEM((TS, PACK, EMB), F32), pltpu.VMEM((HOSTS, PACK, EMB), F32),
            pltpu.VMEM((TR, PACK, EMB), F32),
            pltpu.VMEM((RANK, WIDTH), BF16), pltpu.VMEM((RANK, WIDTH), BF16),
            pltpu.VMEM((SAMPLES, WIDTH), F32), DMA((3,)),
            pltpu.VMEM((2 * SAMPLES, WIDTH), BF16), pltpu.VMEM((2 * SAMPLES, RANK), BF16),
            pltpu.VMEM((LOCALS, PACK, EMB), F32), pltpu.VMEM((HOSTS, PACK, EMB), F32),
            pltpu.VMEM((RANK, 2 * SAMPLES), BF16), pltpu.VMEM((RANK, 2 * SAMPLES), BF16),
            pltpu.VMEM(whole, F32), pltpu.VMEM(whole, F32), pltpu.VMEM(whole, F32),
            pltpu.VMEM((TR, SAMPLES, 2 * EMB), BF16),
            pltpu.VMEM((len(TIES), 2, PACK, EMB), F32),
            DMA((2, HOSTS)), DMA((2, len(TIES))), DMA((2, 4)), DMA((2, 4)), DMA((4,)), DMA, DMA,
        ],
        compiler_params=params(60, collective_id=0, has_side_effects=True),
        name="dense_exchange",
    )(
        labels.reshape(1, -1), cross_bias.reshape(-1, 128), head_weight.reshape(-1, 128), head_bias,
        table_place, bags, small_ids, features, cross_down, cross_up,
    )
    tables = pl.pallas_call(
        pooled_kernel,
        out_shape=shaped((LOCALS * SHARD, EMB)),
        in_specs=[SMEM, HBM],
        out_specs=HBM,
        scratch_shapes=[pltpu.VMEM((HOSTS, PACK, EMB), F32)]
        + [pltpu.VMEM((LOCALS * SHARD, EMB), F32)] * HOT
        + [DMA((LOCALS * SHARD // 256,)), DMA],
        compiler_params=params(60),
        name="pooled_rows",
    )(ids.reshape(-1), got)

    def ring_buffers(first_shape, second_shape):
        near = [pltpu.VMEM(second_shape, F32), pltpu.VMEM(first_shape, F32)]
        return near + [pltpu.VMEM(first_shape, F32), pltpu.VMEM(second_shape, F32)] * 2

    rest = WIDTH - CUT
    half = SHARD // 2
    table_new, acc_new, small_new, small_acc_new, down_step, up_step = pl.pallas_call(
        reduce_kernel,
        out_shape=(
            shaped((SHARD, EMB)), shaped((SHARD // 128, 128)),
            shaped((TR * RS, EMB)), shaped((TR * RS // 128, 128)),
            shaped((4, WIDTH)), shaped((4, WIDTH)),
        ),
        in_specs=[HBM] * 4 + [VMEM] * 4,
        out_specs=(VMEM,) * 6,
        scratch_shapes=[
            pltpu.VMEM((SHARD, EMB), F32), pltpu.VMEM((TR * RS, EMB), F32),
            pltpu.VMEM((LOCALS, 4, 4, 2, 32, EMB), F32), pltpu.VMEM((SHARD, EMB), F32),
            pltpu.VMEM((half, EMB), F32), pltpu.VMEM((half, EMB), F32),
            pltpu.VMEM((4, 4, 32, FULL), F32),
        ]
        + ring_buffers((half, EMB), (half, EMB))
        + ring_buffers((4, 32, 896), (4, 32, 896))
        + ring_buffers((4, 32, 896), (4, 32, 768))
        + ring_buffers((32, 896), (32, 896))
        + ring_buffers((32, 896), (32, 768))
        + ring_buffers((8, CUT), (8, rest))
        + ring_buffers((2, 32, EMB), (2, 32, EMB))
        + ring_buffers((16, EMB), (16, EMB))
        + [
            pltpu.VMEM((4, 32, CUT), F32), pltpu.VMEM((4, 32, rest), F32),
            pltpu.VMEM((32, CUT), F32), pltpu.VMEM((32, rest), F32),
            pltpu.VMEM((4, 32, EMB), F32),
            DMA((2, 6 * CHUNKS)), DMA((7, 2, 6)), DMA((2, 19)), DMA((6,)),
        ],
        compiler_params=params(48, collective_id=1, has_side_effects=True),
        name="reduce_update",
    )(
        tables.reshape(LOCALS, SHARD, EMB), dense.reshape(4, 4, 32, FULL), table_store, small_store,
        table_acc.reshape(-1, 128), small_acc.reshape(-1, 128), down_acc, up_acc,
    )
    return (
        table_new, acc_new.reshape(-1), small_new, small_acc_new.reshape(-1), down_step, up_step,
    )


def solution(mesh):
    both = ("hst", "local")
    rows = P(both, None)
    return jax.shard_map(
        on_device,
        mesh=mesh,
        in_specs=(
            rows, P(both), P(), P(), P(), P(), P(), P(), P(both, None, None), P(both, None, None),
            rows, P(both), P(), P(), rows, rows,
        ),
        out_specs=(rows, P(both), P(), P(), rows, rows),
        check_vma=False,
    )
```

```python
import functools

import jax
import jax.numpy as jnp
from jax import lax
from jax.experimental import pallas as pl
from jax.experimental.pallas import tpu as pltpu
from jax.sharding import PartitionSpec as P

TS = 22
TR = 4
RS = 1024
HOT = 4
SHARD = 4096
EMB = 128
RANK = 512
WIDTH = 3456
HOSTS = 32
LOCALS = 4
SAMPLES = 128
PACK = SAMPLES + 8
FULL = WIDTH + EMB
CUT = 1792
TIES = ((2, 0), (2, 1), (2, 3), (0, 2), (1, 2), (3, 2), (2, 2))
STRAIGHT = ((0, 1), (0, 3), (1, 0), (3, 0), (1, 1), (1, 3), (3, 1), (3, 3))
LEARN_RATE = 0.05
MESH = pl.DeviceIdType.MESH
F32 = jnp.float32
BF16 = jnp.bfloat16


def product(left, right, left_dim=1, right_dim=0):
    return lax.dot_general(
        left, right, (((left_dim,), (right_dim,)), ((), ())), preferred_element_type=F32
    )


def diagonal():
    return lax.broadcasted_iota(jnp.int32, (128, 128), 0) == lax.broadcasted_iota(
        jnp.int32, (128, 128), 1
    )


def dense_backward(
    labels, bias, head, head_bias, place, bags, small_ids, features_hbm, down_hbm, up_hbm,
    pieces, send, small, rights, lows, down, up, cross, sems,
):
    features = rights.at[0:SAMPLES]
    features_copy = pltpu.make_async_copy(features_hbm, features, sems.at[2])
    down_copy = pltpu.make_async_copy(down_hbm, down, sems.at[0])
    up_copy = pltpu.make_async_copy(up_hbm, up, sems.at[1])
    features_copy.start()
    down_copy.start()
    up_copy.start()

    @pl.loop(0, TS)
    def _(table):
        pieces[table, pl.ds(SAMPLES, 8), :] = jnp.concatenate(
            [bags[table].astype(F32), jnp.zeros((HOT, EMB), F32)], axis=0
        )

    for table in range(TR):
        small[table, SAMPLES:, :] = jnp.zeros((PACK - SAMPLES, EMB), F32)
        small[table, SAMPLES : SAMPLES + HOT, :] = small_ids[table].astype(F32)

    parts = [(start, min(256, WIDTH - start)) for start in range(0, WIDTH, 256)]

    def tiles(ref, start, width):
        rows = [ref[t : t + 1, :] for t in range(start // 128, (start + width) // 128)]
        return jnp.concatenate(rows, axis=1)

    features_copy.wait()
    down_copy.wait()
    low_proj = product(features[...], down[...], 1, 1).astype(BF16)
    lows[SAMPLES:, :] = low_proj
    up_copy.wait()
    terms = jnp.zeros((SAMPLES, 128), F32)
    for start, width in parts:
        at = pl.ds(start, width)
        out = product(low_proj, up[:, at]) + tiles(bias, start, width)
        cross[:, at] = out
        wide = features[:, at].astype(F32)
        weighted = (wide * out + wide) * tiles(head, start, width)
        for tile in range(width // 128):
            terms = terms + weighted[:, tile * 128 : (tile + 1) * 128]
    logit = jnp.sum(terms, axis=1, keepdims=True) + head_bias[0]
    label = jnp.sum(
        jnp.where(diagonal(), labels[...].astype(F32), 0.0), axis=1, keepdims=True
    )
    logit_grad = jax.nn.sigmoid(logit) - label
    for start, width in parts:
        at = pl.ds(start, width)
        layer_grad = logit_grad * tiles(head, start, width)
        rights[SAMPLES:, at] = (layer_grad * features[:, at].astype(F32)).astype(BF16)
    low_grad = product(rights[SAMPLES:, :], up[...], 1, 1).astype(BF16)
    lows[0:SAMPLES, :] = low_grad
    for start, width in parts:
        at = pl.ds(start, width)
        layer_grad = logit_grad * tiles(head, start, width)
        grad = layer_grad * (cross[:, at] + 1.0) + product(low_grad, down[:, at])
        for tile in range(width // 128):
            piece = grad[:, tile * 128 : (tile + 1) * 128]
            table = start // 128 + tile - 1
            if 0 <= table < TS:
                pieces[table, 0:SAMPLES, :] = piece
            elif table >= TS:
                small[table - TS, 0:SAMPLES, :] = piece

    @pl.loop(0, HOSTS)
    def _(slot):
        held = jnp.int32(-1)
        for table in range(TS):
            held = jnp.where(place[table] == slot, table, held)
        keep = jnp.where(held >= 0, 1, 0)
        send[slot] = jnp.where(keep == 1, pieces[jnp.maximum(held, 0)], 0.0)


def exchange_kernel(
    labels, bias, head, head_bias, place, bags, small_ids, features_hbm, down_hbm, up_hbm,
    got_hbm, ids, dense,
    pieces, send, small_mine, down, up, cross, dense_sems,
    rights, lows, small, got, left_own, left_other, own, other, arrived, split, relayed,
    sems, relay_sems, core_sems, small_sems, out_sems, in_sem, own_sem,
):
    host = lax.axis_index("hst")
    core = lax.rem(host, 2)
    z, y = host // 8, (host // 2) % 4
    x = lax.axis_index("local")
    partner = host + 1 - 2 * core
    barrier = pltpu.get_barrier_semaphore()

    @pl.loop(1, HOSTS)
    def _(off):
        pl.semaphore_signal(
            barrier, inc=1, device_id={"hst": lax.rem(host + off, HOSTS)}, device_id_type=MESH
        )

    def chip(dz, dy):
        return (lax.rem(z + dz + 4, 4) * 4 + lax.rem(y + dy + 4, 4)) * 2

    def bag_copy(src, to, slot, off, cores):
        at = (off[0] * 4 + off[1]) * 2
        return pltpu.make_async_remote_copy(
            src_ref=src,
            dst_ref=got.at[slot],
            send_sem=sems.at[0, at + cores[1]],
            recv_sem=sems.at[1, at + cores[0]],
            device_id={"hst": to},
            device_id_type=MESH,
        )

    def straight(off, target):
        to = chip(*off) + target
        return bag_copy(send.at[to], to, host, off, (core, target))

    turn = 1 - 2 * core

    def halfway(index):
        dz, dy = TIES[index]
        to = chip(turn if dz == 2 else 0, turn if dy == 2 else 0) + core
        return pltpu.make_async_remote_copy(
            src_ref=send.at[pl.ds(chip(dz, dy), 2)],
            dst_ref=relayed.at[index],
            send_sem=relay_sems.at[0, index],
            recv_sem=relay_sems.at[1, index],
            device_id={"hst": to},
            device_id_type=MESH,
        )

    def onward(index, target):
        dz, dy = TIES[index]
        to = chip(turn if dz == 2 else dz, turn if dy == 2 else dy) + target
        source = chip(-turn if dz == 2 else 0, -turn if dy == 2 else 0) + core
        return bag_copy(relayed.at[index, target], to, source, TIES[index], (core, target))

    def arrival(off, source_core):
        source = chip(-off[0], -off[1]) + source_core
        return bag_copy(send.at[source], source, source, off, (source_core, source_core))

    def neighbour():
        return pltpu.make_async_remote_copy(
            src_ref=send.at[partner],
            dst_ref=got.at[host],
            send_sem=sems.at[0, 0],
            recv_sem=sems.at[1, 0],
            device_id={"hst": partner},
            device_id_type=MESH,
        )

    def from_neighbour():
        return pltpu.make_async_remote_copy(
            src_ref=send.at[partner],
            dst_ref=got.at[partner],
            send_sem=sems.at[0, 0],
            recv_sem=sems.at[1, 0],
            device_id={"hst": partner},
            device_id_type=MESH,
        )

    for step in (1, 2, 3):
        pl.semaphore_signal(
            barrier, inc=1, device_id={"local": lax.rem(x + step, 4)}, device_id_type=MESH
        )

    def small_copy(step, slot):
        to = lax.rem(x + step, 4)
        return pltpu.make_async_remote_copy(
            src_ref=small_mine.at[to],
            dst_ref=small.at[slot],
            send_sem=small_sems.at[0, step],
            recv_sem=small_sems.at[1, step],
            device_id={"local": to},
            device_id_type=MESH,
        )

    dense_backward(
        labels, bias, head, head_bias, place, bags, small_ids, features_hbm, down_hbm, up_hbm,
        pieces, send, small_mine, rights, lows, down, up, cross, dense_sems,
    )
    small_own = pltpu.make_async_copy(small_mine.at[x], small.at[x], in_sem)
    small_own.start()
    pl.semaphore_wait(barrier, HOSTS + 2)
    for step in (1, 2, 3):
        small_copy(step, x).start()
    for index in range(len(TIES)):
        halfway(index).start()
    for off in STRAIGHT:
        for target in range(2):
            straight(off, target).start()
    neighbour().start()
    mine = pltpu.make_async_copy(send.at[host], got.at[host], own_sem)
    mine.start()

    def spread(target, left):
        row = lax.broadcasted_iota(jnp.int32, (RANK, RANK), 0)
        rank = lax.broadcasted_iota(jnp.int32, (RANK, RANK), 1)
        place = row & 7
        base = ((row >> 5) * 2 + target) * 16 + ((row >> 3) & 3) * 4
        for part in range(2):
            want = jnp.where((place >> 2) == part, base + place - 4 * part, -1)
            chosen = jnp.where(want == rank, 1.0, 0.0).astype(BF16)
            left[:, part * SAMPLES : (part + 1) * SAMPLES] = product(
                chosen, lows[part * SAMPLES : (part + 1) * SAMPLES, :], 1, 1
            ).astype(BF16)

    def grads(left, out, group):
        @pl.loop(0, WIDTH // 384)
        def _(part):
            at = pl.ds(pl.multiple_of(part * 384, 384), 384)
            out[group * 128 : (group + 1) * 128, at] = product(
                left[group * 128 : (group + 1) * 128, :], rights[:, at]
            )

    small_own.wait()
    for step in (1, 2, 3):
        small_copy(step, lax.rem(x - step + 4, 4)).wait_recv()

    @pl.loop(0, LOCALS)
    def _(source):
        value = small[source, pl.ds(0, SAMPLES), :]
        high = value.astype(BF16)
        split[source, :, 0:EMB] = high
        split[source, :, EMB:] = (value - high.astype(F32)).astype(BF16)

    def small_sums(target, out, group):
        spot = group * 128 + lax.broadcasted_iota(jnp.int32, (128, SAMPLES), 0)
        row = ((spot >> 5) * 64 + target * 32 + (spot & 31)).astype(F32)
        here = pl.ds(group * 128, 128)
        lanes = pl.ds(WIDTH, EMB)
        out[here, lanes] = jnp.zeros((128, EMB), F32)

        @pl.loop(0, LOCALS)
        def _(source):
            wanted = small[source, pl.ds(SAMPLES, 8), :]
            counts = jnp.zeros((128, SAMPLES), F32)
            for k in range(HOT):
                counts = counts + jnp.where(row == wanted[k : k + 1, :], 1.0, 0.0)
            both = product(counts.astype(BF16), split[source])
            out[here, lanes] = out[here, lanes] + (both[:, 0:EMB] + both[:, EMB:])

    def core_copy(group):
        rows = pl.ds(group * 128, 128)
        return pltpu.make_async_remote_copy(
            src_ref=other.at[rows],
            dst_ref=arrived.at[rows],
            send_sem=core_sems.at[0, group],
            recv_sem=core_sems.at[1, group],
            device_id={"hst": partner},
            device_id_type=MESH,
        )

    def out_copy(group):
        rows = pl.ds(group * 128, 128)
        return pltpu.make_async_copy(own.at[rows], dense.at[rows], out_sems.at[group])

    spread(1 - core, left_other)
    for group in range(4):
        grads(left_other, other, group)
        small_sums(1 - core, other, group)
        core_copy(group).start()
    for index in range(len(TIES)):
        halfway(index).wait_recv()
        for target in range(2):
            onward(index, target).start()
    spread(core, left_own)
    for group in range(4):
        grads(left_own, own, group)
        small_sums(core, own, group)
    for group in range(4):
        core_copy(group).wait_recv()

        @pl.loop(0, 4)
        def _(part):
            rows = pl.ds(pl.multiple_of(group * 128 + part * 32, 32), 32)
            own[rows, :] = own[rows, :] + arrived[rows, :]

        out_copy(group).start()

    mine.wait()
    from_neighbour().wait_recv()
    for off in STRAIGHT + TIES:
        for source_core in range(2):
            arrival(off, source_core).wait_recv()

    @pl.loop(0, HOSTS // 2)
    def _(pair):
        low = got[pair * 2, pl.ds(SAMPLES, 8), :]
        high = got[pair * 2 + 1, pl.ds(SAMPLES, 8), :]
        ids[pl.ds(pl.multiple_of(pair * 8, 8), 8), :] = jnp.concatenate(
            [low[0:HOT], high[0:HOT]], axis=0
        ).astype(jnp.int32)

    result = pltpu.make_async_copy(got, got_hbm, own_sem)
    result.start()
    neighbour().wait_send()
    for step in (1, 2, 3):
        small_copy(step, x).wait_send()
    for off in STRAIGHT:
        for target in range(2):
            straight(off, target).wait_send()
    for index in range(len(TIES)):
        halfway(index).wait_send()
        for target in range(2):
            onward(index, target).wait_send()
    for group in range(4):
        core_copy(group).wait_send()
        out_copy(group).wait()
    result.wait()


def pooled_kernel(ids, grads_hbm, out, grads, *scratch):
    sums, sem, in_sem = scratch[:HOT], scratch[HOT], scratch[HOT + 1]
    operand = pltpu.make_async_copy(grads_hbm, grads, in_sem)
    operand.start()
    row_total = out.shape[0]
    step = 256

    @pl.loop(0, row_total // step)
    def _(i):
        rows = pl.ds(pl.multiple_of(i * step, step), step)
        for total in sums:
            total[rows, :] = jnp.zeros((step, EMB), F32)

    operand.wait()

    @pl.loop(0, HOSTS)
    def _(source):
        @pl.loop(0, SAMPLES // 16)
        def _(group):
            for pair in range(8):
                sample = group * 16 + pair * 2
                first = grads[source, pl.ds(sample, 1), :]
                second = grads[source, pl.ds(sample + 1, 1), :]
                at = [
                    ids[(source * HOT + k % HOT) * SAMPLES + sample + k // HOT]
                    for k in range(2 * HOT)
                ]
                held = [sums[k % HOT][pl.ds(at[k], 1), :] for k in range(2 * HOT)]
                new = [held[k] + first for k in range(HOT)]
                for k in range(HOT):
                    new.append(jnp.where(at[k] == at[HOT + k], new[k], held[HOT + k]) + second)
                for k in range(2 * HOT):
                    sums[k % HOT][pl.ds(at[k], 1), :] = new[k]

    @pl.loop(0, row_total // step)
    def _(i):
        rows = pl.ds(pl.multiple_of(i * step, step), step)
        sums[0][rows, :] = (sums[0][rows, :] + sums[1][rows, :]) + (
            sums[2][rows, :] + sums[3][rows, :]
        )
        pltpu.make_async_copy(sums[0].at[rows], out.at[rows], sem.at[i]).start()

    @pl.loop(0, row_total // step)
    def _(i):
        rows = pl.ds(pl.multiple_of(i * step, step), step)
        pltpu.make_async_copy(sums[0].at[rows], out.at[rows], sem.at[i]).wait()


class Ring:
    def __init__(self, place, right, left, sent, held, near, passed, sums, sems, chunks=1):
        self.place, self.right, self.left = place, right, left
        self.sent, self.held, self.near, self.passed = sent, held, near, passed
        self.sums, self.sems, self.chunks = sums, sems, chunks

    def piece(self, ref, chunk):
        if self.chunks == 1:
            return ref
        rows = ref.shape[0] // self.chunks
        return ref.at[pl.ds(chunk * rows, rows)]

    def copy(self, src, dst, kind, side, chunk):
        index = (kind * 2 + side) * self.chunks + chunk
        return pltpu.make_async_remote_copy(
            src_ref=self.piece(src, chunk), dst_ref=self.piece(dst, chunk),
            send_sem=self.sems.at[0, index], recv_sem=self.sems.at[1, index],
            device_id=self.left if side else self.right, device_id_type=MESH,
        )

    def next(self, side):
        return lax.rem(self.place + (3 if side else 1), 4)

    def far(self, side, chunk=0):
        src = self.sent(lax.rem(self.place + 2, 4), side)
        return self.copy(src, self.passed[side], 0, side, chunk)

    def direct(self, side, chunk=0):
        return self.copy(self.sent(self.next(side), 1 - side), self.near[side], 1, side, chunk)

    def relay(self, side, chunk=0):
        return self.copy(self.passed[side], self.sums[side], 2, side, chunk)

    def start(self, chunk=0):
        for side in range(2):
            self.far(side, chunk).start()

    def start_direct(self, chunk=0):
        for side in range(2):
            self.direct(side, chunk).start()

    def middle(self, chunk=0):
        for side in range(2):
            self.far(side, chunk).wait_recv()
            add_into(
                self.piece(self.passed[side], chunk),
                self.piece(self.held(self.next(side), side), chunk),
            )
            self.relay(side, chunk).start()

    def arrive(self, chunk=0):
        for side in range(2):
            self.relay(side, chunk).wait_recv()
            self.direct(side, chunk).wait_recv()

    def finish(self, outs):
        self.arrive()
        add_three(outs[0], self.held(self.place, 0), self.sums[0], self.near[1])
        add_three(outs[1], self.held(self.place, 1), self.near[0], self.sums[1])

    def drain(self):
        for chunk in range(self.chunks):
            for side in range(2):
                self.far(side, chunk).wait_send()
                self.direct(side, chunk).wait_send()
                self.relay(side, chunk).wait_send()


def blocks_of(shape):
    if len(shape) == 3:
        return shape[0], lambda ref, i: ref.at[i]
    rows = min(shape[0], 32 if shape[1] > 256 else 128)
    return shape[0] // rows, lambda ref, i: ref.at[pl.ds(pl.multiple_of(i * rows, rows), rows)]


def add_into(total, term):
    count, at = blocks_of(total.shape)

    @pl.loop(0, count)
    def _(i):
        at(total, i)[...] = at(total, i)[...] + at(term, i)[...]


def add_three(out, first, second, third):
    count, at = blocks_of(out.shape)

    @pl.loop(0, count)
    def _(i):
        at(out, i)[...] = at(first, i)[...] + at(second, i)[...] + at(third, i)[...]


CHUNKS = 8


def reduce_kernel(
    tables, dense, store_hbm, small_hbm, acc, small_acc, down_acc, up_acc,
    table_new, acc_new, small_new, small_acc_new, down_step, up_step,
    store, small, gathered, mine, ahead, behind, grads,
    t_near0, t_near1, t_pass0, t_pass1, t_sum0, t_sum1,
    a_near0, a_near1, a_pass0, a_pass1, a_sum0, a_sum1,
    b_near0, b_near1, b_pass0, b_pass1, b_sum0, b_sum1,
    c_near0, c_near1, c_pass0, c_pass1, c_sum0, c_sum1,
    d_near0, d_near1, d_pass0, d_pass1, d_sum0, d_sum1,
    e_near0, e_near1, e_pass0, e_pass1, e_sum0, e_sum1,
    u_near0, u_near1, u_pass0, u_pass1, u_sum0, u_sum1,
    v_near0, v_near1, v_pass0, v_pass1, v_sum0, v_sum1,
    a_out, b_out, c_out, d_out, u_out,
    t_sems, r_sems, g_sems, local_sems,
):
    host = lax.axis_index("hst")
    x = lax.axis_index("local")
    z, y, core = host // 8, (host // 2) % 4, host % 2

    def on_z(step):
        return {"hst": (lax.rem(z + step, 4) * 4 + y) * 2 + core}

    def on_y(step):
        return {"hst": (z * 4 + lax.rem(y + step, 4)) * 2 + core}

    def on_x(step):
        return {"local": lax.rem(x + step, 4)}

    barrier = pltpu.get_barrier_semaphore()
    for neighbours in (on_x, on_y, on_z):
        for step in (1, 2, 3):
            pl.semaphore_signal(
                barrier, inc=1, device_id=neighbours(step), device_id_type=MESH
            )
    partner = {"hst": host + 1 - 2 * core}
    pl.semaphore_signal(barrier, inc=1, device_id=partner, device_id_type=MESH)
    half = SHARD // 2
    right, left = lax.rem(x + 1, 4), lax.rem(x + 3, 4)
    locals_ = [
        pltpu.make_async_copy(tables.at[right, pl.ds(0, half)], ahead, local_sems.at[0]),
        pltpu.make_async_copy(tables.at[left, pl.ds(half, half)], behind, local_sems.at[1]),
        pltpu.make_async_copy(dense, grads, local_sems.at[2]),
        pltpu.make_async_copy(tables.at[x], mine, local_sems.at[3]),
        pltpu.make_async_copy(store_hbm, store, local_sems.at[4]),
        pltpu.make_async_copy(small_hbm, small, local_sems.at[5]),
    ]
    for copy in locals_:
        copy.start()
    pl.semaphore_wait(barrier, 10)

    first = {0: pl.ds(0, 896), 1: pl.ds(896, 896)}
    second = {0: pl.ds(CUT, 896), 1: pl.ds(CUT + 896, 768)}
    inner = {0: pl.ds(0, 896), 1: pl.ds(896, 768)}
    third = pl.ds(WIDTH, EMB)
    pairs = (pl.ds(0, 2), pl.ds(2, 2))
    halves = (pl.ds(0, 16), pl.ds(16, 16))
    table_ring = Ring(
        x, on_x(1), on_x(3),
        lambda t, s: tables.at[t, pl.ds(s * half, half)],
        lambda t, s: behind if s else ahead,
        (t_near0, t_near1), (t_pass0, t_pass1), (t_sum0, t_sum1), t_sems, CHUNKS,
    )
    a_ring = Ring(
        z, on_z(1), on_z(3),
        lambda t, s: dense.at[t, :, :, first[s]],
        lambda t, s: grads.at[t, :, :, first[s]],
        (a_near0, a_near1), (a_pass0, a_pass1), (a_sum0, a_sum1), r_sems.at[0],
    )
    b_ring = Ring(
        y, on_y(1), on_y(3),
        lambda t, s: dense.at[:, t, :, second[s]],
        lambda t, s: grads.at[:, t, :, second[s]],
        (b_near0, b_near1), (b_pass0, b_pass1), (b_sum0, b_sum1), r_sems.at[1],
    )
    c_at = lambda t, s: a_out.at[t, :, first[s]]
    c_ring = Ring(
        y, on_y(1), on_y(3), c_at, c_at, (c_near0, c_near1), (c_pass0, c_pass1), (c_sum0, c_sum1), r_sems.at[2]
    )
    d_at = lambda t, s: b_out.at[t, :, inner[s]]
    d_ring = Ring(
        z, on_z(1), on_z(3), d_at, d_at, (d_near0, d_near1), (d_pass0, d_pass1), (d_sum0, d_sum1), r_sems.at[3]
    )
    u_ring = Ring(
        z, on_z(1), on_z(3),
        lambda t, s: dense.at[t, pairs[s], :, third],
        lambda t, s: grads.at[t, pairs[s], :, third],
        (u_near0, u_near1), (u_pass0, u_pass1), (u_sum0, u_sum1), r_sems.at[5],
    )
    v_at = lambda t, s: u_out.at[t, halves[s]]
    v_ring = Ring(
        y, on_y(1), on_y(3), v_at, v_at,
        (v_near0, v_near1), (v_pass0, v_pass1), (v_sum0, v_sum1), r_sems.at[6],
    )
    e_at = lambda t, s: (d_out if s else c_out).at[pl.ds(pl.multiple_of(t * 8, 8), 8)]
    e_ring = Ring(
        x, on_x(1), on_x(3), e_at, e_at, (e_near0, e_near1), (e_pass0, e_pass1), (e_sum0, e_sum1), r_sems.at[4]
    )

    eye = diagonal()

    def update(block, grad, before, acc_before, after, acc_after):
        rows = pl.ds(pl.multiple_of(block * 128, 128), 128)
        at = pl.ds(block, 1)
        acc_here = jnp.sum(jnp.where(eye, acc_before[at, :], 0.0), axis=1, keepdims=True)
        total = acc_here + jnp.sum(grad * grad, axis=1, keepdims=True) * (1.0 / EMB)
        after[rows, :] = before[rows, :] - grad * (LEARN_RATE * lax.rsqrt(total))
        acc_after[at, :] = jnp.sum(jnp.where(eye, total, 0.0), axis=0, keepdims=True)

    def finish_dense(side, start, stop):
        near = (e_near1, e_near0)[side]
        at = pl.ds(start, stop - start)
        return e_ring.held(x, side)[:, at] + e_ring.sums[side][:, at] + near[:, at]

    def gather_copy(index, view, to):
        return pltpu.make_async_remote_copy(
            src_ref=view, dst_ref=view, send_sem=g_sems.at[0, index],
            recv_sem=g_sems.at[1, index], device_id=to, device_id_type=MESH,
        )

    def stage(number, back):
        copies = []
        for step in (1, 2, 3):
            there = lax.rem(4 - step, 4) if back else 0
            at_z, at_y, at_x = (lax.rem(place + there, 4) for place in (z, y, x))
            if number == 0:
                views = [(gathered.at[at_x, z, y, core], on_x)]
            elif number == 1:
                views = [
                    (gathered.at[:, z, at_y, core, halves[0]], on_y),
                    (gathered.at[:, at_z, y, core, halves[1]], on_z),
                ]
            else:
                views = [
                    (gathered.at[:, at_z, :, core, halves[0]], on_z),
                    (gathered.at[:, :, at_y, core, halves[1]], on_y),
                ]
            for view, axis in views:
                copies.append(gather_copy(number * 6 + len(copies), view, axis(step)))
        return copies

    def begin(number):
        for copy in stage(number, False):
            copy.start()

    def arrived(number):
        for copy in stage(number, True):
            copy.wait_recv()

    rows_chunk = half // CHUNKS

    def update_tables(chunk):
        table_ring.arrive(chunk)
        for side in range(2):
            near = (t_near1, t_near0)[side]

            @pl.loop(0, rows_chunk // 128)
            def _(part):
                inside = pl.ds(pl.multiple_of(chunk * rows_chunk + part * 128, 128), 128)
                block = side * (half // 128) + chunk * (rows_chunk // 128) + part
                rows = pl.ds(pl.multiple_of(block * 128, 128), 128)
                grad = mine[rows, :] + table_ring.sums[side][inside, :] + near[inside, :]
                update(block, grad, store, acc, table_new, acc_new)

    def update_small():
        @pl.loop(0, TR * RS // 128)
        def _(block):
            chip = (block % 8) * 2
            pieces = gathered.at[block // 8, chip // 4]
            grad = jnp.concatenate(
                [pieces[chip % 4 + part // 2, part % 2] for part in range(4)], axis=0
            )
            update(block, grad, small, small_acc, small_new, small_acc_new)

    def finish_steps():
        e_ring.arrive()
        for side, stop in ((0, CUT), (1, WIDTH - CUT)):
            total = finish_dense(side, 0, stop)
            at = pl.ds(side * CUT, stop)
            for step, before, rows in ((down_step, down_acc, 0), (up_step, up_acc, 4)):
                grad = total[rows : rows + 4]
                step[:, at] = grad * lax.rsqrt(before[:, at] + grad * grad)

    u_ring.start()
    u_ring.start_direct()
    for chunk in range(CHUNKS):
        table_ring.start(chunk)
    locals_[2].wait()
    u_ring.middle()
    u_ring.finish([u_out.at[pairs[s]] for s in range(2)])
    v_ring.start()
    v_ring.start_direct()
    a_ring.start()
    b_ring.start()
    v_ring.middle()
    v_ring.finish([gathered.at[x, z, y, core, halves[s]] for s in range(2)])
    begin(0)
    locals_[0].wait()
    locals_[1].wait()
    table_ring.middle(0)
    table_ring.start_direct(0)
    a_ring.middle()
    b_ring.middle()
    a_ring.start_direct()
    b_ring.start_direct()
    table_ring.middle(1)
    table_ring.start_direct(1)
    table_ring.middle(2)
    table_ring.start_direct(2)
    arrived(0)
    begin(1)
    for copy in locals_[3:]:
        copy.wait()
    table_ring.middle(3)
    table_ring.start_direct(3)
    a_ring.finish([a_out.at[:, :, first[s]] for s in range(2)])
    c_ring.start()
    c_ring.start_direct()
    b_ring.finish([b_out.at[:, :, inner[s]] for s in range(2)])
    d_ring.start()
    d_ring.start_direct()
    update_tables(0)
    table_ring.middle(4)
    table_ring.start_direct(4)
    arrived(1)
    begin(2)
    c_ring.middle()
    d_ring.middle()
    table_ring.middle(5)
    table_ring.start_direct(5)
    c_ring.finish([c_out.at[:, first[s]] for s in range(2)])
    d_ring.finish([d_out.at[:, inner[s]] for s in range(2)])
    e_ring.start()
    e_ring.start_direct()
    update_tables(1)
    arrived(2)
    gather_copy(18, gathered.at[:, :, :, core], partner).start()
    table_ring.middle(6)
    table_ring.start_direct(6)
    e_ring.middle()
    update_tables(2)
    table_ring.middle(7)
    table_ring.start_direct(7)
    gather_copy(18, gathered.at[:, :, :, 1 - core], partner).wait_recv()
    update_small()
    finish_steps()
    for chunk in range(3, CHUNKS):
        update_tables(chunk)
    for ring in (table_ring, a_ring, b_ring, c_ring, d_ring, e_ring, u_ring, v_ring):
        ring.drain()
    for number in range(3):
        for copy in stage(number, False):
            copy.wait_send()
    gather_copy(18, gathered.at[:, :, :, core], partner).wait_send()


def shaped(shape, dtype=F32):
    return jax.ShapeDtypeStruct(shape, dtype)


HBM = pl.BlockSpec(memory_space=pltpu.HBM)
VMEM = pl.BlockSpec(memory_space=pltpu.VMEM)
SMEM = pl.BlockSpec(memory_space=pltpu.SMEM)
DMA = pltpu.SemaphoreType.DMA


def params(mebibytes, **others):
    return pltpu.CompilerParams(vmem_limit_bytes=mebibytes << 20, **others)


def on_device(
    features, labels, cross_down, cross_up, cross_bias, head_weight, head_bias, table_place,
    bag_rows, small_rows, table_store, table_acc, small_store, small_acc, down_acc, up_acc,
):
    bags = jnp.transpose(bag_rows, (1, 2, 0))
    small_ids = jnp.transpose(small_rows, (1, 2, 0))
    whole = (RANK, FULL)
    got, ids, dense = pl.pallas_call(
        exchange_kernel,
        out_shape=(
            shaped((HOSTS, PACK, EMB)), shaped((HOSTS * HOT, SAMPLES), jnp.int32), shaped(whole),
        ),
        in_specs=[VMEM] * 3 + [SMEM] * 2 + [VMEM] * 2 + [HBM] * 3,
        out_specs=(HBM, VMEM, HBM),
        scratch_shapes=[
            pltpu.VMEM((TS, PACK, EMB), F32), pltpu.VMEM((HOSTS, PACK, EMB), F32),
            pltpu.VMEM((TR, PACK, EMB), F32),
            pltpu.VMEM((RANK, WIDTH), BF16), pltpu.VMEM((RANK, WIDTH), BF16),
            pltpu.VMEM((SAMPLES, WIDTH), F32), DMA((3,)),
            pltpu.VMEM((2 * SAMPLES, WIDTH), BF16), pltpu.VMEM((2 * SAMPLES, RANK), BF16),
            pltpu.VMEM((LOCALS, PACK, EMB), F32), pltpu.VMEM((HOSTS, PACK, EMB), F32),
            pltpu.VMEM((RANK, 2 * SAMPLES), BF16), pltpu.VMEM((RANK, 2 * SAMPLES), BF16),
            pltpu.VMEM(whole, F32), pltpu.VMEM(whole, F32), pltpu.VMEM(whole, F32),
            pltpu.VMEM((TR, SAMPLES, 2 * EMB), BF16),
            pltpu.VMEM((len(TIES), 2, PACK, EMB), F32),
            DMA((2, HOSTS)), DMA((2, len(TIES))), DMA((2, 4)), DMA((2, 4)), DMA((4,)), DMA, DMA,
        ],
        compiler_params=params(60, collective_id=0, has_side_effects=True),
        name="dense_exchange",
    )(
        labels.reshape(1, -1), cross_bias.reshape(-1, 128), head_weight.reshape(-1, 128), head_bias,
        table_place, bags, small_ids, features, cross_down, cross_up,
    )
    tables = pl.pallas_call(
        pooled_kernel,
        out_shape=shaped((LOCALS * SHARD, EMB)),
        in_specs=[SMEM, HBM],
        out_specs=HBM,
        scratch_shapes=[pltpu.VMEM((HOSTS, PACK, EMB), F32)]
        + [pltpu.VMEM((LOCALS * SHARD, EMB), F32)] * HOT
        + [DMA((LOCALS * SHARD // 256,)), DMA],
        compiler_params=params(60),
        name="pooled_rows",
    )(ids.reshape(-1), got)

    def ring_buffers(first_shape, second_shape):
        near = [pltpu.VMEM(second_shape, F32), pltpu.VMEM(first_shape, F32)]
        return near + [pltpu.VMEM(first_shape, F32), pltpu.VMEM(second_shape, F32)] * 2

    rest = WIDTH - CUT
    half = SHARD // 2
    table_new, acc_new, small_new, small_acc_new, down_step, up_step = pl.pallas_call(
        reduce_kernel,
        out_shape=(
            shaped((SHARD, EMB)), shaped((SHARD // 128, 128)),
            shaped((TR * RS, EMB)), shaped((TR * RS // 128, 128)),
            shaped((4, WIDTH)), shaped((4, WIDTH)),
        ),
        in_specs=[HBM] * 4 + [VMEM] * 4,
        out_specs=(VMEM,) * 6,
        scratch_shapes=[
            pltpu.VMEM((SHARD, EMB), F32), pltpu.VMEM((TR * RS, EMB), F32),
            pltpu.VMEM((LOCALS, 4, 4, 2, 32, EMB), F32), pltpu.VMEM((SHARD, EMB), F32),
            pltpu.VMEM((half, EMB), F32), pltpu.VMEM((half, EMB), F32),
            pltpu.VMEM((4, 4, 32, FULL), F32),
        ]
        + ring_buffers((half, EMB), (half, EMB))
        + ring_buffers((4, 32, 896), (4, 32, 896))
        + ring_buffers((4, 32, 896), (4, 32, 768))
        + ring_buffers((32, 896), (32, 896))
        + ring_buffers((32, 896), (32, 768))
        + ring_buffers((8, CUT), (8, rest))
        + ring_buffers((2, 32, EMB), (2, 32, EMB))
        + ring_buffers((16, EMB), (16, EMB))
        + [
            pltpu.VMEM((4, 32, CUT), F32), pltpu.VMEM((4, 32, rest), F32),
            pltpu.VMEM((32, CUT), F32), pltpu.VMEM((32, rest), F32),
            pltpu.VMEM((4, 32, EMB), F32),
            DMA((2, 6 * CHUNKS)), DMA((7, 2, 6)), DMA((2, 19)), DMA((6,)),
        ],
        compiler_params=params(48, collective_id=1, has_side_effects=True),
        name="reduce_update",
    )(
        tables.reshape(LOCALS, SHARD, EMB), dense.reshape(4, 4, 32, FULL), table_store, small_store,
        table_acc.reshape(-1, 128), small_acc.reshape(-1, 128), down_acc, up_acc,
    )
    return (
        table_new, acc_new.reshape(-1), small_new, small_acc_new.reshape(-1), down_step, up_step,
    )


def solution(mesh):
    both = ("hst", "local")
    rows = P(both, None)
    return jax.shard_map(
        on_device,
        mesh=mesh,
        in_specs=(
            rows, P(both), P(), P(), P(), P(), P(), P(), P(both, None, None), P(both, None, None),
            rows, P(both), P(), P(), rows, rows,
        ),
        out_specs=(rows, P(both), P(), P(), rows, rows),
        check_vma=False,
    )
```

```python
import functools

import jax
import jax.numpy as jnp
from jax import lax
from jax.experimental import pallas as pl
from jax.experimental.pallas import tpu as pltpu
from jax.sharding import PartitionSpec as P

TS = 22
TR = 4
RS = 1024
HOT = 4
SHARD = 4096
EMB = 128
RANK = 512
WIDTH = 3456
HOSTS = 32
LOCALS = 4
SAMPLES = 128
PACK = SAMPLES + 8
FULL = WIDTH + EMB
CUT = 1792
TIES = ((2, 0), (2, 1), (2, 3), (0, 2), (1, 2), (3, 2), (2, 2))
STRAIGHT = ((0, 1), (0, 3), (1, 0), (3, 0), (1, 1), (1, 3), (3, 1), (3, 3))
LEARN_RATE = 0.05
MESH = pl.DeviceIdType.MESH
F32 = jnp.float32
BF16 = jnp.bfloat16


def product(left, right, left_dim=1, right_dim=0):
    return lax.dot_general(
        left, right, (((left_dim,), (right_dim,)), ((), ())), preferred_element_type=F32
    )


def diagonal():
    return lax.broadcasted_iota(jnp.int32, (128, 128), 0) == lax.broadcasted_iota(
        jnp.int32, (128, 128), 1
    )


def dense_backward(
    labels, bias, head, head_bias, place, bags, small_ids, features_hbm, down_hbm, up_hbm,
    pieces, send, small, rights, lows, down, up, cross, sems,
):
    features = rights.at[0:SAMPLES]
    features_copy = pltpu.make_async_copy(features_hbm, features, sems.at[2])
    down_copy = pltpu.make_async_copy(down_hbm, down, sems.at[0])
    up_copy = pltpu.make_async_copy(up_hbm, up, sems.at[1])
    features_copy.start()
    down_copy.start()
    up_copy.start()

    @pl.loop(0, TS)
    def _(table):
        pieces[table, pl.ds(SAMPLES, 8), :] = jnp.concatenate(
            [bags[table].astype(F32), jnp.zeros((HOT, EMB), F32)], axis=0
        )

    for table in range(TR):
        small[table, SAMPLES:, :] = jnp.zeros((PACK - SAMPLES, EMB), F32)
        small[table, SAMPLES : SAMPLES + HOT, :] = small_ids[table].astype(F32)

    parts = [(start, min(256, WIDTH - start)) for start in range(0, WIDTH, 256)]

    def tiles(ref, start, width):
        rows = [ref[t : t + 1, :] for t in range(start // 128, (start + width) // 128)]
        return jnp.concatenate(rows, axis=1)

    features_copy.wait()
    down_copy.wait()
    low_proj = product(features[...], down[...], 1, 1).astype(BF16)
    lows[SAMPLES:, :] = low_proj
    up_copy.wait()
    terms = jnp.zeros((SAMPLES, 128), F32)
    for start, width in parts:
        at = pl.ds(start, width)
        out = product(low_proj, up[:, at]) + tiles(bias, start, width)
        cross[:, at] = out
        wide = features[:, at].astype(F32)
        weighted = (wide * out + wide) * tiles(head, start, width)
        for tile in range(width // 128):
            terms = terms + weighted[:, tile * 128 : (tile + 1) * 128]
    logit = jnp.sum(terms, axis=1, keepdims=True) + head_bias[0]
    label = jnp.sum(
        jnp.where(diagonal(), labels[...].astype(F32), 0.0), axis=1, keepdims=True
    )
    logit_grad = jax.nn.sigmoid(logit) - label
    for start, width in parts:
        at = pl.ds(start, width)
        layer_grad = logit_grad * tiles(head, start, width)
        rights[SAMPLES:, at] = (layer_grad * features[:, at].astype(F32)).astype(BF16)
    low_grad = product(rights[SAMPLES:, :], up[...], 1, 1).astype(BF16)
    lows[0:SAMPLES, :] = low_grad
    for start, width in parts:
        at = pl.ds(start, width)
        layer_grad = logit_grad * tiles(head, start, width)
        grad = layer_grad * (cross[:, at] + 1.0) + product(low_grad, down[:, at])
        for tile in range(width // 128):
            piece = grad[:, tile * 128 : (tile + 1) * 128]
            table = start // 128 + tile - 1
            if 0 <= table < TS:
                pieces[table, 0:SAMPLES, :] = piece
            elif table >= TS:
                small[table - TS, 0:SAMPLES, :] = piece

    @pl.loop(0, HOSTS)
    def _(slot):
        held = jnp.int32(-1)
        for table in range(TS):
            held = jnp.where(place[table] == slot, table, held)
        keep = jnp.where(held >= 0, 1, 0)
        send[slot] = jnp.where(keep == 1, pieces[jnp.maximum(held, 0)], 0.0)


def exchange_kernel(
    labels, bias, head, head_bias, place, bags, small_ids, features_hbm, down_hbm, up_hbm,
    got_hbm, ids, dense,
    pieces, send, small_mine, down, up, cross, dense_sems,
    rights, lows, small, got, left_own, left_other, own, other, arrived, split, relayed,
    sems, relay_sems, core_sems, small_sems, out_sems, in_sem, own_sem,
):
    host = lax.axis_index("hst")
    core = lax.rem(host, 2)
    z, y = host // 8, (host // 2) % 4
    x = lax.axis_index("local")
    partner = host + 1 - 2 * core
    barrier = pltpu.get_barrier_semaphore()

    @pl.loop(1, HOSTS)
    def _(off):
        pl.semaphore_signal(
            barrier, inc=1, device_id={"hst": lax.rem(host + off, HOSTS)}, device_id_type=MESH
        )

    def chip(dz, dy):
        return (lax.rem(z + dz + 4, 4) * 4 + lax.rem(y + dy + 4, 4)) * 2

    def bag_copy(src, to, slot, off, cores):
        at = (off[0] * 4 + off[1]) * 2
        return pltpu.make_async_remote_copy(
            src_ref=src,
            dst_ref=got.at[slot],
            send_sem=sems.at[0, at + cores[1]],
            recv_sem=sems.at[1, at + cores[0]],
            device_id={"hst": to},
            device_id_type=MESH,
        )

    def straight(off, target):
        to = chip(*off) + target
        return bag_copy(send.at[to], to, host, off, (core, target))

    turn = 1 - 2 * core

    def halfway(index):
        dz, dy = TIES[index]
        to = chip(turn if dz == 2 else 0, turn if dy == 2 else 0) + core
        return pltpu.make_async_remote_copy(
            src_ref=send.at[pl.ds(chip(dz, dy), 2)],
            dst_ref=relayed.at[index],
            send_sem=relay_sems.at[0, index],
            recv_sem=relay_sems.at[1, index],
            device_id={"hst": to},
            device_id_type=MESH,
        )

    def onward(index, target):
        dz, dy = TIES[index]
        to = chip(turn if dz == 2 else dz, turn if dy == 2 else dy) + target
        source = chip(-turn if dz == 2 else 0, -turn if dy == 2 else 0) + core
        return bag_copy(relayed.at[index, target], to, source, TIES[index], (core, target))

    def arrival(off, source_core):
        source = chip(-off[0], -off[1]) + source_core
        return bag_copy(send.at[source], source, source, off, (source_core, source_core))

    def neighbour():
        return pltpu.make_async_remote_copy(
            src_ref=send.at[partner],
            dst_ref=got.at[host],
            send_sem=sems.at[0, 0],
            recv_sem=sems.at[1, 0],
            device_id={"hst": partner},
            device_id_type=MESH,
        )

    def from_neighbour():
        return pltpu.make_async_remote_copy(
            src_ref=send.at[partner],
            dst_ref=got.at[partner],
            send_sem=sems.at[0, 0],
            recv_sem=sems.at[1, 0],
            device_id={"hst": partner},
            device_id_type=MESH,
        )

    for step in (1, 2, 3):
        pl.semaphore_signal(
            barrier, inc=1, device_id={"local": lax.rem(x + step, 4)}, device_id_type=MESH
        )

    def small_copy(step, slot):
        to = lax.rem(x + step, 4)
        return pltpu.make_async_remote_copy(
            src_ref=small_mine.at[to],
            dst_ref=small.at[slot],
            send_sem=small_sems.at[0, step],
            recv_sem=small_sems.at[1, step],
            device_id={"local": to},
            device_id_type=MESH,
        )

    dense_backward(
        labels, bias, head, head_bias, place, bags, small_ids, features_hbm, down_hbm, up_hbm,
        pieces, send, small_mine, rights, lows, down, up, cross, dense_sems,
    )
    small_own = pltpu.make_async_copy(small_mine.at[x], small.at[x], in_sem)
    small_own.start()
    pl.semaphore_wait(barrier, HOSTS + 2)
    for step in (1, 2, 3):
        small_copy(step, x).start()
    for index in range(len(TIES)):
        halfway(index).start()
    for off in STRAIGHT:
        for target in range(2):
            straight(off, target).start()
    neighbour().start()
    mine = pltpu.make_async_copy(send.at[host], got.at[host], own_sem)
    mine.start()

    def spread(target, left):
        row = lax.broadcasted_iota(jnp.int32, (RANK, RANK), 0)
        rank = lax.broadcasted_iota(jnp.int32, (RANK, RANK), 1)
        place = row & 7
        base = ((row >> 5) * 2 + target) * 16 + ((row >> 3) & 3) * 4
        for part in range(2):
            want = jnp.where((place >> 2) == part, base + place - 4 * part, -1)
            chosen = jnp.where(want == rank, 1.0, 0.0).astype(BF16)
            left[:, part * SAMPLES : (part + 1) * SAMPLES] = product(
                chosen, lows[part * SAMPLES : (part + 1) * SAMPLES, :], 1, 1
            ).astype(BF16)

    def grads(left, out, group):
        @pl.loop(0, WIDTH // 384)
        def _(part):
            at = pl.ds(pl.multiple_of(part * 384, 384), 384)
            out[group * 128 : (group + 1) * 128, at] = product(
                left[group * 128 : (group + 1) * 128, :], rights[:, at]
            )

    small_own.wait()
    for step in (1, 2, 3):
        small_copy(step, lax.rem(x - step + 4, 4)).wait_recv()

    @pl.loop(0, LOCALS)
    def _(source):
        value = small[source, pl.ds(0, SAMPLES), :]
        high = value.astype(BF16)
        split[source, :, 0:EMB] = high
        split[source, :, EMB:] = (value - high.astype(F32)).astype(BF16)

    def small_sums(target, out, group):
        spot = group * 128 + lax.broadcasted_iota(jnp.int32, (128, SAMPLES), 0)
        row = ((spot >> 5) * 64 + target * 32 + (spot & 31)).astype(F32)
        here = pl.ds(group * 128, 128)
        lanes = pl.ds(WIDTH, EMB)
        out[here, lanes] = jnp.zeros((128, EMB), F32)

        @pl.loop(0, LOCALS)
        def _(source):
            wanted = small[source, pl.ds(SAMPLES, 8), :]
            counts = jnp.zeros((128, SAMPLES), F32)
            for k in range(HOT):
                counts = counts + jnp.where(row == wanted[k : k + 1, :], 1.0, 0.0)
            both = product(counts.astype(BF16), split[source])
            out[here, lanes] = out[here, lanes] + (both[:, 0:EMB] + both[:, EMB:])

    def core_copy(group):
        rows = pl.ds(group * 128, 128)
        return pltpu.make_async_remote_copy(
            src_ref=other.at[rows],
            dst_ref=arrived.at[rows],
            send_sem=core_sems.at[0, group],
            recv_sem=core_sems.at[1, group],
            device_id={"hst": partner},
            device_id_type=MESH,
        )

    def out_copy(group):
        rows = pl.ds(group * 128, 128)
        return pltpu.make_async_copy(own.at[rows], dense.at[rows], out_sems.at[group])

    spread(1 - core, left_other)
    for group in range(4):
        grads(left_other, other, group)
        small_sums(1 - core, other, group)
        core_copy(group).start()
    for index in range(len(TIES)):
        halfway(index).wait_recv()
        for target in range(2):
            onward(index, target).start()
    spread(core, left_own)
    for group in range(4):
        grads(left_own, own, group)
        small_sums(core, own, group)
    for group in range(4):
        core_copy(group).wait_recv()

        @pl.loop(0, 4)
        def _(part):
            rows = pl.ds(pl.multiple_of(group * 128 + part * 32, 32), 32)
            own[rows, :] = own[rows, :] + arrived[rows, :]

        out_copy(group).start()

    mine.wait()
    from_neighbour().wait_recv()
    for off in STRAIGHT + TIES:
        for source_core in range(2):
            arrival(off, source_core).wait_recv()

    @pl.loop(0, HOSTS // 2)
    def _(pair):
        low = got[pair * 2, pl.ds(SAMPLES, 8), :]
        high = got[pair * 2 + 1, pl.ds(SAMPLES, 8), :]
        ids[pl.ds(pl.multiple_of(pair * 8, 8), 8), :] = jnp.concatenate(
            [low[0:HOT], high[0:HOT]], axis=0
        ).astype(jnp.int32)

    result = pltpu.make_async_copy(got, got_hbm, own_sem)
    result.start()
    neighbour().wait_send()
    for step in (1, 2, 3):
        small_copy(step, x).wait_send()
    for off in STRAIGHT:
        for target in range(2):
            straight(off, target).wait_send()
    for index in range(len(TIES)):
        halfway(index).wait_send()
        for target in range(2):
            onward(index, target).wait_send()
    for group in range(4):
        core_copy(group).wait_send()
        out_copy(group).wait()
    result.wait()


def pooled_kernel(ids, grads_hbm, out, grads, *scratch):
    sums, sem, in_sem = scratch[:HOT], scratch[HOT], scratch[HOT + 1]
    operand = pltpu.make_async_copy(grads_hbm, grads, in_sem)
    operand.start()
    row_total = out.shape[0]
    step = 256

    @pl.loop(0, row_total // step)
    def _(i):
        rows = pl.ds(pl.multiple_of(i * step, step), step)
        for total in sums:
            total[rows, :] = jnp.zeros((step, EMB), F32)

    operand.wait()

    @pl.loop(0, HOSTS)
    def _(source):
        @pl.loop(0, SAMPLES // 16)
        def _(group):
            for pair in range(8):
                sample = group * 16 + pair * 2
                first = grads[source, pl.ds(sample, 1), :]
                second = grads[source, pl.ds(sample + 1, 1), :]
                at = [
                    ids[(source * HOT + k % HOT) * SAMPLES + sample + k // HOT]
                    for k in range(2 * HOT)
                ]
                held = [sums[k % HOT][pl.ds(at[k], 1), :] for k in range(2 * HOT)]
                new = [held[k] + first for k in range(HOT)]
                for k in range(HOT):
                    new.append(jnp.where(at[k] == at[HOT + k], new[k], held[HOT + k]) + second)
                for k in range(2 * HOT):
                    sums[k % HOT][pl.ds(at[k], 1), :] = new[k]

    @pl.loop(0, row_total // step)
    def _(i):
        rows = pl.ds(pl.multiple_of(i * step, step), step)
        sums[0][rows, :] = (sums[0][rows, :] + sums[1][rows, :]) + (
            sums[2][rows, :] + sums[3][rows, :]
        )
        pltpu.make_async_copy(sums[0].at[rows], out.at[rows], sem.at[i]).start()

    @pl.loop(0, row_total // step)
    def _(i):
        rows = pl.ds(pl.multiple_of(i * step, step), step)
        pltpu.make_async_copy(sums[0].at[rows], out.at[rows], sem.at[i]).wait()


class Ring:
    def __init__(self, place, right, left, sent, held, near, passed, sums, sems, chunks=1):
        self.place, self.right, self.left = place, right, left
        self.sent, self.held, self.near, self.passed = sent, held, near, passed
        self.sums, self.sems, self.chunks = sums, sems, chunks

    def piece(self, ref, chunk):
        if self.chunks == 1:
            return ref
        rows = ref.shape[0] // self.chunks
        return ref.at[pl.ds(chunk * rows, rows)]

    def copy(self, src, dst, kind, side, chunk):
        index = (kind * 2 + side) * self.chunks + chunk
        return pltpu.make_async_remote_copy(
            src_ref=self.piece(src, chunk), dst_ref=self.piece(dst, chunk),
            send_sem=self.sems.at[0, index], recv_sem=self.sems.at[1, index],
            device_id=self.left if side else self.right, device_id_type=MESH,
        )

    def next(self, side):
        return lax.rem(self.place + (3 if side else 1), 4)

    def far(self, side, chunk=0):
        src = self.sent(lax.rem(self.place + 2, 4), side)
        return self.copy(src, self.passed[side], 0, side, chunk)

    def direct(self, side, chunk=0):
        return self.copy(self.sent(self.next(side), 1 - side), self.near[side], 1, side, chunk)

    def relay(self, side, chunk=0):
        return self.copy(self.passed[side], self.sums[side], 2, side, chunk)

    def start(self, chunk=0):
        for side in range(2):
            self.far(side, chunk).start()

    def start_direct(self, chunk=0):
        for side in range(2):
            self.direct(side, chunk).start()

    def middle(self, chunk=0):
        for side in range(2):
            self.far(side, chunk).wait_recv()
            add_into(
                self.piece(self.passed[side], chunk),
                self.piece(self.held(self.next(side), side), chunk),
            )
            self.relay(side, chunk).start()

    def arrive(self, chunk=0):
        for side in range(2):
            self.relay(side, chunk).wait_recv()
            self.direct(side, chunk).wait_recv()

    def finish(self, outs):
        self.arrive()
        add_three(outs[0], self.held(self.place, 0), self.sums[0], self.near[1])
        add_three(outs[1], self.held(self.place, 1), self.near[0], self.sums[1])

    def drain(self):
        for chunk in range(self.chunks):
            for side in range(2):
                self.far(side, chunk).wait_send()
                self.direct(side, chunk).wait_send()
                self.relay(side, chunk).wait_send()


def blocks_of(shape):
    if len(shape) == 3:
        return shape[0], lambda ref, i: ref.at[i]
    rows = min(shape[0], 32 if shape[1] > 256 else 128)
    return shape[0] // rows, lambda ref, i: ref.at[pl.ds(pl.multiple_of(i * rows, rows), rows)]


def add_into(total, term):
    count, at = blocks_of(total.shape)

    @pl.loop(0, count)
    def _(i):
        at(total, i)[...] = at(total, i)[...] + at(term, i)[...]


def add_three(out, first, second, third):
    count, at = blocks_of(out.shape)

    @pl.loop(0, count)
    def _(i):
        at(out, i)[...] = at(first, i)[...] + at(second, i)[...] + at(third, i)[...]


CHUNKS = 8


def reduce_kernel(
    tables, dense, store_hbm, small_hbm, acc, small_acc, down_acc, up_acc,
    table_new, acc_new, small_new, small_acc_new, down_step, up_step,
    store, small, gathered, mine, ahead, behind, grads,
    t_near0, t_near1, t_pass0, t_pass1, t_sum0, t_sum1,
    a_near0, a_near1, a_pass0, a_pass1, a_sum0, a_sum1,
    b_near0, b_near1, b_pass0, b_pass1, b_sum0, b_sum1,
    c_near0, c_near1, c_pass0, c_pass1, c_sum0, c_sum1,
    d_near0, d_near1, d_pass0, d_pass1, d_sum0, d_sum1,
    e_near0, e_near1, e_pass0, e_pass1, e_sum0, e_sum1,
    u_near0, u_near1, u_pass0, u_pass1, u_sum0, u_sum1,
    v_near0, v_near1, v_pass0, v_pass1, v_sum0, v_sum1,
    a_out, b_out, c_out, d_out, u_out,
    t_sems, r_sems, g_sems, local_sems,
):
    host = lax.axis_index("hst")
    x = lax.axis_index("local")
    z, y, core = host // 8, (host // 2) % 4, host % 2

    def on_z(step):
        return {"hst": (lax.rem(z + step, 4) * 4 + y) * 2 + core}

    def on_y(step):
        return {"hst": (z * 4 + lax.rem(y + step, 4)) * 2 + core}

    def on_x(step):
        return {"local": lax.rem(x + step, 4)}

    barrier = pltpu.get_barrier_semaphore()
    for neighbours in (on_x, on_y, on_z):
        for step in (1, 2, 3):
            pl.semaphore_signal(
                barrier, inc=1, device_id=neighbours(step), device_id_type=MESH
            )
    partner = {"hst": host + 1 - 2 * core}
    pl.semaphore_signal(barrier, inc=1, device_id=partner, device_id_type=MESH)
    half = SHARD // 2
    right, left = lax.rem(x + 1, 4), lax.rem(x + 3, 4)
    locals_ = [
        pltpu.make_async_copy(tables.at[right, pl.ds(0, half)], ahead, local_sems.at[0]),
        pltpu.make_async_copy(tables.at[left, pl.ds(half, half)], behind, local_sems.at[1]),
        pltpu.make_async_copy(
            dense.at[:, :, :, pl.ds(WIDTH, EMB)], grads.at[:, :, :, pl.ds(WIDTH, EMB)],
            local_sems.at[2],
        ),
        pltpu.make_async_copy(tables.at[x], mine, local_sems.at[3]),
        pltpu.make_async_copy(store_hbm, store, local_sems.at[4]),
        pltpu.make_async_copy(small_hbm, small, local_sems.at[5]),
        pltpu.make_async_copy(
            dense.at[:, :, :, pl.ds(0, WIDTH)], grads.at[:, :, :, pl.ds(0, WIDTH)],
            local_sems.at[6],
        ),
    ]
    for copy in (locals_[2], locals_[0], locals_[1], locals_[6]):
        copy.start()
    pl.semaphore_wait(barrier, 10)

    first = {0: pl.ds(0, 896), 1: pl.ds(896, 896)}
    second = {0: pl.ds(CUT, 896), 1: pl.ds(CUT + 896, 768)}
    inner = {0: pl.ds(0, 896), 1: pl.ds(896, 768)}
    third = pl.ds(WIDTH, EMB)
    pairs = (pl.ds(0, 2), pl.ds(2, 2))
    halves = (pl.ds(0, 16), pl.ds(16, 16))
    table_ring = Ring(
        x, on_x(1), on_x(3),
        lambda t, s: tables.at[t, pl.ds(s * half, half)],
        lambda t, s: behind if s else ahead,
        (t_near0, t_near1), (t_pass0, t_pass1), (t_sum0, t_sum1), t_sems, CHUNKS,
    )
    a_ring = Ring(
        z, on_z(1), on_z(3),
        lambda t, s: dense.at[t, :, :, first[s]],
        lambda t, s: grads.at[t, :, :, first[s]],
        (a_near0, a_near1), (a_pass0, a_pass1), (a_sum0, a_sum1), r_sems.at[0],
    )
    b_ring = Ring(
        y, on_y(1), on_y(3),
        lambda t, s: dense.at[:, t, :, second[s]],
        lambda t, s: grads.at[:, t, :, second[s]],
        (b_near0, b_near1), (b_pass0, b_pass1), (b_sum0, b_sum1), r_sems.at[1],
    )
    c_at = lambda t, s: a_out.at[t, :, first[s]]
    c_ring = Ring(
        y, on_y(1), on_y(3), c_at, c_at, (c_near0, c_near1), (c_pass0, c_pass1), (c_sum0, c_sum1), r_sems.at[2]
    )
    d_at = lambda t, s: b_out.at[t, :, inner[s]]
    d_ring = Ring(
        z, on_z(1), on_z(3), d_at, d_at, (d_near0, d_near1), (d_pass0, d_pass1), (d_sum0, d_sum1), r_sems.at[3]
    )
    u_ring = Ring(
        z, on_z(1), on_z(3),
        lambda t, s: dense.at[t, pairs[s], :, third],
        lambda t, s: grads.at[t, pairs[s], :, third],
        (u_near0, u_near1), (u_pass0, u_pass1), (u_sum0, u_sum1), r_sems.at[5],
    )
    v_at = lambda t, s: u_out.at[t, halves[s]]
    v_ring = Ring(
        y, on_y(1), on_y(3), v_at, v_at,
        (v_near0, v_near1), (v_pass0, v_pass1), (v_sum0, v_sum1), r_sems.at[6],
    )
    e_at = lambda t, s: (d_out if s else c_out).at[pl.ds(pl.multiple_of(t * 8, 8), 8)]
    e_ring = Ring(
        x, on_x(1), on_x(3), e_at, e_at, (e_near0, e_near1), (e_pass0, e_pass1), (e_sum0, e_sum1), r_sems.at[4]
    )

    eye = diagonal()

    def update(block, grad, before, acc_before, after, acc_after):
        rows = pl.ds(pl.multiple_of(block * 128, 128), 128)
        at = pl.ds(block, 1)
        acc_here = jnp.sum(jnp.where(eye, acc_before[at, :], 0.0), axis=1, keepdims=True)
        total = acc_here + jnp.sum(grad * grad, axis=1, keepdims=True) * (1.0 / EMB)
        after[rows, :] = before[rows, :] - grad * (LEARN_RATE * lax.rsqrt(total))
        acc_after[at, :] = jnp.sum(jnp.where(eye, total, 0.0), axis=0, keepdims=True)

    def finish_dense(side, start, stop):
        near = (e_near1, e_near0)[side]
        at = pl.ds(start, stop - start)
        return e_ring.held(x, side)[:, at] + e_ring.sums[side][:, at] + near[:, at]

    def gather_copy(index, view, to):
        return pltpu.make_async_remote_copy(
            src_ref=view, dst_ref=view, send_sem=g_sems.at[0, index],
            recv_sem=g_sems.at[1, index], device_id=to, device_id_type=MESH,
        )

    def stage(number, back):
        copies = []
        for step in (1, 2, 3):
            there = lax.rem(4 - step, 4) if back else 0
            at_z, at_y, at_x = (lax.rem(place + there, 4) for place in (z, y, x))
            if number == 0:
                views = [(gathered.at[at_x, z, y, core], on_x)]
            elif number == 1:
                views = [
                    (gathered.at[:, z, at_y, core, halves[0]], on_y),
                    (gathered.at[:, at_z, y, core, halves[1]], on_z),
                ]
            else:
                views = [
                    (gathered.at[:, at_z, :, core, halves[0]], on_z),
                    (gathered.at[:, :, at_y, core, halves[1]], on_y),
                ]
            for view, axis in views:
                copies.append(gather_copy(number * 6 + len(copies), view, axis(step)))
        return copies

    def begin(number):
        for copy in stage(number, False):
            copy.start()

    def arrived(number):
        for copy in stage(number, True):
            copy.wait_recv()

    rows_chunk = half // CHUNKS

    def update_tables(chunk):
        table_ring.arrive(chunk)
        for side in range(2):
            near = (t_near1, t_near0)[side]

            @pl.loop(0, rows_chunk // 128)
            def _(part):
                inside = pl.ds(pl.multiple_of(chunk * rows_chunk + part * 128, 128), 128)
                block = side * (half // 128) + chunk * (rows_chunk // 128) + part
                rows = pl.ds(pl.multiple_of(block * 128, 128), 128)
                grad = mine[rows, :] + table_ring.sums[side][inside, :] + near[inside, :]
                update(block, grad, store, acc, table_new, acc_new)

    def update_small():
        @pl.loop(0, TR * RS // 128)
        def _(block):
            chip = (block % 8) * 2
            pieces = gathered.at[block // 8, chip // 4]
            grad = jnp.concatenate(
                [pieces[chip % 4 + part // 2, part % 2] for part in range(4)], axis=0
            )
            update(block, grad, small, small_acc, small_new, small_acc_new)

    def finish_steps():
        e_ring.arrive()
        for side, stop in ((0, CUT), (1, WIDTH - CUT)):
            total = finish_dense(side, 0, stop)
            at = pl.ds(side * CUT, stop)
            for step, before, rows in ((down_step, down_acc, 0), (up_step, up_acc, 4)):
                grad = total[rows : rows + 4]
                step[:, at] = grad * lax.rsqrt(before[:, at] + grad * grad)

    u_ring.start()
    u_ring.start_direct()
    for chunk in range(CHUNKS):
        table_ring.start(chunk)
    locals_[2].wait()
    for copy in locals_[3:6]:
        copy.start()
    u_ring.middle()
    u_ring.finish([u_out.at[pairs[s]] for s in range(2)])
    v_ring.start()
    v_ring.start_direct()
    a_ring.start()
    b_ring.start()
    v_ring.middle()
    v_ring.finish([gathered.at[x, z, y, core, halves[s]] for s in range(2)])
    begin(0)
    locals_[0].wait()
    locals_[1].wait()
    locals_[6].wait()
    table_ring.middle(0)
    table_ring.start_direct(0)
    a_ring.middle()
    b_ring.middle()
    a_ring.start_direct()
    b_ring.start_direct()
    table_ring.middle(1)
    table_ring.start_direct(1)
    table_ring.middle(2)
    table_ring.start_direct(2)
    arrived(0)
    begin(1)
    for copy in locals_[3:6]:
        copy.wait()
    table_ring.middle(3)
    table_ring.start_direct(3)
    a_ring.finish([a_out.at[:, :, first[s]] for s in range(2)])
    c_ring.start()
    c_ring.start_direct()
    b_ring.finish([b_out.at[:, :, inner[s]] for s in range(2)])
    d_ring.start()
    d_ring.start_direct()
    update_tables(0)
    table_ring.middle(4)
    table_ring.start_direct(4)
    arrived(1)
    begin(2)
    c_ring.middle()
    d_ring.middle()
    table_ring.middle(5)
    table_ring.start_direct(5)
    c_ring.finish([c_out.at[:, first[s]] for s in range(2)])
    d_ring.finish([d_out.at[:, inner[s]] for s in range(2)])
    e_ring.start()
    e_ring.start_direct()
    update_tables(1)
    arrived(2)
    gather_copy(18, gathered.at[:, :, :, core], partner).start()
    table_ring.middle(6)
    table_ring.start_direct(6)
    e_ring.middle()
    update_tables(2)
    table_ring.middle(7)
    table_ring.start_direct(7)
    gather_copy(18, gathered.at[:, :, :, 1 - core], partner).wait_recv()
    update_small()
    finish_steps()
    for chunk in range(3, CHUNKS):
        update_tables(chunk)
    for ring in (table_ring, a_ring, b_ring, c_ring, d_ring, e_ring, u_ring, v_ring):
        ring.drain()
    for number in range(3):
        for copy in stage(number, False):
            copy.wait_send()
    gather_copy(18, gathered.at[:, :, :, core], partner).wait_send()


def shaped(shape, dtype=F32):
    return jax.ShapeDtypeStruct(shape, dtype)


HBM = pl.BlockSpec(memory_space=pltpu.HBM)
VMEM = pl.BlockSpec(memory_space=pltpu.VMEM)
SMEM = pl.BlockSpec(memory_space=pltpu.SMEM)
DMA = pltpu.SemaphoreType.DMA


def params(mebibytes, **others):
    return pltpu.CompilerParams(vmem_limit_bytes=mebibytes << 20, **others)


def on_device(
    features, labels, cross_down, cross_up, cross_bias, head_weight, head_bias, table_place,
    bag_rows, small_rows, table_store, table_acc, small_store, small_acc, down_acc, up_acc,
):
    bags = jnp.transpose(bag_rows, (1, 2, 0))
    small_ids = jnp.transpose(small_rows, (1, 2, 0))
    whole = (RANK, FULL)
    got, ids, dense = pl.pallas_call(
        exchange_kernel,
        out_shape=(
            shaped((HOSTS, PACK, EMB)), shaped((HOSTS * HOT, SAMPLES), jnp.int32), shaped(whole),
        ),
        in_specs=[VMEM] * 3 + [SMEM] * 2 + [VMEM] * 2 + [HBM] * 3,
        out_specs=(HBM, VMEM, HBM),
        scratch_shapes=[
            pltpu.VMEM((TS, PACK, EMB), F32), pltpu.VMEM((HOSTS, PACK, EMB), F32),
            pltpu.VMEM((TR, PACK, EMB), F32),
            pltpu.VMEM((RANK, WIDTH), BF16), pltpu.VMEM((RANK, WIDTH), BF16),
            pltpu.VMEM((SAMPLES, WIDTH), F32), DMA((3,)),
            pltpu.VMEM((2 * SAMPLES, WIDTH), BF16), pltpu.VMEM((2 * SAMPLES, RANK), BF16),
            pltpu.VMEM((LOCALS, PACK, EMB), F32), pltpu.VMEM((HOSTS, PACK, EMB), F32),
            pltpu.VMEM((RANK, 2 * SAMPLES), BF16), pltpu.VMEM((RANK, 2 * SAMPLES), BF16),
            pltpu.VMEM(whole, F32), pltpu.VMEM(whole, F32), pltpu.VMEM(whole, F32),
            pltpu.VMEM((TR, SAMPLES, 2 * EMB), BF16),
            pltpu.VMEM((len(TIES), 2, PACK, EMB), F32),
            DMA((2, HOSTS)), DMA((2, len(TIES))), DMA((2, 4)), DMA((2, 4)), DMA((4,)), DMA, DMA,
        ],
        compiler_params=params(60, collective_id=0, has_side_effects=True),
        name="dense_exchange",
    )(
        labels.reshape(1, -1), cross_bias.reshape(-1, 128), head_weight.reshape(-1, 128), head_bias,
        table_place, bags, small_ids, features, cross_down, cross_up,
    )
    tables = pl.pallas_call(
        pooled_kernel,
        out_shape=shaped((LOCALS * SHARD, EMB)),
        in_specs=[SMEM, HBM],
        out_specs=HBM,
        scratch_shapes=[pltpu.VMEM((HOSTS, PACK, EMB), F32)]
        + [pltpu.VMEM((LOCALS * SHARD, EMB), F32)] * HOT
        + [DMA((LOCALS * SHARD // 256,)), DMA],
        compiler_params=params(60),
        name="pooled_rows",
    )(ids.reshape(-1), got)

    def ring_buffers(first_shape, second_shape):
        near = [pltpu.VMEM(second_shape, F32), pltpu.VMEM(first_shape, F32)]
        return near + [pltpu.VMEM(first_shape, F32), pltpu.VMEM(second_shape, F32)] * 2

    rest = WIDTH - CUT
    half = SHARD // 2
    table_new, acc_new, small_new, small_acc_new, down_step, up_step = pl.pallas_call(
        reduce_kernel,
        out_shape=(
            shaped((SHARD, EMB)), shaped((SHARD // 128, 128)),
            shaped((TR * RS, EMB)), shaped((TR * RS // 128, 128)),
            shaped((4, WIDTH)), shaped((4, WIDTH)),
        ),
        in_specs=[HBM] * 4 + [VMEM] * 4,
        out_specs=(VMEM,) * 6,
        scratch_shapes=[
            pltpu.VMEM((SHARD, EMB), F32), pltpu.VMEM((TR * RS, EMB), F32),
            pltpu.VMEM((LOCALS, 4, 4, 2, 32, EMB), F32), pltpu.VMEM((SHARD, EMB), F32),
            pltpu.VMEM((half, EMB), F32), pltpu.VMEM((half, EMB), F32),
            pltpu.VMEM((4, 4, 32, FULL), F32),
        ]
        + ring_buffers((half, EMB), (half, EMB))
        + ring_buffers((4, 32, 896), (4, 32, 896))
        + ring_buffers((4, 32, 896), (4, 32, 768))
        + ring_buffers((32, 896), (32, 896))
        + ring_buffers((32, 896), (32, 768))
        + ring_buffers((8, CUT), (8, rest))
        + ring_buffers((2, 32, EMB), (2, 32, EMB))
        + ring_buffers((16, EMB), (16, EMB))
        + [
            pltpu.VMEM((4, 32, CUT), F32), pltpu.VMEM((4, 32, rest), F32),
            pltpu.VMEM((32, CUT), F32), pltpu.VMEM((32, rest), F32),
            pltpu.VMEM((4, 32, EMB), F32),
            DMA((2, 6 * CHUNKS)), DMA((7, 2, 6)), DMA((2, 19)), DMA((7,)),
        ],
        compiler_params=params(48, collective_id=1, has_side_effects=True),
        name="reduce_update",
    )(
        tables.reshape(LOCALS, SHARD, EMB), dense.reshape(4, 4, 32, FULL), table_store, small_store,
        table_acc.reshape(-1, 128), small_acc.reshape(-1, 128), down_acc, up_acc,
    )
    return (
        table_new, acc_new.reshape(-1), small_new, small_acc_new.reshape(-1), down_step, up_step,
    )


def solution(mesh):
    both = ("hst", "local")
    rows = P(both, None)
    return jax.shard_map(
        on_device,
        mesh=mesh,
        in_specs=(
            rows, P(both), P(), P(), P(), P(), P(), P(), P(both, None, None), P(both, None, None),
            rows, P(both), P(), P(), rows, rows,
        ),
        out_specs=(rows, P(both), P(), P(), rows, rows),
        check_vma=False,
    )
```
